32 devices in a mesh: tp: 4 (over x, core), dp: 8 (over z, y).
Axes of the slice: x: 2, y: 2, z: 4, core: 2. Of those that a mesh axis runs over, the one named last changes fastest.
Arguments:
- tokens: bfloat16 [2, 8, 640, 768], P(None, 'dp'), may hold values from -6 to 6
- out_grad: bfloat16 [2, 8, 640, 768], P(None, 'dp'), may hold values from -0.119628906 to 0.119628906
- lengths: int32 [2, 8, 2], P(None, 'dp'), may hold values from 32 to 512, as said below
- attn_in: bfloat16 [3, 768, 768], P(None, 'dp', 'tp'), may hold values from -0.21875 to 0.21875
- attn_in_bias: bfloat16 [2, 768], P(None, ('tp', 'dp')), may hold values from -0.59765625 to 0.59765625
- attn_out: bfloat16 [768, 768], P('tp', 'dp'), may hold values from -0.875 to 0.875
- out_biases: bfloat16 [2, 768], P(None, 'dp'), may hold values from -0.59765625 to 0.59765625
- ffn_in: bfloat16 [768, 3072], P('dp', 'tp'), may hold values from -0.21875 to 0.21875
- ffn_in_bias: bfloat16 [3072], P(('tp', 'dp')), may hold values from -1.1953125 to 1.1953125
- ffn_out: bfloat16 [3072, 768], P('tp', 'dp'), may hold values from -0.109375 to 0.109375
- norm_gains: bfloat16 [2, 768], P(None, 'dp'), may hold values from 0.5 to 1.5
- norm_shifts: bfloat16 [2, 768], P(None, 'dp'), may hold values from -0.29882812 to 0.29882812
Outputs:
- out_tokens: bfloat16 [2, 8, 640, 768], P(None, 'dp')
- in_grad: float32 [2, 8, 640, 768], P(None, 'dp')
- loss: float32 [], replicated
- grad_attn_in: float32 [3, 768, 768], P(None, 'dp', 'tp')
- grad_attn_in_bias: float32 [2, 768], P(None, ('tp', 'dp'))
- grad_attn_out: float32 [768, 768], P('tp', 'dp')
- grad_out_biases: float32 [2, 768], P(None, 'dp')
- grad_ffn_in: float32 [768, 3072], P('dp', 'tp')
- grad_ffn_in_bias: float32 [3072], P(('tp', 'dp'))
- grad_ffn_out: float32 [3072, 768], P('tp', 'dp')
- grad_norm_gains: float32 [2, 768], P(None, 'dp')
- grad_norm_shifts: float32 [2, 768], P(None, 'dp')
The draws below stay inside these ranges and needn't reach their ends.
Inputs may be any that keep to these rules, and one draw needn't show every extreme that they name: lengths[m, i, 0] is the query's length, 32 to 128; lengths[m, i, 1] is the passage's length, 64 to 512; in every draw some query has length 128 and some passage length 512.
All inputs are finite; a program needn't handle non-finite values.
Results may differ from the reference program's by a relative error of at most 0.015.
Values may be sent and summed in bfloat16 or wider, within the bound.
No kernel may reach another device: no remote copies, remote signals or barrier semaphores. Data moves between devices by JAX's collectives and lax.ppermute only.
A program may use at most 128 MiB of HBM per device.

```python
import math
import jax
import jax.numpy as jnp
from jax import lax

D = 768
HEADS = 12
HEAD_DIM = 64
FF = 3072
QLEN = 128
PLEN = 512
MICRO = 2
SLOT = 640
PAIRS = 8


def draw_lengths(key, part):
    key = jax.random.fold_in(key, 7)
    subkeys = jax.random.split(key, 4)
    pair_total = MICRO * PAIRS
    query_len = jax.random.randint(subkeys[0], (pair_total,), QLEN // 4, QLEN + 1)
    passage_len = jax.random.randint(subkeys[1], (pair_total,), PLEN // 8, PLEN + 1)
    query_len = query_len.at[jax.random.randint(subkeys[2], (), 0, pair_total)].set(QLEN)
    passage_len = passage_len.at[jax.random.randint(subkeys[3], (), 0, pair_total)].set(PLEN)
    return jnp.stack([query_len, passage_len], axis=-1).reshape(MICRO, PAIRS, 2).astype(jnp.int32)


def levels(stream_key, extent, cuts, smallest, high):
    def one(axis_at, shards_of):
        draws = jax.random.uniform(jax.random.fold_in(jax.random.fold_in(stream_key, 6), axis_at), (shards_of,), jnp.float32, smallest / len(cuts), high / len(cuts))
        return jnp.repeat(jnp.exp(draws), extent[axis_at] // shards_of).reshape((-1,) + (1,) * (len(extent) - axis_at - 1))

    level = one(*cuts[0])
    for cut in cuts[1:]:
        level = level * one(*cut)
    return level


def normal_values(stream_key, extent, spread, bound, cuts=(), held_as=jnp.bfloat16):
    level = levels(stream_key, extent, cuts, -0.22, 0.18) if cuts else 1.0
    drawn = jax.random.normal(stream_key, extent, jnp.float32) * spread * level
    return jnp.minimum(jnp.maximum(drawn, -bound), bound).astype(held_as)


def setup_inputs(seed: int = 0) -> dict:
    arg_keys = jax.random.split(jax.random.key(seed), 13)
    return {
        "tokens": normal_values(arg_keys[0], (MICRO, PAIRS, SLOT, D), 1.0, 6.0, ((1, 8),)),
        "out_grad": normal_values(arg_keys[1], (MICRO, PAIRS, SLOT, D), 0.02, 0.119628906, ((1, 8),)),
        "lengths": draw_lengths(jax.random.fold_in(arg_keys[12], 71), 0),
        "attn_in": normal_values(arg_keys[3], (3, D, D), D ** -0.5, 0.21875, ((1, 8), (2, 4))),
        "attn_in_bias": normal_values(arg_keys[4], (2, D), 0.1, 0.59765625, ((1, 32),)),
        "attn_out": normal_values(arg_keys[5], (D, D), (D // 16) ** -0.5, 0.875, ((0, 4), (1, 8))),
        "out_biases": normal_values(arg_keys[6], (2, D), 0.1, 0.59765625, ((1, 8),)),
        "ffn_in": normal_values(arg_keys[7], (D, FF), D ** -0.5, 0.21875, ((0, 8), (1, 4))),
        "ffn_in_bias": normal_values(arg_keys[8], (FF,), 0.2, 1.1953125, ((0, 32),)),
        "ffn_out": normal_values(arg_keys[9], (FF, D), FF ** -0.5, 0.109375, ((0, 4), (1, 8))),
        "norm_gains": jnp.clip(1.0 + 0.1 * jax.random.normal(arg_keys[10], (2, D), jnp.float32), 0.5, 1.5).astype(jnp.bfloat16),
        "norm_shifts": normal_values(arg_keys[11], (2, D), 0.05, 0.29882812, ((1, 8),)),
    }


@jax.custom_vjp
def low(v):
    return lax.optimization_barrier(v.astype(jnp.bfloat16)).astype(jnp.float32)

@jax.custom_vjp
def low_back(v):
    return v

def low_keep(v):
    return (low(v), None)

def low_pass(kept, grad):
    return (grad,)

def back_keep(v):
    return (v, None)

def back_low(kept, grad):
    return (low(grad),)
low.defvjp(low_keep, low_pass)
low_back.defvjp(back_keep, back_low)
SOFTMAX_TEMP = 0.01

def dense_projection_step(left, right, form):
    return jnp.einsum(form, left, right, precision=lax.Precision.HIGHEST)

def layer_norm(hidden, gain, shift):
    center = hidden - lax.optimization_barrier(jnp.mean(hidden, axis=-1, keepdims=True))
    variance = lax.optimization_barrier(jnp.mean(center * center, axis=-1, keepdims=True))
    return center * lax.rsqrt(variance + 1e-12) * gain + shift

def attend(queries, keys_in, values, length):
    count = queries.shape[0]
    head_q = queries.reshape(count, HEADS, HEAD_DIM)
    head_k = keys_in.reshape(count, HEADS, HEAD_DIM)
    head_v = values.reshape(count, HEADS, HEAD_DIM)
    scores = dense_projection_step(head_q, head_k, 'she,the->hst') * (1.0 / math.sqrt(HEAD_DIM))
    visible = jnp.arange(count) < length
    scores = low_back(jnp.where(visible[None, None, :], scores, -1e+30))
    weights = jax.nn.softmax(scores, axis=-1)
    return dense_projection_step(low(weights), head_v, 'hst,the->she').reshape(count, D)

def pooled(hidden, length):
    visible = (jnp.arange(hidden.shape[0]) < length).astype(jnp.float32)
    summed = lax.optimization_barrier(jnp.sum(hidden * visible[:, None], axis=0)) / length.astype(jnp.float32)
    return summed * lax.rsqrt(jnp.sum(summed * summed) + 1e-06)

def pair_forward(params, token_rows, pair_len):
    attn_in, attn_in_bias, attn_out, out_biases, ffn_in, ffn_in_bias, ffn_out, norm_gains, norm_shifts = params
    projected = dense_projection_step(token_rows, attn_in, 'rd,jdc->jrc')
    queries = low_back(low(projected[0] + attn_in_bias[0]))
    keys_in = low_back(low(projected[1]))
    values = low_back(low(projected[2] + attn_in_bias[1]))
    mixed = jnp.concatenate([attend(queries[:QLEN], keys_in[:QLEN], values[:QLEN], pair_len[0]), attend(queries[QLEN:], keys_in[QLEN:], values[QLEN:], pair_len[1])], axis=0)
    mixed = low_back(low(mixed))
    branch = low_back(dense_projection_step(mixed, attn_out, 'rc,cd->rd') + out_biases[0])
    first = layer_norm(token_rows + branch, norm_gains[0], norm_shifts[0])
    inner = low_back(dense_projection_step(low(first), ffn_in, 'rd,df->rf') + ffn_in_bias)
    hidden = low(jax.nn.gelu(inner, approximate=False))
    second = low_back(dense_projection_step(hidden, ffn_out, 'rf,fd->rd') + out_biases[1])
    final = layer_norm(first + second, norm_gains[1], norm_shifts[1])
    return (final, pooled(final[:QLEN], pair_len[0]), pooled(final[QLEN:], pair_len[1]))

def forward_all(token_rows, params, all_lengths):

    def step(carry, item):
        return (carry, pair_forward(params, item[0], item[1]))
    _, (final, query_embedding, passage_embedding) = lax.scan(jax.checkpoint(step), jnp.zeros((), jnp.float32), (token_rows, all_lengths))
    query_embedding = query_embedding.reshape(MICRO, PAIRS, D)
    passage_embedding = passage_embedding.reshape(MICRO, PAIRS, D)
    similarity_logits = dense_projection_step(query_embedding, passage_embedding, 'rst,rut->rsu') / SOFTMAX_TEMP
    entropy = jax.nn.logsumexp(similarity_logits, axis=-1) - jnp.diagonal(similarity_logits, axis1=1, axis2=2)
    return (final, jnp.sum(entropy))

def reference(tokens, out_grad, lengths, attn_in, attn_in_bias, attn_out, out_biases, ffn_in, ffn_in_bias, ffn_out, norm_gains, norm_shifts):
    params = (attn_in.astype(jnp.float32), attn_in_bias.astype(jnp.float32), attn_out.astype(jnp.float32), out_biases.astype(jnp.float32), ffn_in.astype(jnp.float32), ffn_in_bias.astype(jnp.float32), ffn_out.astype(jnp.float32), norm_gains.astype(jnp.float32), norm_shifts.astype(jnp.float32))
    flat_tokens = tokens.astype(jnp.float32).reshape(MICRO * PAIRS, SLOT, D)
    flat_lengths = lengths.reshape(MICRO * PAIRS, 2).astype(jnp.int32)

    def objective(token_rows, weights):
        return forward_all(token_rows, weights, flat_lengths)
    (final, entropy_sum), pull = jax.vjp(objective, flat_tokens, params)
    positions = jnp.arange(SLOT)[None, :]
    visible = jnp.where(positions < QLEN, positions < flat_lengths[:, 0:1], positions - QLEN < flat_lengths[:, 1:2]).astype(jnp.float32)
    cotangent = out_grad.astype(jnp.float32).reshape(MICRO * PAIRS, SLOT, D) * visible[:, :, None]
    grad_tokens, grads = pull((cotangent, jnp.ones((), jnp.float32)))
    return (final.reshape(MICRO, PAIRS, SLOT, D).astype(jnp.bfloat16), grad_tokens.reshape(MICRO, PAIRS, SLOT, D), entropy_sum / (MICRO * PAIRS), grads[0], grads[1], grads[2], grads[3], grads[4], grads[5], grads[6], grads[7], grads[8])
```

```python
import math

import jax
import jax.numpy as jnp
from jax import lax
from jax.experimental import pallas as pl
from jax.experimental.pallas import tpu as pltpu
from jax.sharding import PartitionSpec as P

HEAD_DIM = 64
QLEN = 128
SOFTMAX_TEMP = 0.01
NEG_LARGE = -1e30
ROOT_HALF = 0.7071067811865476
DENSITY_NORM = 0.3989422804014327
VMEM_BYTES = 56 * 2**20
EXTRA = 16
BF = jnp.bfloat16
F32 = jnp.float32
NN = (((1,), (0,)), ((), ()))
NT = (((1,), (1,)), ((), ()))
TN = (((0,), (0,)), ((), ()))
HBM = pl.BlockSpec(memory_space=pl.ANY)
SMEM = pl.BlockSpec(memory_space=pltpu.SMEM)
VMEM = pl.BlockSpec(memory_space=pltpu.VMEM)


def mm(left, right, dims=NN, precision=None):
    return lax.dot_general(left, right, dims, precision=precision, preferred_element_type=F32)


def shape(dims, dtype):
    return jax.ShapeDtypeStruct(dims, dtype)


def kernel_call(body, name, in_specs, outs, args, flops, moved, scratch=(), out_specs=None, aliases=None):
    return pl.pallas_call(
        body,
        name=name,
        grid=(1,) if out_specs is not None else (),
        in_specs=in_specs,
        out_specs=out_specs if out_specs is not None else [VMEM] * len(outs),
        out_shape=outs,
        scratch_shapes=scratch,
        input_output_aliases=aliases or {},
        compiler_params=pltpu.CompilerParams(vmem_limit_bytes=VMEM_BYTES),
        cost_estimate=pl.CostEstimate(flops=int(flops), bytes_accessed=int(moved), transcendentals=0),
    )(*args)


def micro_spec(arr, micro):
    return pl.BlockSpec((1,) + arr.shape[1:], lambda i: (micro,) + (0,) * (len(arr.shape) - 1))


def assemble_body(block_rows, head_bias, count):
    def body(ids_ref, *refs):
        blocks, (w_ref, vec_ref, bias_ref) = refs[:count], refs[count:]
        width = w_ref.shape[1]
        qkv_width = bias_ref.shape[1]
        vectors = jnp.zeros(vec_ref.shape, F32)
        biases = jnp.zeros(bias_ref.shape, F32)
        lane = lax.broadcasted_iota(jnp.int32, (128, width), 0)
        place = lax.broadcasted_iota(jnp.int32, (128, width), 1)
        for k in range(count):
            owner = ids_ref[2 + k]
            w_ref[pl.ds(pl.multiple_of(owner * block_rows, 16), block_rows), :] = blocks[k][:block_rows, :]
            small = blocks[k][block_rows : block_rows + EXTRA, :128]
            pick = (place == owner * block_rows + lane) & (lane < block_rows)
            vectors += mm(small, jnp.where(pick, 1.0, 0.0).astype(BF))
            biases += mm(small, bias_pick(owner, head_bias, qkv_width, lane, place))
        vec_ref[...] = vectors
        bias_ref[...] = biases

    return body


def bias_pick(owner, head_bias, qkv_width, lane, place):
    lane, place = lane[:, :qkv_width], place[:, :qkv_width]
    values_at = qkv_width * 2 // 3
    for_query = (lane < head_bias) & (place == owner * head_bias + lane)
    for_value = (
        (lane >= head_bias)
        & (lane < 2 * head_bias)
        & (place == values_at + owner * head_bias + lane - head_bias)
    )
    return jnp.where(for_query | for_value, 1.0, 0.0).astype(BF)


def split_halves(full_ref, core, send_ref, keep_ref):
    half = send_ref.shape[0]
    send_ref[...] = full_ref[pl.ds(pl.multiple_of((1 - core) * half, 16), half), :]
    keep_ref[...] = full_ref[pl.ds(pl.multiple_of(core * half, 16), half), :]


def join_halves(full_ref, core, own_ref, other_ref):
    half = own_ref.shape[0]
    full_ref[pl.ds(pl.multiple_of(core * half, 16), half), :] = own_ref[...]
    full_ref[pl.ds(pl.multiple_of((1 - core) * half, 16), half), :] = other_ref[...]


def segments(rows):
    return ((0, QLEN), (QLEN, rows))


def attend_body(micro):
    def body(ids_ref, len_ref, x_ref, w_ref, bias_ref, qkv_ref, mixed_ref, pq_ref, pp_ref, send_ref, keep_ref, full_ref):
        rows = x_ref.shape[2]
        heads = pq_ref.shape[0]
        width = heads * HEAD_DIM
        x = x_ref[micro, 0]
        bias = bias_ref[7:8, :]
        qkv_ref[...] = (mm(x, w_ref[:, : 3 * width]) + bias).astype(BF)
        factor = 1.0 / math.sqrt(HEAD_DIM)
        for seg, (low, high) in enumerate(segments(rows)):
            length = len_ref[micro, 0, seg]
            size = high - low
            p_ref = pp_ref if seg else pq_ref
            visible = lax.broadcasted_iota(jnp.int32, (size, size), 1) < length
            for h in range(heads):
                at = h * HEAD_DIM
                queries = qkv_ref[low:high, at : at + HEAD_DIM]
                keys_low = qkv_ref[low:high, width + at : width + at + HEAD_DIM]
                values = qkv_ref[low:high, 2 * width + at : 2 * width + at + HEAD_DIM]
                scores = jnp.where(visible, mm(queries, keys_low, NT) * factor, NEG_LARGE)
                raised = jnp.exp(scores - jnp.max(scores, axis=-1, keepdims=True))
                weights = (raised / jnp.sum(raised, axis=-1, keepdims=True)).astype(BF)
                p_ref[h] = weights
                mixed_ref[low:high, at : at + HEAD_DIM] = mm(weights, values).astype(BF)
        full_ref[...] = mm(mixed_ref[...], w_ref[:, 3 * width :], NT).astype(BF)
        split_halves(full_ref, ids_ref[0], send_ref, keep_ref)

    return body


def norm_one(x, branch, shift_out):
    hidden = x.astype(F32) + (branch.astype(F32) + shift_out)
    center = hidden - jnp.mean(hidden, axis=-1, keepdims=True)
    inverse = lax.rsqrt(jnp.mean(center * center, axis=-1, keepdims=True) + 1e-12)
    return center * inverse, inverse


def ffn_body(micro, chunk):
    def body(ids_ref, x_ref, own_ref, other_ref, vec_ref, fi_ref, fo_ref, first_ref, low_ref, hidden_ref, slope_ref, send_ref, keep_ref, full_ref):
        rows = x_ref.shape[2]
        join_halves(full_ref, ids_ref[0], own_ref, other_ref)
        for at in range(0, rows, chunk):
            part = slice(at, at + chunk)
            normed, _ = norm_one(x_ref[micro, 0, part, :], full_ref[part, :], vec_ref[0:1, :])
            first = normed * vec_ref[2:3, :] + vec_ref[4:5, :]
            first_ref[part, :] = first
            low = first.astype(BF)
            low_ref[part, :] = low
            inner = mm(low, fi_ref[...]) + vec_ref[6:7, :]
            cumulative = 0.5 * (1.0 + lax.erf(inner * ROOT_HALF))
            density = jnp.exp(-0.5 * inner * inner) * DENSITY_NORM
            hidden = (inner * cumulative).astype(BF)
            hidden_ref[part, :] = hidden
            slope_ref[part, :] = (cumulative + inner * density).astype(BF)
            full_ref[part, :] = mm(hidden, fo_ref[...], NT).astype(BF)
        split_halves(full_ref, ids_ref[0], send_ref, keep_ref)

    return body


def pool_body(micro, aliased):
    def body(ids_ref, len_ref, first_ref, own_ref, other_ref, vec_ref, *refs):
        out_ref, normed_ref, inv_ref, pooled_ref, emb_ref, full_ref = refs[aliased:]
        rows = first_ref.shape[0]
        join_halves(full_ref, ids_ref[0], own_ref, other_ref)
        sums = [0.0, 0.0]
        for at in range(0, rows, QLEN):
            part = slice(at, at + QLEN)
            seg = 1 if at else 0
            hidden = first_ref[part, :] + (full_ref[part, :].astype(F32) + vec_ref[1:2, :])
            center = hidden - jnp.mean(hidden, axis=-1, keepdims=True)
            inverse = lax.rsqrt(jnp.mean(center * center, axis=-1, keepdims=True) + 1e-12)
            normed = center * inverse
            normed_ref[part, :] = normed
            inv_ref[part, :] = inverse
            final = normed * vec_ref[3:4, :] + vec_ref[5:6, :]
            out_ref[0, 0, part, :] = final.astype(BF)
            place = lax.broadcasted_iota(jnp.int32, final.shape, 0) + (at - seg * QLEN)
            kept = jnp.where(place < len_ref[micro, 0, seg], final, 0.0)
            sums[seg] = sums[seg] + jnp.sum(kept, axis=0, keepdims=True)
        for seg in range(2):
            summed = sums[seg] / len_ref[micro, 0, seg].astype(F32)
            unit = summed * lax.rsqrt(jnp.sum(summed * summed, axis=-1, keepdims=True) + 1e-06)
            pooled_ref[seg : seg + 1, :] = summed
            for k in range(emb_ref.shape[0]):
                emb_ref[k, seg : seg + 1, :] = unit

    return body


def loss_grads(queries, passages, own):
    highest = lax.Precision.HIGHEST
    count = queries.shape[0]
    row = lax.broadcasted_iota(jnp.int32, (count, count), 0)
    col = lax.broadcasted_iota(jnp.int32, (count, count), 1)
    same = jnp.where(row == col, 1.0, 0.0)
    logits = mm(queries, passages, NT, highest) / SOFTMAX_TEMP
    top = jnp.max(logits, axis=-1, keepdims=True)
    log_norm = top + jnp.log(jnp.sum(jnp.exp(logits - top), axis=-1, keepdims=True))
    entropy = jnp.sum(jnp.sum(same * (log_norm - logits), axis=-1, keepdims=True), axis=0, keepdims=True)
    grad = (jnp.exp(logits - log_norm) - same) / SOFTMAX_TEMP
    turned = mm(passages, queries, NT, highest) / SOFTMAX_TEMP
    top_t = jnp.max(turned, axis=0, keepdims=True)
    norm_t = top_t + jnp.log(jnp.sum(jnp.exp(turned - top_t), axis=0, keepdims=True))
    grad_t = (jnp.exp(turned - norm_t) - same) / SOFTMAX_TEMP
    own_col = jnp.sum(jnp.where(col == own, grad, 0.0), axis=1, keepdims=True)
    own_row = jnp.sum(jnp.where(col == own, grad_t, 0.0), axis=1, keepdims=True)
    grad_query = jnp.sum(own_row * passages, axis=0, keepdims=True)
    grad_passage = jnp.sum(own_col * queries, axis=0, keepdims=True)
    return entropy, (grad_query, grad_passage)


def norm_backward(upstream, normed, inverse, gain):
    scaled = upstream * gain
    centered = scaled - jnp.mean(scaled, axis=-1, keepdims=True)
    return inverse * (centered - normed * jnp.mean(scaled * normed, axis=-1, keepdims=True))


def ffn_back_body(micro):
    def body(
        ids_ref, len_ref, emb_ref, pooled_ref, cot_ref, normed_ref, inv_ref, slope_ref, vec_ref, fi_ref, fo_ref,
        second_ref, inner_ref, gh_ref, sums_ref, loss_ref, send_ref, keep_ref, full_ref,
    ):
        rows = normed_ref.shape[0]
        entropy, unit_grads = loss_grads(emb_ref[:, 0, :], emb_ref[:, 1, :], ids_ref[1])
        loss_ref[...] = jnp.broadcast_to(entropy, loss_ref.shape)
        spread = []
        for seg in range(2):
            summed = pooled_ref[seg : seg + 1, :]
            up = unit_grads[seg]
            inverse = lax.rsqrt(jnp.sum(summed * summed, axis=-1, keepdims=True) + 1e-06)
            cubed = inverse * inverse * inverse
            grad = inverse * up - cubed * summed * jnp.sum(summed * up, axis=-1, keepdims=True)
            spread.append(grad / len_ref[micro, 0, seg].astype(F32))
        gain_sum, shift_sum, bias_sum = 0.0, 0.0, 0.0
        for at in range(0, rows, QLEN):
            part = slice(at, at + QLEN)
            seg = 1 if at else 0
            cot = cot_ref[micro, 0, part, :].astype(F32) + spread[seg]
            place = lax.broadcasted_iota(jnp.int32, cot.shape, 0) + (at - seg * QLEN)
            grad_final = jnp.where(place < len_ref[micro, 0, seg], cot, 0.0)
            normed = normed_ref[part, :]
            grad_h = norm_backward(grad_final, normed, inv_ref[part, :], vec_ref[3:4, :])
            gh_ref[part, :] = grad_h
            low = grad_h.astype(BF)
            second_ref[part, :] = low
            gain_sum = gain_sum + jnp.sum(grad_final * normed, axis=0, keepdims=True)
            shift_sum = shift_sum + jnp.sum(grad_final, axis=0, keepdims=True)
            bias_sum = bias_sum + jnp.sum(low.astype(F32), axis=0, keepdims=True)
        grad_hidden = mm(second_ref[...], fo_ref[...])
        grad_inner = (grad_hidden * slope_ref[...].astype(F32)).astype(BF)
        inner_ref[...] = grad_inner
        inner_sum = jnp.sum(grad_inner.astype(F32), axis=0, keepdims=True)
        full_ref[...] = mm(inner_ref[...], fi_ref[...], NT).astype(BF)
        split_halves(full_ref, ids_ref[0], send_ref, keep_ref)
        sums_ref[...] = jnp.zeros(sums_ref.shape, F32)
        sums_ref[1:2, :] = bias_sum
        sums_ref[3:4, :] = gain_sum
        sums_ref[5:6, :] = shift_sum
        sums_ref[6:7, :] = inner_sum

    return body


def attend_back_body(micro):
    def body(
        ids_ref, x_ref, branch_own_ref, branch_other_ref, own_ref, other_ref, gh_ref, qkv_ref, mixed_ref, pq_ref, pp_ref, vec_ref, w_ref,
        branch_ref, gqkv_ref, gh1_ref, sums_ref, bias_ref, send_ref, keep_ref, full_ref, sum_ref, gm_ref,
    ):
        rows = x_ref.shape[2]
        heads = pq_ref.shape[0]
        width = heads * HEAD_DIM
        core = ids_ref[0]
        join_halves(full_ref, core, branch_own_ref, branch_other_ref)
        join_halves(sum_ref, core, own_ref, other_ref)
        gain_sum, shift_sum, out_sum = 0.0, 0.0, 0.0
        for at in range(0, rows, QLEN):
            part = slice(at, at + QLEN)
            normed, inverse = norm_one(x_ref[micro, 0, part, :], full_ref[part, :], vec_ref[0:1, :])
            upstream = sum_ref[part, :].astype(F32) + gh_ref[part, :]
            grad_h = norm_backward(upstream, normed, inverse, vec_ref[2:3, :])
            gh1_ref[part, :] = grad_h
            low = grad_h.astype(BF)
            branch_ref[part, :] = low
            gain_sum = gain_sum + jnp.sum(upstream * normed, axis=0, keepdims=True)
            shift_sum = shift_sum + jnp.sum(upstream, axis=0, keepdims=True)
            out_sum = out_sum + jnp.sum(low.astype(F32), axis=0, keepdims=True)
        sums_ref[...] = jnp.zeros(sums_ref.shape, F32)
        sums_ref[0:1, :] = out_sum
        sums_ref[2:3, :] = gain_sum
        sums_ref[4:5, :] = shift_sum
        gm_ref[...] = mm(branch_ref[...], w_ref[:, 3 * width :]).astype(BF)
        factor = 1.0 / math.sqrt(HEAD_DIM)
        for seg, (low_row, high_row) in enumerate(segments(rows)):
            part = slice(low_row, high_row)
            p_ref = pp_ref if seg else pq_ref
            for h in range(heads):
                at = h * HEAD_DIM
                columns = [slice(j * width + at, j * width + at + HEAD_DIM) for j in range(3)]
                grad = gm_ref[part, columns[0]]
                weights = p_ref[h]
                grad_values = mm(weights, grad, TN)
                delta = jnp.sum(grad.astype(F32) * mixed_ref[part, columns[0]].astype(F32), axis=-1, keepdims=True)
                grad_weights = mm(grad, qkv_ref[part, columns[2]], NT)
                grad_scores = (weights.astype(F32) * (grad_weights - delta)).astype(BF)
                gqkv_ref[part, columns[0]] = (mm(grad_scores, qkv_ref[part, columns[1]]) * factor).astype(BF)
                gqkv_ref[part, columns[1]] = (mm(grad_scores, qkv_ref[part, columns[0]], TN) * factor).astype(BF)
                gqkv_ref[part, columns[2]] = grad_values.astype(BF)
        gqkv = gqkv_ref[...]
        bias_ref[...] = jnp.zeros(bias_ref.shape, F32)
        bias_ref[7:8, :] = jnp.sum(gqkv.astype(F32), axis=0, keepdims=True)
        full_ref[...] = mm(gqkv, w_ref[:, : 3 * width], NT).astype(BF)
        split_halves(full_ref, core, send_ref, keep_ref)

    return body


def ffn_weight_body(block_rows, count):
    def body(ids_ref, low_a, low_b, gi_a, gi_b, hid_a, hid_b, gs_a, gs_b, *refs):
        outs, (fi_ref, fo_ref) = refs[:-2], refs[-2:]
        fi_ref[...] = mm(low_a[...], gi_a[...], TN) + mm(low_b[...], gi_b[...], TN)
        fo_ref[...] = mm(gs_a[...], hid_a[...], TN) + mm(gs_b[...], hid_b[...], TN)
        for k in range(count):
            at = pl.ds(pl.multiple_of(ids_ref[2 + k] * block_rows, 16), block_rows)
            outs[k][:block_rows, :] = fi_ref[at, :].astype(BF)
            outs[k][block_rows:, :] = fo_ref[at, :].astype(BF)

    return body


def attend_weight_body(block_rows, head_bias, count):
    def body(
        ids_ref, x_ref, gq_a, gq_b, gb_a, gb_b, mx_a, mx_b, s4_a, s4_b, s5_a, s5_b, b_a, b_b, *refs
    ):
        outs, (w_ref,) = refs[:-1], refs[-1:]
        qkv = gq_a.shape[1]
        width = w_ref.shape[0]
        w_ref[:, :qkv] = mm(x_ref[0, 0], gq_a[...], TN) + mm(x_ref[1, 0], gq_b[...], TN)
        w_ref[:, qkv:] = mm(gb_a[...], mx_a[...], TN) + mm(gb_b[...], mx_b[...], TN)
        sums = (s4_a[...] + s4_b[...] + s5_a[...] + s5_b[...]).astype(BF)
        biases = (b_a[...] + b_b[...]).astype(BF)
        lane = lax.broadcasted_iota(jnp.int32, (128, width), 0)
        place = lax.broadcasted_iota(jnp.int32, (128, width), 1)
        for k in range(count):
            owner = ids_ref[2 + k]
            at = pl.ds(pl.multiple_of(owner * block_rows, 16), block_rows)
            outs[k][:block_rows, :] = w_ref[at, :].astype(BF)
            outs[k][block_rows:, 128:] = jnp.zeros((EXTRA, width - 128), BF)
            pick = (place == owner * block_rows + lane) & (lane < block_rows)
            small = mm(sums, jnp.where(pick, 1.0, 0.0).astype(BF), NT)
            small += mm(biases, bias_pick(owner, head_bias, qkv, lane, place), NT)
            outs[k][block_rows:, :128] = small.astype(BF)

    return body


def finish_body(aliased):
    def body(ids_ref, gh_ref, own_ref, other_ref, *refs):
        out_ref = refs[aliased]
        core = ids_ref[0]
        half = own_ref.shape[0]
        for piece, at in ((own_ref, core), (other_ref, 1 - core)):
            part = pl.ds(pl.multiple_of(at * half, 16), half)
            out_ref[0, 0, part, :] = piece[...].astype(F32) + gh_ref[part, :]

    return body


def core_swap(value, count):
    return lax.ppermute(value, "tp", [(i, i ^ 1) for i in range(count)])


def chip_swap(value, count):
    return lax.ppermute(value, "tp", [(i, i ^ 2) for i in range(count)])


def add_low(left, right):
    return (left.astype(F32) + right.astype(F32)).astype(BF)


def tp_sum(send, keep, count):
    mine = add_low(keep, core_swap(send, count))
    total = add_low(mine, chip_swap(mine, count))
    return total, core_swap(total, count)


def ring_order(count):
    return list(range(0, count, 2)) + list(range(count - 1, 0, -2))


def ring_step(value, order, step):
    count = len(order)
    return lax.ppermute(value, "dp", [(order[i], order[(i + step) % count]) for i in range(count)])


def ring_gather(block, order):
    count = len(order)
    up = count // 2
    ahead, behind = [], []
    from_behind = from_ahead = block
    for step in range(up):
        from_behind = ring_step(from_behind, order, 1)
        behind.append(from_behind)
        if step < count - 1 - up:
            from_ahead = ring_step(from_ahead, order, -1)
            ahead.append(from_ahead)
    return [block] + ahead + behind[::-1]


def ring_scatter(blocks, order):
    count = len(order)
    up = count // 2
    moving_up = blocks[up]
    moving_down = blocks[up + 1]
    for step in range(up):
        moving_up = ring_step(moving_up, order, 1)
        if step < up - 1:
            moving_up = add_low(moving_up, blocks[up - 1 - step])
        if step < count - 1 - up:
            moving_down = ring_step(moving_down, order, -1)
            if step < count - 2 - up:
                moving_down = add_low(moving_down, blocks[up + 2 + step])
    return moving_up.astype(F32) + moving_down.astype(F32) + blocks[0].astype(F32)


def on_device(mesh_tp, mesh_dp, *arrays):
    tokens, out_grad, lengths, attn_in, attn_in_bias, attn_out, out_biases, ffn_in, ffn_in_bias, ffn_out, norm_gains, norm_shifts = arrays
    micro_count, _, rows, width = tokens.shape
    block = attn_in.shape[1]
    inner_width = ffn_in.shape[1]
    head_width = attn_in.shape[2]
    heads = head_width // HEAD_DIM
    qkv_width = 3 * head_width
    head_bias = attn_in_bias.shape[1]
    half = rows // 2
    ring = block % 16 == 0
    order = ring_order(mesh_dp)
    place_of = [order.index(i) for i in range(mesh_dp)]
    dp_at = lax.axis_index("dp")
    if ring:
        around = (jnp.asarray(place_of, jnp.int32)[dp_at] + jnp.arange(mesh_dp, dtype=jnp.int32)) % mesh_dp
        owners = jnp.asarray(order, jnp.int32)[around]
    else:
        owners = jnp.arange(mesh_dp, dtype=jnp.int32)
    ids = jnp.concatenate([jnp.stack([lax.axis_index("tp") % 2, dp_at]).astype(jnp.int32), owners])

    attn_rows = jnp.concatenate([attn_in.transpose(1, 0, 2).reshape(block, qkv_width), attn_out.T], axis=1)
    vectors = jnp.concatenate(
        [
            out_biases,
            norm_gains,
            norm_shifts,
            ffn_in_bias[None],
            jnp.pad(attn_in_bias.reshape(1, 2 * head_bias), ((0, 0), (0, block - 2 * head_bias))),
        ]
    )
    all_cols = qkv_width + head_width
    vec_shape, bias_shape = shape((EXTRA, width), F32), shape((EXTRA, qkv_width), F32)
    if ring:
        small = jnp.pad(vectors, ((0, EXTRA - 8), (0, all_cols - block)))
        blocks = ring_gather(jnp.concatenate([attn_rows, small]), order)
        w_attn, vec, qkv_bias = kernel_call(
            assemble_body(block, head_bias, mesh_dp),
            "assemble",
            [SMEM] + [VMEM] * mesh_dp,
            [shape((width, all_cols), BF), vec_shape, bias_shape],
            [ids] + blocks,
            1e8,
            3e6,
        )
    else:
        w_attn = lax.all_gather(attn_rows, "dp", axis=0, tiled=True)
        every = lax.all_gather(vectors, "dp", axis=0).astype(F32)
        vec = jnp.pad(every.transpose(1, 0, 2).reshape(8, width), ((0, EXTRA - 8), (0, 0)))
        pair = every[:, 7, : 2 * head_bias].reshape(mesh_dp, 2, head_bias).transpose(1, 0, 2).reshape(2, head_width)
        both = jnp.concatenate([pair[0], jnp.zeros((head_width,), F32), pair[1]])
        qkv_bias = jnp.pad(both[None], ((7, EXTRA - 8), (0, 0)))
    w_fi = lax.all_gather(ffn_in, "dp", axis=0, tiled=True)
    w_fo = lax.all_gather(ffn_out.T, "dp", axis=0, tiled=True)

    halves = [shape((half, width), BF)] * 2
    full_low = pltpu.VMEM((rows, width), BF)
    micros = range(micro_count)
    matmul = 2.0 * rows * width

    attended, branch = [], []
    for m in micros:
        qkv, mixed, p_query, p_passage, send, keep = kernel_call(
            attend_body(m),
            "attend",
            [SMEM, SMEM, VMEM, VMEM, VMEM],
            [
                shape((rows, qkv_width), BF),
                shape((rows, head_width), BF),
                shape((heads, QLEN, QLEN), BF),
                shape((heads, rows - QLEN, rows - QLEN), BF),
            ]
            + halves,
            [ids, lengths, tokens, w_attn, qkv_bias],
            matmul * all_cols * 4,
            6e6,
            scratch=[full_low],
        )
        attended.append((qkv, mixed, p_query, p_passage))
        branch.append(tp_sum(send, keep, mesh_tp))

    fed, second = [], []
    for m in micros:
        first, first_low, hidden, slope, send, keep = kernel_call(
            ffn_body(m, half),
            "ffn",
            [SMEM] + [VMEM] * 6,
            [
                shape((rows, width), F32),
                shape((rows, width), BF),
                shape((rows, inner_width), BF),
                shape((rows, inner_width), BF),
            ]
            + halves,
            [ids, tokens, *branch[m], vec, w_fi, w_fo],
            matmul * inner_width * 3,
            9e6,
            scratch=[full_low],
        )
        fed.append((first, first_low, hidden, slope))
        second.append(tp_sum(send, keep, mesh_tp))

    out_tokens = None
    pooled = []
    for m in micros:
        aliased = 0 if out_tokens is None else 1
        out_tokens, normed, inverse, sums, emb = kernel_call(
            pool_body(m, aliased),
            "pool",
            [SMEM, SMEM] + [VMEM] * 4 + [HBM] * aliased,
            [
                shape(tokens.shape, BF),
                shape((rows, width), F32),
                shape((rows, 1), F32),
                shape((8, width), F32),
                shape((mesh_dp, 2, width), F32),
            ],
            [ids, lengths, fed[m][0], *second[m], vec] + ([out_tokens] if aliased else []),
            2e8,
            6e6,
            scratch=[full_low],
            out_specs=[micro_spec(tokens, m)] + [VMEM] * 4,
            aliases={6: 0} if aliased else None,
        )
        gathered = lax.all_to_all(emb, "dp", 0, 0, tiled=True)
        pooled.append((normed, inverse, sums, gathered))

    back, grad_first, entropies = [], [], []
    for m in micros:
        normed, inverse, sums, gathered = pooled[m]
        grad_second, grad_inner, grad_h2, sums4, entropy, send, keep = kernel_call(
            ffn_back_body(m),
            "ffn_back",
            [SMEM, SMEM] + [VMEM] * 9,
            [
                shape((rows, width), BF),
                shape((rows, inner_width), BF),
                shape((rows, width), F32),
                shape((EXTRA, width), F32),
                shape((8, 128), F32),
            ]
            + halves,
            [ids, lengths, gathered, sums, out_grad, normed, inverse, fed[m][3], vec, w_fi, w_fo],
            matmul * inner_width * 3,
            10e6,
            scratch=[full_low],
        )
        back.append((grad_second, grad_inner, grad_h2, sums4))
        entropies.append(entropy[0, 0])
        grad_first.append(tp_sum(send, keep, mesh_tp))

    def pairs(items):
        return [item for item in items]

    if ring:
        ffn_outs = [shape((2 * block, width), BF)] * mesh_dp
        ffn_blocks = kernel_call(
            ffn_weight_body(block, mesh_dp),
            "ffn_weights",
            [SMEM] + [VMEM] * 8,
            ffn_outs,
            [ids] + [fed[m][1] for m in micros] + [back[m][1] for m in micros] + [fed[m][2] for m in micros] + [back[m][0] for m in micros],
            matmul * inner_width * 4,
            14e6,
            scratch=[pltpu.VMEM((width, inner_width), F32)] * 2,
        )
        ffn_total = ring_scatter(list(ffn_blocks), order)
        grad_fi, grad_fo = ffn_total[:block], ffn_total[block:].T
    else:
        grad_fi = sum(mm(fed[m][1], back[m][1], TN) for m in micros)
        grad_fo = sum(mm(back[m][0], fed[m][2], TN) for m in micros)
        grad_fi = lax.psum_scatter(grad_fi, "dp", scatter_dimension=0, tiled=True)
        grad_fo = lax.psum_scatter(grad_fo, "dp", scatter_dimension=0, tiled=True).T

    in_grad = None
    last = []
    for m in micros:
        qkv, mixed, p_query, p_passage = attended[m]
        grad_branch, grad_qkv, grad_h1, sums5, bias5, send, keep = kernel_call(
            attend_back_body(m),
            "attend_back",
            [SMEM] + [VMEM] * 12,
            [
                shape((rows, width), BF),
                shape((rows, qkv_width), BF),
                shape((rows, width), F32),
                shape((EXTRA, width), F32),
                shape((EXTRA, qkv_width), F32),
            ]
            + halves,
            [ids, tokens, *branch[m], *grad_first[m], back[m][2], qkv, mixed, p_query, p_passage, vec, w_attn],
            matmul * all_cols * 6,
            12e6,
            scratch=[full_low, full_low, pltpu.VMEM((rows, head_width), BF)],
        )
        last.append((grad_branch, grad_qkv, sums5, bias5))
        aliased = 0 if in_grad is None else 1
        in_grad = kernel_call(
            finish_body(aliased),
            "finish",
            [SMEM] + [VMEM] * 3 + [HBM] * aliased,
            [shape(tokens.shape, F32)],
            [ids, grad_h1, *tp_sum(send, keep, mesh_tp)] + ([in_grad] if aliased else []),
            1e8,
            5e6,
            out_specs=[micro_spec(tokens, m)],
            aliases={4: 0} if aliased else None,
        )[0]

    if ring:
        attn_blocks = kernel_call(
            attend_weight_body(block, head_bias, mesh_dp),
            "attend_weights",
            [SMEM] + [VMEM] * 13,
            [shape((block + EXTRA, all_cols), BF)] * mesh_dp,
            [ids, tokens]
            + [last[m][1] for m in micros]
            + [last[m][0] for m in micros]
            + [attended[m][1] for m in micros]
            + [back[m][3] for m in micros]
            + [last[m][2] for m in micros]
            + [last[m][3] for m in micros],
            matmul * all_cols * 2,
            8e6,
            scratch=[pltpu.VMEM((width, all_cols), F32)],
        )
        attn_total = ring_scatter(list(attn_blocks), order)
        small = attn_total[block : block + 8, :block]
        attn_total = attn_total[:block]
    else:
        grad_w = sum(
            jnp.concatenate([mm(tokens[m, 0], last[m][1], TN), mm(last[m][0], attended[m][1], TN)], axis=1) for m in micros
        )
        attn_total = lax.psum_scatter(grad_w, "dp", scatter_dimension=0, tiled=True)
        sums = sum(back[m][3] + last[m][2] for m in micros)[:8].reshape(8, mesh_dp, block).transpose(1, 0, 2)
        bias = sum(last[m][3] for m in micros)[7].reshape(3, mesh_dp, head_bias)[0::2].transpose(1, 0, 2)
        bias = jnp.pad(bias.reshape(mesh_dp, 1, 2 * head_bias), ((0, 0), (7, 0), (0, block - 2 * head_bias)))
        small = lax.psum_scatter(sums + bias, "dp", scatter_dimension=0)

    loss = sum(entropies) / (micro_count * mesh_dp)
    return (
        out_tokens,
        in_grad,
        loss,
        attn_total[:, :qkv_width].reshape(block, 3, head_width).transpose(1, 0, 2),
        small[7, : 2 * head_bias].reshape(2, head_bias),
        attn_total[:, qkv_width:].T,
        small[0:2],
        grad_fi,
        small[6],
        grad_fo,
        small[2:4],
        small[4:6],
    )


def solution(mesh):
    placed = (
        P(None, "dp", None, None),
        P(None, "dp", None, None),
        P(None, "dp", None),
        P(None, "dp", "tp"),
        P(None, ("tp", "dp")),
        P("tp", "dp"),
        P(None, "dp"),
        P("dp", "tp"),
        P(("tp", "dp")),
        P("tp", "dp"),
        P(None, "dp"),
        P(None, "dp"),
    )
    sizes = (mesh.shape["tp"], mesh.shape["dp"])

    def run(*arrays):
        return on_device(*sizes, *arrays)

    return jax.shard_map(
        run,
        mesh=mesh,
        in_specs=placed,
        out_specs=placed[:2] + (P(),) + placed[3:],
        check_vma=False,
    )
```

```python
import math

import jax
import jax.numpy as jnp
from jax import lax
from jax.experimental import pallas as pl
from jax.experimental.pallas import tpu as pltpu
from jax.sharding import PartitionSpec as P

HEAD_DIM = 64
QLEN = 128
SOFTMAX_TEMP = 0.01
NEG_LARGE = -1e30
ROOT_HALF = 0.7071067811865476
DENSITY_NORM = 0.3989422804014327
VMEM_BYTES = 20 * 2**20
EXTRA = 16
BF = jnp.bfloat16
F32 = jnp.float32
NN = (((1,), (0,)), ((), ()))
NT = (((1,), (1,)), ((), ()))
TN = (((0,), (0,)), ((), ()))
HBM = pl.BlockSpec(memory_space=pl.ANY)
SMEM = pl.BlockSpec(memory_space=pltpu.SMEM)
VMEM = pl.BlockSpec(memory_space=pltpu.VMEM)


def mm(left, right, dims=NN, precision=None):
    return lax.dot_general(left, right, dims, precision=precision, preferred_element_type=F32)


def shape(dims, dtype):
    return jax.ShapeDtypeStruct(dims, dtype)


def kernel_call(body, name, in_specs, outs, args, flops, moved, scratch=(), out_specs=None, aliases=None):
    return pl.pallas_call(
        body,
        name=name,
        grid=(1,) if out_specs is not None else (),
        in_specs=in_specs,
        out_specs=out_specs if out_specs is not None else [VMEM] * len(outs),
        out_shape=outs,
        scratch_shapes=scratch,
        input_output_aliases=aliases or {},
        compiler_params=pltpu.CompilerParams(vmem_limit_bytes=VMEM_BYTES),
        cost_estimate=pl.CostEstimate(flops=int(flops), bytes_accessed=int(moved), transcendentals=0),
    )(*args)


def micro_spec(arr, micro):
    return pl.BlockSpec((1,) + arr.shape[1:], lambda i: (micro,) + (0,) * (len(arr.shape) - 1))


def ring_owner(at, step, count):
    half = count // 2
    place = jnp.where(at % 2 == 0, at // 2, half + (count - 1 - at) // 2)
    place = (place + step) % count
    return jnp.where(place < half, 2 * place, count - 1 - 2 * (place - half))


def pack_body(*refs):
    sources, (attn_ref, ffn_ref), held, sem = refs[:9], refs[9:11], refs[11:20], refs[20]
    copies = [pltpu.make_async_copy(sources[k], held[k], sem.at[k]) for k in range(9)]
    for copy in copies:
        copy.start()
    for copy in copies:
        copy.wait()
    ai_ref, ab_ref, ao_ref, ob_ref, fi_ref, fb_ref, fo_ref, ng_ref, ns_ref = held
    block, head_width = ai_ref.shape[1], ai_ref.shape[2]
    head_bias = ab_ref.shape[1]
    for j in range(3):
        attn_ref[:block, j * head_width : (j + 1) * head_width] = ai_ref[j]
    attn_ref[:block, 3 * head_width :] = ao_ref[...].T
    attn_ref[block:, :] = jnp.zeros((attn_ref.shape[0] - block, attn_ref.shape[1]), BF)
    small = [ob_ref[...], ng_ref[...], ns_ref[...], fb_ref[...]]
    small.append(jnp.concatenate([ab_ref[0:1, :], ab_ref[1:2, :], jnp.zeros((1, block - 2 * head_bias), BF)], axis=1))
    attn_ref[block : block + 8, :block] = jnp.concatenate([part.astype(F32) for part in small]).astype(BF)
    ffn_ref[:block, :] = fi_ref[...]
    ffn_ref[block:, :] = fo_ref[...]


def assemble_body(block_rows, head_bias, count):
    def body(ids_ref, *refs):
        blocks, (w_ref, vec_ref, bias_ref) = refs[:count], refs[count:]
        width = w_ref.shape[1]
        qkv_width = bias_ref.shape[1]
        vectors = jnp.zeros(vec_ref.shape, F32)
        biases = jnp.zeros(bias_ref.shape, F32)
        lane = lax.broadcasted_iota(jnp.int32, (128, width), 0)
        place = lax.broadcasted_iota(jnp.int32, (128, width), 1)
        for k in range(count):
            owner = ring_owner(ids_ref[1], k, count)
            w_ref[pl.ds(pl.multiple_of(owner * block_rows, 16), block_rows), :] = blocks[k][:block_rows, :]
            small = blocks[k][block_rows : block_rows + EXTRA, :128]
            pick = (place == owner * block_rows + lane) & (lane < block_rows)
            vectors += mm(small, jnp.where(pick, 1.0, 0.0).astype(BF))
            biases += mm(small, bias_pick(owner, head_bias, qkv_width, lane, place))
        vec_ref[...] = vectors
        bias_ref[...] = biases

    return body


def assemble_pair_body(block_rows, count):
    def body(ids_ref, *refs):
        blocks, (fi_ref, fo_ref) = refs[:count], refs[count:]
        for k in range(count):
            owner = ring_owner(ids_ref[1], k, count)
            at = pl.ds(pl.multiple_of(owner * block_rows, 16), block_rows)
            fi_ref[at, :] = blocks[k][:block_rows, :]
            fo_ref[at, :] = blocks[k][block_rows:, :]

    return body


def bias_pick(owner, head_bias, qkv_width, lane, place):
    lane, place = lane[:, :qkv_width], place[:, :qkv_width]
    values_at = qkv_width * 2 // 3
    for_query = (lane < head_bias) & (place == owner * head_bias + lane)
    for_value = (
        (lane >= head_bias)
        & (lane < 2 * head_bias)
        & (place == values_at + owner * head_bias + lane - head_bias)
    )
    return jnp.where(for_query | for_value, 1.0, 0.0).astype(BF)


def split_halves(full_ref, core, send_a, send_b, keep_ref):
    half, piece = keep_ref.shape[0], send_a.shape[0]
    keep_ref[...] = full_ref[pl.ds(pl.multiple_of(core * half, 16), half), :]
    for k, ref in enumerate((send_a, send_b)):
        ref[...] = full_ref[pl.ds(pl.multiple_of((1 - core) * half + k * piece, 16), piece), :]


def half_body(keep_ref, a_ref, b_ref, out_ref):
    piece = a_ref.shape[0]
    for k, ref in enumerate((a_ref, b_ref)):
        part = slice(k * piece, (k + 1) * piece)
        out_ref[part, :] = add_low(keep_ref[part, :], ref[...])


def join_halves(full_ref, core, parts):
    half = parts[0].shape[0]
    for near, far, place in ((parts[0], parts[1], core), (parts[2], parts[3], 1 - core)):
        full_ref[pl.ds(pl.multiple_of(place * half, 16), half), :] = near[...].astype(F32) + far[...].astype(F32)


def segments(rows):
    return ((0, QLEN), (QLEN, rows))


def attend_body():
    def body(ids_ref, len_ref, x_ref, w_ref, bias_ref, qkv_ref, mixed_ref, pq_ref, pp_ref, send_a, send_b, keep_ref, part_ref):
        micro = ids_ref[2]
        rows = x_ref.shape[2]
        heads = pq_ref.shape[0]
        width = heads * HEAD_DIM
        x = x_ref[micro, 0]
        bias = bias_ref[7:8, :]
        qkv_ref[...] = (mm(x, w_ref[:, : 3 * width]) + bias).astype(BF)
        factor = 1.0 / math.sqrt(HEAD_DIM)
        for seg, (low, high) in enumerate(segments(rows)):
            length = len_ref[micro, 0, seg]
            size = high - low
            p_ref = pp_ref if seg else pq_ref
            visible = lax.broadcasted_iota(jnp.int32, (size, size), 1) < length
            for h in range(heads):
                at = h * HEAD_DIM
                queries = qkv_ref[low:high, at : at + HEAD_DIM]
                keys_low = qkv_ref[low:high, width + at : width + at + HEAD_DIM]
                values = qkv_ref[low:high, 2 * width + at : 2 * width + at + HEAD_DIM]
                scores = jnp.where(visible, mm(queries, keys_low, NT) * factor, NEG_LARGE)
                raised = jnp.exp(scores - jnp.max(scores, axis=-1, keepdims=True))
                weights = (raised / jnp.sum(raised, axis=-1, keepdims=True)).astype(BF)
                p_ref[h] = weights
                mixed_ref[low:high, at : at + HEAD_DIM] = mm(weights, values).astype(BF)
        part_ref[...] = mm(mixed_ref[...], w_ref[:, 3 * width :], NT).astype(BF)
        split_halves(part_ref, ids_ref[0], send_a, send_b, keep_ref)

    return body


def norm_one(x, branch, shift_out):
    hidden = x.astype(F32) + (branch.astype(F32) + shift_out)
    center = hidden - jnp.mean(hidden, axis=-1, keepdims=True)
    inverse = lax.rsqrt(jnp.mean(center * center, axis=-1, keepdims=True) + 1e-12)
    return center * inverse, inverse


def ffn_body(chunk):
    def body(ids_ref, x_ref, s0, s1, s2, s3, vec_ref, fi_ref, fo_ref, normed_ref, inv_ref, first_ref, low_ref, hidden_ref, slope_ref, send_a, send_b, keep_ref, full_ref, part_ref):
        micro = ids_ref[2]
        rows = x_ref.shape[2]
        join_halves(full_ref, ids_ref[0], (s0, s1, s2, s3))
        for at in range(0, rows, chunk):
            part = slice(at, at + chunk)
            normed, inverse = norm_one(x_ref[micro, 0, part, :], full_ref[part, :], vec_ref[0:1, :])
            normed_ref[part, :] = normed.astype(BF)
            inv_ref[part, :] = inverse
            first = normed * vec_ref[2:3, :] + vec_ref[4:5, :]
            first_ref[part, :] = first
            low = first.astype(BF)
            low_ref[part, :] = low
            inner = mm(low, fi_ref[...]) + vec_ref[6:7, :]
            cumulative = 0.5 * (1.0 + lax.erf(inner * ROOT_HALF))
            density = jnp.exp(-0.5 * inner * inner) * DENSITY_NORM
            hidden = (inner * cumulative).astype(BF)
            hidden_ref[part, :] = hidden
            slope_ref[part, :] = (cumulative + inner * density).astype(BF)
            part_ref[part, :] = mm(hidden, fo_ref[...], NT).astype(BF)
        split_halves(part_ref, ids_ref[0], send_a, send_b, keep_ref)

    return body


def pool_body(aliased):
    def body(ids_ref, len_ref, first_ref, s0, s1, s2, s3, vec_ref, *refs):
        out_ref, normed_ref, inv_ref, pooled_ref, emb_ref, full_ref = refs[aliased:]
        micro = ids_ref[2]
        rows = first_ref.shape[0]
        join_halves(full_ref, ids_ref[0], (s0, s1, s2, s3))
        pooled_ref[...] = jnp.zeros(pooled_ref.shape, F32)

        def step(k, carry):
            part = pl.ds(pl.multiple_of(k * QLEN, QLEN), QLEN)
            seg = jnp.minimum(k, 1)
            hidden = first_ref[part, :] + (full_ref[part, :] + vec_ref[1:2, :])
            center = hidden - jnp.mean(hidden, axis=-1, keepdims=True)
            inverse = lax.rsqrt(jnp.mean(center * center, axis=-1, keepdims=True) + 1e-12)
            normed = center * inverse
            normed_ref[part, :] = normed.astype(BF)
            inv_ref[part, :] = inverse
            final = normed * vec_ref[3:4, :] + vec_ref[5:6, :]
            out_ref[0, 0, part, :] = final.astype(BF)
            place = lax.broadcasted_iota(jnp.int32, final.shape, 0) + (k - seg) * QLEN
            kept = jnp.where(place < len_ref[micro, 0, seg], final, 0.0)
            pooled_ref[pl.ds(seg, 1), :] += jnp.sum(kept, axis=0, keepdims=True)
            return carry

        lax.fori_loop(0, rows // QLEN, step, 0)
        for seg in range(2):
            summed = pooled_ref[seg : seg + 1, :] / len_ref[micro, 0, seg].astype(F32)
            unit = summed * lax.rsqrt(jnp.sum(summed * summed, axis=-1, keepdims=True) + 1e-06)
            pooled_ref[seg : seg + 1, :] = summed
            emb_ref[0, seg : seg + 1, :] = unit

    return body


def loss_grads(queries, passages, own):
    highest = lax.Precision.HIGHEST
    count = queries.shape[0]
    row = lax.broadcasted_iota(jnp.int32, (count, count), 0)
    col = lax.broadcasted_iota(jnp.int32, (count, count), 1)
    same = jnp.where(row == col, 1.0, 0.0)
    logits = mm(queries, passages, NT, highest) / SOFTMAX_TEMP
    top = jnp.max(logits, axis=-1, keepdims=True)
    log_norm = top + jnp.log(jnp.sum(jnp.exp(logits - top), axis=-1, keepdims=True))
    entropy = jnp.sum(jnp.sum(same * (log_norm - logits), axis=-1, keepdims=True), axis=0, keepdims=True)
    grad = (jnp.exp(logits - log_norm) - same) / SOFTMAX_TEMP
    turned = mm(passages, queries, NT, highest) / SOFTMAX_TEMP
    top_t = jnp.max(turned, axis=0, keepdims=True)
    norm_t = top_t + jnp.log(jnp.sum(jnp.exp(turned - top_t), axis=0, keepdims=True))
    grad_t = (jnp.exp(turned - norm_t) - same) / SOFTMAX_TEMP
    own_col = jnp.sum(jnp.where(col == own, grad, 0.0), axis=1, keepdims=True)
    own_row = jnp.sum(jnp.where(col == own, grad_t, 0.0), axis=1, keepdims=True)
    grad_query = jnp.sum(own_row * passages, axis=0, keepdims=True)
    grad_passage = jnp.sum(own_col * queries, axis=0, keepdims=True)
    return entropy, (grad_query, grad_passage)


def norm_backward(upstream, normed, inverse, gain):
    scaled = upstream * gain
    centered = scaled - jnp.mean(scaled, axis=-1, keepdims=True)
    return inverse * (centered - normed * jnp.mean(scaled * normed, axis=-1, keepdims=True))


def loss_body(*refs):
    ids_ref, len_ref, pooled_ref = refs[:3]
    pieces, (spread_ref, loss_ref, emb_ref) = refs[3:-3], refs[-3:]
    place = 0
    for piece in pieces:
        for k in range(piece.shape[0]):
            emb_ref[ids_ref[1] ^ place] = piece[k]
            place += 1
    entropy, unit_grads = loss_grads(emb_ref[:, 0, :], emb_ref[:, 1, :], ids_ref[1])
    loss_ref[...] = jnp.broadcast_to(entropy, loss_ref.shape)
    for seg in range(2):
        summed = pooled_ref[seg : seg + 1, :]
        up = unit_grads[seg]
        inverse = lax.rsqrt(jnp.sum(summed * summed, axis=-1, keepdims=True) + 1e-06)
        cubed = inverse * inverse * inverse
        grad = inverse * up - cubed * summed * jnp.sum(summed * up, axis=-1, keepdims=True)
        spread_ref[seg : seg + 1, :] = grad / len_ref[ids_ref[2], 0, seg].astype(F32)


def ffn_back_body():
    def body(
        ids_ref, len_ref, spread_ref, cot_ref, normed_ref, inv_ref, slope_ref, vec_ref, fi_ref, fo_ref,
        second_ref, inner_ref, sums_ref, send_a, send_b, keep_ref, part_ref,
    ):
        micro = ids_ref[2]
        rows = normed_ref.shape[0]
        zero = jnp.zeros((1, normed_ref.shape[1]), F32)

        def step(k, sums):
            part = pl.ds(pl.multiple_of(k * QLEN, QLEN), QLEN)
            seg = jnp.minimum(k, 1)
            cot = cot_ref[micro, 0, part, :].astype(F32) + spread_ref[pl.ds(seg, 1), :]
            place = lax.broadcasted_iota(jnp.int32, cot.shape, 0) + (k - seg) * QLEN
            grad_final = jnp.where(place < len_ref[micro, 0, seg], cot, 0.0)
            normed = normed_ref[part, :].astype(F32)
            low = norm_backward(grad_final, normed, inv_ref[part, :], vec_ref[3:4, :]).astype(BF)
            second_ref[part, :] = low
            terms = (grad_final * normed, grad_final, low.astype(F32))
            return tuple(total + jnp.sum(term, axis=0, keepdims=True) for total, term in zip(sums, terms))

        gain_sum, shift_sum, bias_sum = lax.fori_loop(0, rows // QLEN, step, (zero, zero, zero))
        grad_hidden = mm(second_ref[...], fo_ref[...])
        grad_inner = (grad_hidden * slope_ref[...].astype(F32)).astype(BF)
        inner_ref[...] = grad_inner
        inner_sum = jnp.sum(grad_inner.astype(F32), axis=0, keepdims=True)
        part_ref[...] = mm(inner_ref[...], fi_ref[...], NT).astype(BF)
        split_halves(part_ref, ids_ref[0], send_a, send_b, keep_ref)
        sums_ref[...] = jnp.zeros(sums_ref.shape, F32)
        sums_ref[1:2, :] = bias_sum
        sums_ref[3:4, :] = gain_sum
        sums_ref[5:6, :] = shift_sum
        sums_ref[6:7, :] = inner_sum

    return body


def attend_back_body():
    def body(
        ids_ref, normed_ref, inv_ref, s0, s1, s2, s3, second_ref, qkv_ref, mixed_ref, pq_ref, pp_ref, vec_ref, w_ref,
        branch_ref, gqkv_ref, sums_ref, bias_ref, send_a, send_b, keep_ref, sum_ref, gm_ref, part_ref,
    ):
        rows = normed_ref.shape[0]
        heads = pq_ref.shape[0]
        width = heads * HEAD_DIM
        core = ids_ref[0]
        join_halves(sum_ref, core, (s0, s1, s2, s3))
        zero = jnp.zeros((1, normed_ref.shape[1]), F32)

        def step(k, sums):
            part = pl.ds(pl.multiple_of(k * QLEN, QLEN), QLEN)
            normed = normed_ref[part, :].astype(F32)
            upstream = sum_ref[part, :] + second_ref[part, :].astype(F32)
            low = norm_backward(upstream, normed, inv_ref[part, :], vec_ref[2:3, :]).astype(BF)
            branch_ref[part, :] = low
            terms = (upstream * normed, upstream, low.astype(F32))
            return tuple(total + jnp.sum(term, axis=0, keepdims=True) for total, term in zip(sums, terms))

        gain_sum, shift_sum, out_sum = lax.fori_loop(0, rows // QLEN, step, (zero, zero, zero))
        sums_ref[...] = jnp.zeros(sums_ref.shape, F32)
        sums_ref[0:1, :] = out_sum
        sums_ref[2:3, :] = gain_sum
        sums_ref[4:5, :] = shift_sum
        gm_ref[...] = mm(branch_ref[...], w_ref[:, 3 * width :]).astype(BF)
        factor = 1.0 / math.sqrt(HEAD_DIM)
        for seg, (low_row, high_row) in enumerate(segments(rows)):
            part = slice(low_row, high_row)
            p_ref = pp_ref if seg else pq_ref
            for h in range(heads):
                at = h * HEAD_DIM
                columns = [slice(j * width + at, j * width + at + HEAD_DIM) for j in range(3)]
                grad = gm_ref[part, columns[0]]
                weights = p_ref[h]
                grad_values = mm(weights, grad, TN)
                delta = jnp.sum(grad.astype(F32) * mixed_ref[part, columns[0]].astype(F32), axis=-1, keepdims=True)
                grad_weights = mm(grad, qkv_ref[part, columns[2]], NT)
                grad_scores = (weights.astype(F32) * (grad_weights - delta)).astype(BF)
                gqkv_ref[part, columns[0]] = (mm(grad_scores, qkv_ref[part, columns[1]]) * factor).astype(BF)
                gqkv_ref[part, columns[1]] = (mm(grad_scores, qkv_ref[part, columns[0]], TN) * factor).astype(BF)
                gqkv_ref[part, columns[2]] = grad_values.astype(BF)
        gqkv = gqkv_ref[...]
        bias_ref[...] = jnp.zeros(bias_ref.shape, F32)
        bias_ref[7:8, :] = jnp.sum(gqkv.astype(F32), axis=0, keepdims=True)
        part_ref[...] = mm(gqkv, w_ref[:, : 3 * width], NT).astype(BF)
        split_halves(part_ref, core, send_a, send_b, keep_ref)

    return body


def ffn_weight_body(block_rows, count):
    def body(ids_ref, low_a, low_b, gi_a, gi_b, hid_a, hid_b, gs_a, gs_b, *refs):
        outs, (fi_ref, fo_ref) = refs[:-2], refs[-2:]
        fi_ref[...] = mm(low_a[...], gi_a[...], TN) + mm(low_b[...], gi_b[...], TN)
        fo_ref[...] = mm(gs_a[...], hid_a[...], TN) + mm(gs_b[...], hid_b[...], TN)
        for k in range(count):
            at = pl.ds(pl.multiple_of(ring_owner(ids_ref[1], k, count) * block_rows, 16), block_rows)
            outs[k][:block_rows, :] = fi_ref[at, :].astype(BF)
            outs[k][block_rows:, :] = fo_ref[at, :].astype(BF)

    return body


def attend_weight_body(block_rows, head_bias, count):
    def body(
        ids_ref, x_ref, gq_a, gq_b, gb_a, gb_b, mx_a, mx_b, s4_a, s4_b, s5_a, s5_b, b_a, b_b, *refs
    ):
        outs, w_ref = refs[:-1], refs[-1]
        qkv = gq_a.shape[1]
        width = w_ref.shape[0]
        w_ref[:, :qkv] = mm(x_ref[0, 0], gq_a[...], TN) + mm(x_ref[1, 0], gq_b[...], TN)
        w_ref[:, qkv:] = mm(gb_a[...], mx_a[...], TN) + mm(gb_b[...], mx_b[...], TN)
        sums = (s4_a[...] + s4_b[...] + s5_a[...] + s5_b[...]).astype(BF)
        biases = (b_a[...] + b_b[...]).astype(BF)
        lane = lax.broadcasted_iota(jnp.int32, (128, width), 0)
        place = lax.broadcasted_iota(jnp.int32, (128, width), 1)
        for k in range(count):
            owner = ring_owner(ids_ref[1], k, count)
            outs[k][:block_rows, :] = w_ref[pl.ds(pl.multiple_of(owner * block_rows, 16), block_rows), :].astype(BF)
            outs[k][block_rows:, 128:] = jnp.zeros((EXTRA, width - 128), BF)
            pick = (place == owner * block_rows + lane) & (lane < block_rows)
            small = mm(sums, jnp.where(pick, 1.0, 0.0).astype(BF), NT)
            small += mm(biases, bias_pick(owner, head_bias, qkv, lane, place), NT)
            outs[k][block_rows:, :128] = small.astype(BF)

    return body


def unpack_attn_body(own_ref, up_ref, down_ref, ai_ref, ab_ref, ao_ref, ob_ref, fb_ref, ng_ref, ns_ref):
    block, head_width = ai_ref.shape[1], ai_ref.shape[2]
    head_bias = ab_ref.shape[1]
    total = own_ref[...].astype(F32) + up_ref[...].astype(F32) + down_ref[...].astype(F32)
    for j in range(3):
        ai_ref[j] = total[:block, j * head_width : (j + 1) * head_width]
    ao_ref[...] = total[:block, 3 * head_width :].T
    small = total[block : block + 8, :128]
    ob_ref[...] = small[0:2, :block]
    ng_ref[...] = small[2:4, :block]
    ns_ref[...] = small[4:6, :block]
    fb_ref[...] = small[6:7, :block]
    for j in range(2):
        ab_ref[j : j + 1, :] = small[7:8, j * head_bias : (j + 1) * head_bias]


def unpack_ffn_body(own_ref, up_ref, down_ref, fi_ref, fo_ref):
    block = fi_ref.shape[0]
    for part, out_ref in ((slice(0, block), fi_ref), (slice(block, 2 * block), fo_ref)):
        out_ref[...] = own_ref[part, :].astype(F32) + up_ref[part, :].astype(F32) + down_ref[part, :].astype(F32)


def finish_body(aliased):
    def body(ids_ref, gh_ref, s0, s1, s2, s3, *refs):
        out_ref, full_ref = refs[aliased:]
        join_halves(full_ref, ids_ref[0], (s0, s1, s2, s3))
        out_ref[0, 0] = full_ref[...] + gh_ref[...].astype(F32)

    return body


def core_swap(value, count):
    return lax.ppermute(value, "tp", [(i, i ^ 1) for i in range(count)])


def chip_swap(value, count):
    return lax.ppermute(value, "tp", [(i, i ^ 2) for i in range(count)])


def add_low(left, right):
    return (left.astype(F32) + right.astype(F32)).astype(BF)


def tp_start(parts, count):
    send_a, send_b, keep = parts
    got = [core_swap(send_a, count), core_swap(send_b, count)]
    near = kernel_call(half_body, "half", [VMEM] * 3, [shape(keep.shape, BF)], [keep, *got], 5e5, 2e6)[0]
    return near, chip_swap(near, count), core_swap(near, count)


def tp_finish(started, count, later):
    near, far, near_other = started
    return near, far, near_other, core_swap(after(far, later), count)


def pair_gather(value, count):
    pieces, step = [value], 1
    while step < count:
        send = pieces[0] if step == 1 else jnp.concatenate(pieces)
        pieces.append(lax.ppermute(send, "dp", [(i, i ^ step) for i in range(count)]))
        step *= 2
    return pieces


def after(ids, *values):
    return lax.optimization_barrier((ids, *values))[0]


def ring_order(count):
    return list(range(0, count, 2)) + list(range(count - 1, 0, -2))


def ring_step(value, order, step):
    count = len(order)
    return lax.ppermute(value, "dp", [(order[i], order[(i + step) % count]) for i in range(count)])


def ring_gather(block, order, up, after_up=None, after_down=None):
    count = len(order)
    ahead, behind = [], []
    from_behind = block if after_up is None else after(block, after_up)
    from_ahead = block if after_down is None else after(block, after_down)
    for step in range(up):
        from_behind = ring_step(from_behind, order, 1)
        behind.append(from_behind)
    for step in range(count - 1 - up):
        from_ahead = ring_step(from_ahead, order, -1)
        ahead.append(from_ahead)
    return [block] + ahead + behind[::-1], behind, ahead


def ring_scatter(blocks, order, up, before_last=None):
    count = len(order)
    ups, downs = [], []
    moving = blocks[up]
    for step in range(up):
        if step == up - 1 and before_last is not None:
            moving = after(moving, before_last)
        moving = ring_step(moving, order, 1)
        if step < up - 1:
            moving = add_low(moving, blocks[up - 1 - step])
        ups.append(moving)
    moving = blocks[up + 1]
    for step in range(count - 1 - up):
        moving = ring_step(moving, order, -1)
        if step < count - 2 - up:
            moving = add_low(moving, blocks[up + 2 + step])
        downs.append(moving)
    return [blocks[0], ups[-1], downs[-1]], ups, downs


def on_device(mesh_tp, mesh_dp, *arrays):
    tokens, out_grad, lengths, attn_in, attn_in_bias, attn_out, out_biases, ffn_in, ffn_in_bias, ffn_out, norm_gains, norm_shifts = arrays
    micro_count, _, rows, width = tokens.shape
    block = attn_in.shape[1]
    inner_width = ffn_in.shape[1]
    head_width = attn_in.shape[2]
    heads = head_width // HEAD_DIM
    qkv_width = 3 * head_width
    head_bias = attn_in_bias.shape[1]
    half = rows // 2
    ring = block % 16 == 0
    order = ring_order(mesh_dp)
    all_cols = qkv_width + head_width
    matmul = 2.0 * rows * width
    micros = range(micro_count)
    here = [lax.axis_index("tp") % 2, lax.axis_index("dp")]
    ids_of = [jnp.stack([*here, m]).astype(jnp.int32) for m in micros]
    ids = ids_of[0]

    vec_shape, bias_shape = shape((EXTRA, width), F32), shape((EXTRA, qkv_width), F32)
    full_weight = shape((width, inner_width), BF)
    if ring:
        raw = [attn_in, attn_in_bias, attn_out, out_biases, ffn_in, ffn_in_bias[None], ffn_out.T, norm_gains, norm_shifts]
        attn_block, ffn_block = kernel_call(
            pack_body,
            "pack",
            [pl.BlockSpec(memory_space=pltpu.HBM)] * 9,
            [shape((block + EXTRA, all_cols), BF), shape((2 * block, inner_width), BF)],
            raw,
            1e6,
            1e6,
            scratch=[pltpu.VMEM(arr.shape, arr.dtype) for arr in raw] + [pltpu.SemaphoreType.DMA((9,))],
        )
        more, less = mesh_dp // 2, mesh_dp - 1 - mesh_dp // 2
        blocks, ups, downs = ring_gather(attn_block, order, more)
        w_attn, vec, qkv_bias = kernel_call(
            assemble_body(block, head_bias, mesh_dp),
            "assemble",
            [SMEM] + [VMEM] * mesh_dp,
            [shape((width, all_cols), BF), vec_shape, bias_shape],
            [ids] + blocks,
            1e8,
            3e6,
        )
        ffn_blocks, ups, downs = ring_gather(ffn_block, order, less, ups[-1], downs[-1])
        arrivals = [downs[:1], [ups[0], downs[1]]] + [()] * (micro_count - 2)
        w_fi, w_fo = kernel_call(
            assemble_pair_body(block, mesh_dp),
            "assemble_ffn",
            [SMEM] + [VMEM] * mesh_dp,
            [full_weight, full_weight],
            [ids] + ffn_blocks,
            1e6,
            5e6,
        )
    else:
        attn_rows = jnp.concatenate([attn_in.transpose(1, 0, 2).reshape(block, qkv_width), attn_out.T], axis=1)
        last_row = jnp.pad(attn_in_bias.reshape(1, 2 * head_bias), ((0, 0), (0, block - 2 * head_bias)))
        vectors = jnp.concatenate([out_biases, norm_gains, norm_shifts, ffn_in_bias[None], last_row])
        w_attn = lax.all_gather(attn_rows, "dp", axis=0, tiled=True)
        every = lax.all_gather(vectors, "dp", axis=0).astype(F32)
        vec = jnp.pad(every.transpose(1, 0, 2).reshape(8, width), ((0, EXTRA - 8), (0, 0)))
        pair = every[:, 7, : 2 * head_bias].reshape(mesh_dp, 2, head_bias).transpose(1, 0, 2).reshape(2, head_width)
        both = jnp.concatenate([pair[0], jnp.zeros((head_width,), F32), pair[1]])
        qkv_bias = jnp.pad(both[None], ((7, EXTRA - 8), (0, 0)))
        arrivals = [()] * micro_count
        w_fi = lax.all_gather(ffn_in, "dp", axis=0, tiled=True)
        w_fo = lax.all_gather(ffn_out.T, "dp", axis=0, tiled=True)

    part_out = [shape((half // 2, width), BF)] * 2 + [shape((half, width), BF)]
    full_low = pltpu.VMEM((rows, width), BF)
    full_sum = pltpu.VMEM((rows, width), F32)

    attended, part = [], []
    done = []
    for m in micros:
        qkv, mixed, p_query, p_passage, *sends = kernel_call(
            attend_body(),
            "attend",
            [SMEM, SMEM, VMEM, VMEM, VMEM],
            [
                shape((rows, qkv_width), BF),
                shape((rows, head_width), BF),
                shape((heads, QLEN, QLEN), BF),
                shape((heads, rows - QLEN, rows - QLEN), BF),
            ]
            + part_out,
            [after(ids_of[m], *done, *arrivals[m]), lengths, tokens, w_attn, qkv_bias],
            matmul * all_cols * 4,
            6e6,
            scratch=[full_low],
        )
        attended.append((qkv, mixed, p_query, p_passage))
        part.append(tp_start(sends, mesh_tp))
        done = [part[m][0]]

    fed, before = [], attended[-1][0]
    for m in micros:
        branch = tp_finish(part[m], mesh_tp, before)
        normed, inverse, first, first_low, hidden, slope, *sends = kernel_call(
            ffn_body(half),
            "ffn",
            [SMEM] + [VMEM] * 8,
            [
                shape((rows, width), BF),
                shape((rows, 1), F32),
                shape((rows, width), F32),
                shape((rows, width), BF),
                shape((rows, inner_width), BF),
                shape((rows, inner_width), BF),
            ]
            + part_out,
            [after(ids_of[m], *done), tokens, *branch, vec, w_fi, w_fo],
            matmul * inner_width * 3,
            9e6,
            scratch=[full_sum, full_low],
        )
        before = first_low
        fed.append((first, first_low, hidden, slope, normed, inverse))
        part[m] = tp_start(sends, mesh_tp)
        done = [part[m][0]]

    out_tokens = None
    pooled = []
    for m in micros:
        second = tp_finish(part[m], mesh_tp, before)
        aliased = 0 if out_tokens is None else 1
        out_tokens, normed, inverse, sums, emb = kernel_call(
            pool_body(aliased),
            "pool",
            [SMEM, SMEM] + [VMEM] * 6 + [HBM] * aliased,
            [
                shape(tokens.shape, BF),
                shape((rows, width), BF),
                shape((rows, 1), F32),
                shape((8, width), F32),
                shape((1, 2, width), F32),
            ],
            [after(ids_of[m], *done), lengths, fed[m][0], *second, vec] + ([out_tokens] if aliased else []),
            2e8,
            6e6,
            scratch=[full_sum],
            out_specs=[micro_spec(tokens, m)] + [VMEM] * 4,
            aliases={8: 0} if aliased else None,
        )
        done = [sums]
        gathered = pair_gather(emb, mesh_dp)
        before = gathered[min(2, len(gathered) - 1)]
        pooled.append((normed, inverse, sums, gathered))

    back, entropies = [], []
    for m in micros:
        normed, inverse, sums, gathered = pooled[m]
        spread, entropy = kernel_call(
            loss_body,
            "loss",
            [SMEM, SMEM] + [VMEM] * (1 + len(gathered)),
            [shape((8, width), F32), shape((8, 128), F32)],
            [ids_of[m], lengths, sums, *gathered],
            1e6,
            1e5,
            scratch=[pltpu.VMEM((mesh_dp, 2, width), F32)],
        )
        grad_second, grad_inner, sums4, *sends = kernel_call(
            ffn_back_body(),
            "ffn_back",
            [SMEM, SMEM] + [VMEM] * 8,
            [
                shape((rows, width), BF),
                shape((rows, inner_width), BF),
                shape((EXTRA, width), F32),
            ]
            + part_out,
            [after(ids_of[m], *done), lengths, spread, out_grad, normed, inverse, fed[m][3], vec, w_fi, w_fo],
            matmul * inner_width * 3,
            10e6,
            scratch=[full_low],
        )
        before = grad_inner
        back.append((grad_second, grad_inner, sums4))
        entropies.append(entropy[0, 0])
        part[m] = tp_start(sends, mesh_tp)
        done = [part[m][0]]

    ring_steps = ()
    if ring:
        ffn_blocks = kernel_call(
            ffn_weight_body(block, mesh_dp),
            "ffn_weights",
            [SMEM] + [VMEM] * 8,
            [shape((2 * block, width), BF)] * mesh_dp,
            [after(ids, *done)] + [fed[m][1] for m in micros] + [back[m][1] for m in micros] + [fed[m][2] for m in micros] + [back[m][0] for m in micros],
            matmul * inner_width * 4,
            14e6,
            scratch=[pltpu.VMEM((width, inner_width), F32)] * 2,
        )
        done = [ffn_blocks[0]]
        before = ffn_blocks[0]
        pieces, ups, downs = ring_scatter(list(ffn_blocks), order, less)
        ring_steps = tuple(zip(ups, downs))
        grad_fi, grad_fo = kernel_call(
            unpack_ffn_body,
            "unpack_ffn",
            [VMEM] * 3,
            [shape(ffn_in.shape, F32)] * 2,
            pieces,
            1e6,
            2e6,
        )
        grad_fo = grad_fo.T
    else:
        grad_fi = sum(mm(fed[m][1], back[m][1], TN) for m in micros)
        grad_fo = sum(mm(back[m][0], fed[m][2], TN) for m in micros)
        grad_fi = lax.psum_scatter(grad_fi, "dp", scatter_dimension=0, tiled=True)
        grad_fo = lax.psum_scatter(grad_fo, "dp", scatter_dimension=0, tiled=True).T

    last = []
    for m in micros:
        grad_first = tp_finish(part[m], mesh_tp, before)
        qkv, mixed, p_query, p_passage = attended[m]
        grad_branch, grad_qkv, sums5, bias5, *sends = kernel_call(
            attend_back_body(),
            "attend_back",
            [SMEM] + [VMEM] * 13,
            [
                shape((rows, width), BF),
                shape((rows, qkv_width), BF),
                shape((EXTRA, width), F32),
                shape((EXTRA, qkv_width), F32),
            ]
            + part_out,
            [after(ids, *done), fed[m][4], fed[m][5], *grad_first, back[m][0], qkv, mixed, p_query, p_passage, vec, w_attn],
            matmul * all_cols * 6,
            12e6,
            scratch=[full_sum, pltpu.VMEM((rows, head_width), BF), full_low],
        )
        before = grad_qkv
        part[m] = tp_start(sends, mesh_tp)
        done = [part[m][0], *(ring_steps[m] if ring_steps else ())]
        last.append((grad_branch, grad_qkv, sums5, bias5))

    if ring:
        attn_blocks = kernel_call(
            attend_weight_body(block, head_bias, mesh_dp),
            "attend_weights",
            [SMEM] + [VMEM] * 13,
            [shape((block + EXTRA, all_cols), BF)] * mesh_dp,
            [after(ids, *done, *ring_steps[2]), tokens]
            + [last[m][1] for m in micros]
            + [last[m][0] for m in micros]
            + [attended[m][1] for m in micros]
            + [back[m][2] for m in micros]
            + [last[m][2] for m in micros]
            + [last[m][3] for m in micros],
            matmul * all_cols * 2,
            8e6,
            scratch=[pltpu.VMEM((width, all_cols), F32)],
        )
    else:
        grad_w = sum(
            jnp.concatenate([mm(tokens[m, 0], last[m][1], TN), mm(last[m][0], attended[m][1], TN)], axis=1) for m in micros
        )
        attn_blocks = [grad_w]
    in_grad = None
    for m in micros:
        aliased = 0 if in_grad is None else 1
        in_grad = kernel_call(
            finish_body(aliased),
            "finish",
            [SMEM] + [VMEM] * 5 + [HBM] * aliased,
            [shape(tokens.shape, F32)],
            [ids, last[m][0], *tp_finish(part[m], mesh_tp, attn_blocks[0])] + ([in_grad] if aliased else []),
            1e8,
            5e6,
            out_specs=[micro_spec(tokens, m)],
            aliases={6: 0} if aliased else None,
            scratch=[full_sum],
        )[0]

    if ring:
        pieces, _, _ = ring_scatter(list(attn_blocks), order, more, in_grad)
        grads = kernel_call(
            unpack_attn_body,
            "unpack_attn",
            [VMEM] * 3,
            [
                shape(attn_in.shape, F32),
                shape(attn_in_bias.shape, F32),
                shape(attn_out.shape, F32),
                shape(out_biases.shape, F32),
                shape((1, block), F32),
                shape(norm_gains.shape, F32),
                shape(norm_shifts.shape, F32),
            ],
            pieces,
            1e6,
            2e6,
        )
        grad_ai, grad_ab, grad_ao, grad_ob, grad_fb, grad_ng, grad_ns = grads
        grad_fb = grad_fb.reshape(block)
    else:
        attn_total = lax.psum_scatter(grad_w, "dp", scatter_dimension=0, tiled=True)
        sums = sum(back[m][2] + last[m][2] for m in micros)[:8].reshape(8, mesh_dp, block).transpose(1, 0, 2)
        bias = sum(last[m][3] for m in micros)[7].reshape(3, mesh_dp, head_bias)[0::2].transpose(1, 0, 2)
        bias = jnp.pad(bias.reshape(mesh_dp, 1, 2 * head_bias), ((0, 0), (7, 0), (0, block - 2 * head_bias)))
        small = lax.psum_scatter(sums + bias, "dp", scatter_dimension=0)
        grad_ai = attn_total[:, :qkv_width].reshape(block, 3, head_width).transpose(1, 0, 2)
        grad_ao = attn_total[:, qkv_width:].T
        grad_ab = small[7, : 2 * head_bias].reshape(2, head_bias)
        grad_ob, grad_ng, grad_ns, grad_fb = small[0:2], small[2:4], small[4:6], small[6]

    loss = sum(entropies) / (micro_count * mesh_dp)
    return out_tokens, in_grad, loss, grad_ai, grad_ab, grad_ao, grad_ob, grad_fi, grad_fb, grad_fo, grad_ng, grad_ns


def solution(mesh):
    placed = (
        P(None, "dp", None, None),
        P(None, "dp", None, None),
        P(None, "dp", None),
        P(None, "dp", "tp"),
        P(None, ("tp", "dp")),
        P("tp", "dp"),
        P(None, "dp"),
        P("dp", "tp"),
        P(("tp", "dp")),
        P("tp", "dp"),
        P(None, "dp"),
        P(None, "dp"),
    )
    sizes = (mesh.shape["tp"], mesh.shape["dp"])

    def run(*arrays):
        return on_device(*sizes, *arrays)

    return jax.shard_map(
        run,
        mesh=mesh,
        in_specs=placed,
        out_specs=placed[:2] + (P(),) + placed[3:],
        check_vma=False,
    )
```

```python
import math

import jax
import jax.numpy as jnp
from jax import lax
from jax.experimental import pallas as pl
from jax.experimental.pallas import tpu as pltpu
from jax.sharding import PartitionSpec as P

HEAD_DIM = 64
QLEN = 128
SOFTMAX_TEMP = 0.01
NEG_LARGE = -1e30
ROOT_HALF = 0.7071067811865476
DENSITY_NORM = 0.3989422804014327
VMEM_BYTES = 20 * 2**20
EXTRA = 16
BF = jnp.bfloat16
F32 = jnp.float32
NN = (((1,), (0,)), ((), ()))
NT = (((1,), (1,)), ((), ()))
TN = (((0,), (0,)), ((), ()))
HBM = pl.BlockSpec(memory_space=pl.ANY)
SMEM = pl.BlockSpec(memory_space=pltpu.SMEM)
VMEM = pl.BlockSpec(memory_space=pltpu.VMEM)


def mm(left, right, dims=NN, precision=None):
    return lax.dot_general(left, right, dims, precision=precision, preferred_element_type=F32)


def shape(dims, dtype):
    return jax.ShapeDtypeStruct(dims, dtype)


def kernel_call(body, name, in_specs, outs, args, flops, moved, scratch=(), out_specs=None, aliases=None):
    return pl.pallas_call(
        body,
        name=name,
        grid=(1,) if out_specs is not None else (),
        in_specs=in_specs,
        out_specs=out_specs if out_specs is not None else [VMEM] * len(outs),
        out_shape=outs,
        scratch_shapes=scratch,
        input_output_aliases=aliases or {},
        compiler_params=pltpu.CompilerParams(vmem_limit_bytes=VMEM_BYTES),
        cost_estimate=pl.CostEstimate(flops=int(flops), bytes_accessed=int(moved), transcendentals=0),
    )(*args)


def micro_spec(arr, micro):
    return pl.BlockSpec((1,) + arr.shape[1:], lambda i: (micro,) + (0,) * (len(arr.shape) - 1))


def ring_owner(at, step, count):
    half = count // 2
    place = jnp.where(at % 2 == 0, at // 2, half + (count - 1 - at) // 2)
    place = (place + step) % count
    return jnp.where(place < half, 2 * place, count - 1 - 2 * (place - half))


def pack_attn_body(ai_ref, ao_ref, small_ref, out_ref):
    block, head_width = ai_ref.shape[1], ai_ref.shape[2]
    for j in range(3):
        out_ref[:block, j * head_width : (j + 1) * head_width] = ai_ref[j]
    out_ref[:block, 3 * head_width :] = ao_ref[...].T
    out_ref[block:, :] = jnp.zeros((out_ref.shape[0] - block, out_ref.shape[1]), BF)
    out_ref[block:, :block] = small_ref[...]


def pack_ffn_body(fi_ref, fo_ref, tokens_ref, out_ref):
    block = fi_ref.shape[0]
    out_ref[:block, :] = fi_ref[...]
    out_ref[block:, :] = fo_ref[...]


def assemble_body(block_rows, head_bias, count, steps, first):
    def body(ids_ref, *refs):
        blocks, (w_ref, vec_ref, bias_ref) = refs[: len(steps)], refs[-3:]
        width = w_ref.shape[1]
        qkv_width = bias_ref.shape[1]
        vectors, biases = jnp.zeros(vec_ref.shape, F32), jnp.zeros(bias_ref.shape, F32)
        if not first:
            vectors, biases = refs[-5][...], refs[-4][...]
        lane = lax.broadcasted_iota(jnp.int32, (128, width), 0)
        place = lax.broadcasted_iota(jnp.int32, (128, width), 1)
        for block, k in zip(blocks, steps):
            owner = ring_owner(ids_ref[1], k, count)
            w_ref[pl.ds(pl.multiple_of(owner * block_rows, 16), block_rows), :] = block[:block_rows, :]
            small = block[block_rows : block_rows + EXTRA, :128]
            pick = (place == owner * block_rows + lane) & (lane < block_rows)
            vectors += mm(small, jnp.where(pick, 1.0, 0.0).astype(BF))
            biases += mm(small, bias_pick(owner, head_bias, qkv_width, lane, place))
        vec_ref[...] = vectors
        bias_ref[...] = biases

    return body


def assemble_pair_body(block_rows, count):
    def body(ids_ref, *refs):
        blocks, (fi_ref, fo_ref) = refs[:count], refs[count:]
        for k in range(count):
            owner = ring_owner(ids_ref[1], k, count)
            at = pl.ds(pl.multiple_of(owner * block_rows, 16), block_rows)
            fi_ref[at, :] = blocks[k][:block_rows, :]
            fo_ref[at, :] = blocks[k][block_rows:, :]

    return body


def bias_pick(owner, head_bias, qkv_width, lane, place):
    lane, place = lane[:, :qkv_width], place[:, :qkv_width]
    values_at = qkv_width * 2 // 3
    for_query = (lane < head_bias) & (place == owner * head_bias + lane)
    for_value = (
        (lane >= head_bias)
        & (lane < 2 * head_bias)
        & (place == values_at + owner * head_bias + lane - head_bias)
    )
    return jnp.where(for_query | for_value, 1.0, 0.0).astype(BF)


def split_halves(full_ref, core, send_a, send_b, keep_ref):
    half, piece = keep_ref.shape[0], send_a.shape[0]
    keep_ref[...] = full_ref[pl.ds(pl.multiple_of(core * half, 16), half), :]
    for k, ref in enumerate((send_a, send_b)):
        ref[...] = full_ref[pl.ds(pl.multiple_of((1 - core) * half + k * piece, 16), piece), :]


def halves(core, half):
    return [pl.ds(pl.multiple_of(place * half, 16), half) for place in (1 - core, core)]


def send_halves(make, core, send_a, send_b, keep_ref):
    half, piece = keep_ref.shape[0], send_a.shape[0]
    away, here = halves(core, half)
    value = make(away).astype(BF)
    send_a[...] = value[:piece]
    send_b[...] = value[piece:]
    keep_ref[...] = make(here).astype(BF)


def half_body(keep_ref, a_ref, b_ref, out_ref):
    piece = a_ref.shape[0]
    for k, ref in enumerate((a_ref, b_ref)):
        part = slice(k * piece, (k + 1) * piece)
        out_ref[part, :] = add_low(keep_ref[part, :], ref[...])


def join_halves(full_ref, core, parts):
    half = parts[0].shape[0]
    for near, far, place in ((parts[0], parts[1], core), (parts[2], parts[3], 1 - core)):
        full_ref[pl.ds(pl.multiple_of(place * half, 16), half), :] = near[...].astype(F32) + far[...].astype(F32)


def over_sum(core, parts, step):
    half = parts[0].shape[0]
    piece = half // 2
    for near, far, place in ((parts[0], parts[1], core), (parts[2], parts[3], 1 - core)):

        def one(k, carry, near=near, far=far, place=place):
            at = pl.ds(pl.multiple_of(k * piece, 16), piece)
            start = pl.multiple_of(place * half + k * piece, 16)
            step(pl.ds(start, piece), start, near[at, :].astype(F32) + far[at, :].astype(F32))
            return carry

        lax.fori_loop(0, 2, one, 0)


def segment_masks(start, dims, lengths):
    row = lax.broadcasted_iota(jnp.int32, dims, 0) + start
    return row < QLEN, (row < QLEN) & (row < lengths[0]), (row >= QLEN) & (row - QLEN < lengths[1])


def segments(rows):
    return ((0, QLEN), (QLEN, rows))


def attend_body():
    def body(ids_ref, len_ref, x_ref, w_ref, bias_ref, qkv_ref, mixed_ref, pq_ref, pp_ref, send_a, send_b, keep_ref, part_ref):
        micro = ids_ref[2]
        rows = x_ref.shape[2]
        heads = pq_ref.shape[0]
        width = heads * HEAD_DIM
        x = x_ref[micro, 0]
        bias = bias_ref[7:8, :]
        qkv_ref[...] = (mm(x, w_ref[:, : 3 * width]) + bias).astype(BF)
        factor = 1.0 / math.sqrt(HEAD_DIM)
        for seg, (low, high) in enumerate(segments(rows)):
            length = len_ref[micro, 0, seg]
            size = high - low
            p_ref = pp_ref if seg else pq_ref
            visible = lax.broadcasted_iota(jnp.int32, (size, size), 0) < length
            for h in range(heads):
                at = h * HEAD_DIM
                queries = qkv_ref[low:high, at : at + HEAD_DIM]
                keys_low = qkv_ref[low:high, width + at : width + at + HEAD_DIM]
                values = qkv_ref[low:high, 2 * width + at : 2 * width + at + HEAD_DIM]
                scores = jnp.where(visible, mm(keys_low, queries, NT) * factor, NEG_LARGE)
                raised = jnp.exp(scores - jnp.max(scores, axis=0, keepdims=True))
                weights = (raised * (1.0 / jnp.sum(raised, axis=0, keepdims=True))).astype(BF)
                p_ref[h] = weights
                mixed_ref[low:high, at : at + HEAD_DIM] = mm(values, weights, TN).T.astype(BF)
        part_ref[...] = mm(mixed_ref[...], w_ref[:, 3 * width :], NT).astype(BF)
        split_halves(part_ref, ids_ref[0], send_a, send_b, keep_ref)

    return body


def norm_one(x, branch, shift_out):
    hidden = x.astype(F32) + (branch.astype(F32) + shift_out)
    center = hidden - jnp.mean(hidden, axis=-1, keepdims=True)
    inverse = lax.rsqrt(jnp.mean(center * center, axis=-1, keepdims=True) + 1e-12)
    return center * inverse, inverse


def ffn_body():
    def body(
        ids_ref, x_ref, s0, s1, s2, s3, vec_ref, fi_ref, fo_ref,
        normed_ref, inv_ref, first_ref, low_ref, hidden_ref, slope_ref, send_a, send_b, keep_ref,
    ):
        micro, core = ids_ref[2], ids_ref[0]
        half, piece = keep_ref.shape[0], send_a.shape[0]
        for part, near, far, away in zip(halves(core, half), (s2, s0), (s3, s1), (True, False)):
            branch = near[...].astype(F32) + far[...].astype(F32)
            normed, inverse = norm_one(x_ref[micro, 0, part, :], branch, vec_ref[0:1, :])
            normed_ref[part, :] = normed.astype(BF)
            inv_ref[part, :] = inverse
            first = normed * vec_ref[2:3, :] + vec_ref[4:5, :]
            first_ref[part, :] = first
            low = first.astype(BF)
            low_ref[part, :] = low
            inner = mm(low, fi_ref[...]) + vec_ref[6:7, :]
            cumulative = 0.5 * (1.0 + lax.erf(inner * ROOT_HALF))
            density = jnp.exp(-0.5 * inner * inner) * DENSITY_NORM
            hidden = (inner * cumulative).astype(BF)
            hidden_ref[part, :] = hidden
            slope_ref[part, :] = (cumulative + inner * density).astype(BF)
            second = mm(hidden, fo_ref[...], NT).astype(BF)
            if away:
                send_a[...] = second[:piece]
                send_b[...] = second[piece:]
            else:
                keep_ref[...] = second

    return body


def pool_body():
    def body(
        ids_ref, len_ref, first_ref, s0, s1, s2, s3, vec_ref, out_ref, normed_ref, inv_ref, pooled_ref, emb_ref
    ):
        micro = ids_ref[2]
        pooled_ref[...] = jnp.zeros(pooled_ref.shape, F32)
        lengths = [len_ref[micro, 0, seg] for seg in range(2)]

        def step(part, start, second):
            hidden = first_ref[part, :] + (second + vec_ref[1:2, :])
            center = hidden - jnp.mean(hidden, axis=-1, keepdims=True)
            inverse = lax.rsqrt(jnp.mean(center * center, axis=-1, keepdims=True) + 1e-12)
            normed = center * inverse
            normed_ref[part, :] = normed.astype(BF)
            inv_ref[part, :] = inverse
            final = normed * vec_ref[3:4, :] + vec_ref[5:6, :]
            out_ref[part, :] = final.astype(BF)
            masks = segment_masks(start, (final.shape[0], 1), lengths)
            for seg in range(2):
                kept = jnp.where(masks[seg + 1], final, 0.0)
                pooled_ref[seg : seg + 1, :] += jnp.sum(kept, axis=0, keepdims=True)

        over_sum(ids_ref[0], (s0, s1, s2, s3), step)
        for seg in range(2):
            summed = pooled_ref[seg : seg + 1, :] / len_ref[micro, 0, seg].astype(F32)
            unit = summed * lax.rsqrt(jnp.sum(summed * summed, axis=-1, keepdims=True) + 1e-06)
            pooled_ref[seg : seg + 1, :] = summed
            emb_ref[0, seg : seg + 1, :] = unit

    return body


def loss_grads(queries, passages, own):
    highest = lax.Precision.HIGHEST
    count = queries.shape[0]
    row = lax.broadcasted_iota(jnp.int32, (count, count), 0)
    col = lax.broadcasted_iota(jnp.int32, (count, count), 1)
    same = jnp.where(row == col, 1.0, 0.0)
    logits = mm(queries, passages, NT, highest) / SOFTMAX_TEMP
    top = jnp.max(logits, axis=-1, keepdims=True)
    log_norm = top + jnp.log(jnp.sum(jnp.exp(logits - top), axis=-1, keepdims=True))
    entropy = jnp.sum(jnp.sum(same * (log_norm - logits), axis=-1, keepdims=True), axis=0, keepdims=True)
    grad = (jnp.exp(logits - log_norm) - same) / SOFTMAX_TEMP
    turned = mm(passages, queries, NT, highest) / SOFTMAX_TEMP
    top_t = jnp.max(turned, axis=0, keepdims=True)
    norm_t = top_t + jnp.log(jnp.sum(jnp.exp(turned - top_t), axis=0, keepdims=True))
    grad_t = (jnp.exp(turned - norm_t) - same) / SOFTMAX_TEMP
    own_col = jnp.sum(jnp.where(col == own, grad, 0.0), axis=1, keepdims=True)
    own_row = jnp.sum(jnp.where(col == own, grad_t, 0.0), axis=1, keepdims=True)
    grad_query = jnp.sum(own_row * passages, axis=0, keepdims=True)
    grad_passage = jnp.sum(own_col * queries, axis=0, keepdims=True)
    return entropy, (grad_query, grad_passage)


def norm_backward(upstream, normed, inverse, gain):
    scaled = upstream * gain
    centered = scaled - jnp.mean(scaled, axis=-1, keepdims=True)
    return inverse * (centered - normed * jnp.mean(scaled * normed, axis=-1, keepdims=True))


def loss_body(*refs):
    ids_ref, len_ref, pooled_ref = refs[:3]
    pieces, (spread_ref, loss_ref, emb_ref) = refs[3:-3], refs[-3:]
    place = 0
    for piece in pieces:
        for k in range(piece.shape[0]):
            emb_ref[ids_ref[1] ^ place] = piece[k]
            place += 1
    entropy, unit_grads = loss_grads(emb_ref[:, 0, :], emb_ref[:, 1, :], ids_ref[1])
    loss_ref[...] = jnp.broadcast_to(entropy, loss_ref.shape)
    for seg in range(2):
        summed = pooled_ref[seg : seg + 1, :]
        up = unit_grads[seg]
        inverse = lax.rsqrt(jnp.sum(summed * summed, axis=-1, keepdims=True) + 1e-06)
        cubed = inverse * inverse * inverse
        grad = inverse * up - cubed * summed * jnp.sum(summed * up, axis=-1, keepdims=True)
        spread_ref[seg : seg + 1, :] = grad / len_ref[ids_ref[2], 0, seg].astype(F32)


def ffn_back_body():
    def body(
        ids_ref, len_ref, spread_ref, cot_ref, normed_ref, inv_ref, slope_ref, vec_ref, fi_ref, fo_ref,
        second_ref, inner_ref, sums_ref, send_a, send_b, keep_ref, part_ref,
    ):
        micro = ids_ref[2]
        rows = normed_ref.shape[0]
        zero = jnp.zeros((1, normed_ref.shape[1]), F32)

        def step(k, sums):
            part = pl.ds(pl.multiple_of(k * QLEN, QLEN), QLEN)
            seg = jnp.minimum(k, 1)
            cot = cot_ref[micro, 0, part, :].astype(F32) + spread_ref[pl.ds(seg, 1), :]
            place = lax.broadcasted_iota(jnp.int32, cot.shape, 0) + (k - seg) * QLEN
            grad_final = jnp.where(place < len_ref[micro, 0, seg], cot, 0.0)
            normed = normed_ref[part, :].astype(F32)
            low = norm_backward(grad_final, normed, inv_ref[part, :], vec_ref[3:4, :]).astype(BF)
            second_ref[part, :] = low
            terms = (grad_final * normed, grad_final, low.astype(F32))
            return tuple(total + jnp.sum(term, axis=0, keepdims=True) for total, term in zip(sums, terms))

        gain_sum, shift_sum, bias_sum = lax.fori_loop(0, rows // QLEN, step, (zero, zero, zero))
        grad_hidden = mm(second_ref[...], fo_ref[...])
        grad_inner = (grad_hidden * slope_ref[...].astype(F32)).astype(BF)
        inner_ref[...] = grad_inner
        inner_sum = jnp.sum(grad_inner.astype(F32), axis=0, keepdims=True)
        part_ref[...] = mm(inner_ref[...], fi_ref[...], NT).astype(BF)
        split_halves(part_ref, ids_ref[0], send_a, send_b, keep_ref)
        sums_ref[...] = jnp.zeros(sums_ref.shape, F32)
        sums_ref[1:2, :] = bias_sum
        sums_ref[3:4, :] = gain_sum
        sums_ref[5:6, :] = shift_sum
        sums_ref[6:7, :] = inner_sum

    return body


def attend_back_body():
    def body(
        ids_ref, normed_ref, inv_ref, s0, s1, s2, s3, second_ref, qkv_ref, mixed_ref, pq_ref, pp_ref, vec_ref, w_ref,
        branch_ref, gqkv_ref, sums_ref, bias_ref, send_a, send_b, keep_ref, sum_ref, gm_ref, part_ref,
    ):
        rows = normed_ref.shape[0]
        heads = pq_ref.shape[0]
        width = heads * HEAD_DIM
        core = ids_ref[0]
        join_halves(sum_ref, core, (s0, s1, s2, s3))
        zero = jnp.zeros((1, normed_ref.shape[1]), F32)

        def step(k, sums):
            part = pl.ds(pl.multiple_of(k * QLEN, QLEN), QLEN)
            normed = normed_ref[part, :].astype(F32)
            upstream = sum_ref[part, :] + second_ref[part, :].astype(F32)
            low = norm_backward(upstream, normed, inv_ref[part, :], vec_ref[2:3, :]).astype(BF)
            branch_ref[part, :] = low
            terms = (upstream * normed, upstream, low.astype(F32))
            return tuple(total + jnp.sum(term, axis=0, keepdims=True) for total, term in zip(sums, terms))

        gain_sum, shift_sum, out_sum = lax.fori_loop(0, rows // QLEN, step, (zero, zero, zero))
        sums_ref[...] = jnp.zeros(sums_ref.shape, F32)
        sums_ref[0:1, :] = out_sum
        sums_ref[2:3, :] = gain_sum
        sums_ref[4:5, :] = shift_sum
        gm_ref[...] = mm(branch_ref[...], w_ref[:, 3 * width :]).astype(BF)
        factor = 1.0 / math.sqrt(HEAD_DIM)
        for seg, (low_row, high_row) in enumerate(segments(rows)):
            part = slice(low_row, high_row)
            p_ref = pp_ref if seg else pq_ref
            for h in range(heads):
                at = h * HEAD_DIM
                columns = [slice(j * width + at, j * width + at + HEAD_DIM) for j in range(3)]
                grad = gm_ref[part, columns[0]]
                weights = p_ref[h]
                grad_weights = mm(qkv_ref[part, columns[2]], grad, NT)
                low_weights = weights.astype(F32)
                delta = jnp.sum(low_weights * grad_weights, axis=0, keepdims=True)
                grad_scores = (low_weights * (grad_weights - delta)).astype(BF)
                gqkv_ref[part, columns[0]] = (mm(qkv_ref[part, columns[1]], grad_scores, TN) * factor).T.astype(BF)
                gqkv_ref[part, columns[1]] = (mm(grad_scores, qkv_ref[part, columns[0]]) * factor).astype(BF)
                gqkv_ref[part, columns[2]] = mm(weights, grad).astype(BF)
        gqkv = gqkv_ref[...]
        bias_ref[...] = jnp.zeros(bias_ref.shape, F32)
        bias_ref[7:8, :] = jnp.sum(gqkv.astype(F32), axis=0, keepdims=True)
        part_ref[...] = mm(gqkv, w_ref[:, : 3 * width], NT).astype(BF)
        split_halves(part_ref, core, send_a, send_b, keep_ref)

    return body


def ffn_weight_body(block_rows, count):
    def body(ids_ref, low_a, low_b, gi_a, gi_b, hid_a, hid_b, gs_a, gs_b, *refs):
        outs, (fi_ref, fo_ref) = refs[:-2], refs[-2:]
        fi_ref[...] = mm(low_a[...], gi_a[...], TN) + mm(low_b[...], gi_b[...], TN)
        fo_ref[...] = mm(gs_a[...], hid_a[...], TN) + mm(gs_b[...], hid_b[...], TN)
        for k in range(count):
            at = pl.ds(pl.multiple_of(ring_owner(ids_ref[1], k, count) * block_rows, 16), block_rows)
            outs[k][:block_rows, :] = fi_ref[at, :].astype(BF)
            outs[k][block_rows:, :] = fo_ref[at, :].astype(BF)

    return body


def attend_weight_body(block_rows, head_bias, count):
    def body(
        ids_ref, x_ref, gq_a, gq_b, gb_a, gb_b, mx_a, mx_b, s4_a, s4_b, s5_a, s5_b, b_a, b_b, *refs
    ):
        outs, w_ref = refs[:-1], refs[-1]
        qkv = gq_a.shape[1]
        width = w_ref.shape[0]
        w_ref[:, :qkv] = mm(x_ref[0, 0], gq_a[...], TN) + mm(x_ref[1, 0], gq_b[...], TN)
        w_ref[:, qkv:] = mm(gb_a[...], mx_a[...], TN) + mm(gb_b[...], mx_b[...], TN)
        sums = (s4_a[...] + s4_b[...] + s5_a[...] + s5_b[...]).astype(BF)
        biases = (b_a[...] + b_b[...]).astype(BF)
        lane = lax.broadcasted_iota(jnp.int32, (128, width), 0)
        place = lax.broadcasted_iota(jnp.int32, (128, width), 1)
        for k in range(count):
            owner = ring_owner(ids_ref[1], k, count)
            outs[k][:block_rows, :] = w_ref[pl.ds(pl.multiple_of(owner * block_rows, 16), block_rows), :].astype(BF)
            outs[k][block_rows:, 128:] = jnp.zeros((EXTRA, width - 128), BF)
            pick = (place == owner * block_rows + lane) & (lane < block_rows)
            small = mm(sums, jnp.where(pick, 1.0, 0.0).astype(BF), NT)
            small += mm(biases, bias_pick(owner, head_bias, qkv, lane, place), NT)
            outs[k][block_rows:, :128] = small.astype(BF)

    return body


def unpack_attn_body(own_ref, up_ref, down_ref, ai_ref, ab_ref, ao_ref, ob_ref, fb_ref, ng_ref, ns_ref):
    block, head_width = ai_ref.shape[1], ai_ref.shape[2]
    head_bias = ab_ref.shape[1]
    total = own_ref[...].astype(F32) + up_ref[...].astype(F32) + down_ref[...].astype(F32)
    for j in range(3):
        ai_ref[j] = total[:block, j * head_width : (j + 1) * head_width]
    ao_ref[...] = total[:block, 3 * head_width :].T
    small = total[block : block + 8, :128]
    ob_ref[...] = small[0:2, :block]
    ng_ref[...] = small[2:4, :block]
    ns_ref[...] = small[4:6, :block]
    fb_ref[...] = small[6:7, :block]
    for j in range(2):
        ab_ref[j : j + 1, :] = small[7:8, j * head_bias : (j + 1) * head_bias]


def unpack_ffn_body(own_ref, up_ref, down_ref, fi_ref, fo_ref):
    block = fi_ref.shape[0]
    for part, out_ref in ((slice(0, block), fi_ref), (slice(block, 2 * block), fo_ref)):
        out_ref[...] = own_ref[part, :].astype(F32) + up_ref[part, :].astype(F32) + down_ref[part, :].astype(F32)


def finish_body(aliased):
    def body(ids_ref, final_ref, gh_ref, s0, s1, s2, s3, *refs):
        tokens_ref, out_ref, full_ref = refs[aliased:]
        tokens_ref[0, 0] = final_ref[...]
        join_halves(full_ref, ids_ref[0], (s0, s1, s2, s3))
        out_ref[0, 0] = full_ref[...] + gh_ref[...].astype(F32)

    return body


def core_swap(value, count):
    return lax.ppermute(value, "tp", [(i, i ^ 1) for i in range(count)])


def chip_swap(value, count):
    return lax.ppermute(value, "tp", [(i, i ^ 2) for i in range(count)])


def add_low(left, right):
    return (left.astype(F32) + right.astype(F32)).astype(BF)


def tp_start(parts, count, ready=()):
    send_a, send_b, keep = parts
    send_a = after(send_a, *ready)
    got = [core_swap(send_a, count), core_swap(send_b, count)]
    near = kernel_call(half_body, "half", [VMEM] * 3, [shape(keep.shape, BF)], [keep, *got], 5e5, 2e6)[0]
    return near, chip_swap(near, count), core_swap(near, count)


def tp_finish(started, count, *later):
    near, far, near_other = started
    return near, far, near_other, core_swap(after(far, *later), count)


def pair_gather(value, count):
    pieces, step = [value], 1
    while step < count:
        send = pieces[0] if step == 1 else jnp.concatenate(pieces)
        pieces.append(lax.ppermute(send, "dp", [(i, i ^ step) for i in range(count)]))
        step *= 2
    return pieces


def after(ids, *values):
    return lax.optimization_barrier((ids, *values))[0]


def ring_order(count):
    return list(range(0, count, 2)) + list(range(count - 1, 0, -2))


def ring_step(value, order, step):
    count = len(order)
    return lax.ppermute(value, "dp", [(order[i], order[(i + step) % count]) for i in range(count)])


def ring_gather(block, order, up, after_up=None, after_down=None):
    count = len(order)
    ahead, behind = [], []
    from_behind = block if after_up is None else after(block, after_up)
    from_ahead = block if after_down is None else after(block, after_down)
    for step in range(up):
        from_behind = ring_step(from_behind, order, 1)
        behind.append(from_behind)
    for step in range(count - 1 - up):
        from_ahead = ring_step(from_ahead, order, -1)
        ahead.append(from_ahead)
    return [block] + ahead + behind[::-1], behind, ahead


class RingSum:
    def __init__(self, parts, order, way):
        self.parts, self.order, self.way = parts, order, way
        self.moving, self.at = parts[0], 1

    def send(self, *ready):
        self.moving = ring_step(after(self.moving, *ready), self.order, self.way)

    def absorb(self, *ready):
        self.moving = after(self.moving, *ready)
        if self.at < len(self.parts):
            self.moving = add_low(self.moving, self.parts[self.at])
        self.at += 1
        return self.moving


def ring_sums(blocks, order, up):
    return RingSum(blocks[up:0:-1], order, 1), RingSum(blocks[up + 1 :], order, -1)


def on_device(mesh_tp, mesh_dp, *arrays):
    tokens, out_grad, lengths, attn_in, attn_in_bias, attn_out, out_biases, ffn_in, ffn_in_bias, ffn_out, norm_gains, norm_shifts = arrays
    micro_count, _, rows, width = tokens.shape
    block = attn_in.shape[1]
    inner_width = ffn_in.shape[1]
    head_width = attn_in.shape[2]
    heads = head_width // HEAD_DIM
    qkv_width = 3 * head_width
    head_bias = attn_in_bias.shape[1]
    half = rows // 2
    ring = block % 16 == 0
    order = ring_order(mesh_dp)
    all_cols = qkv_width + head_width
    matmul = 2.0 * rows * width
    micros = range(micro_count)
    here = [lax.axis_index("tp") % 2, lax.axis_index("dp")]
    ids_of = [jnp.stack([*here, m]).astype(jnp.int32) for m in micros]
    ids = ids_of[0]

    vec_shape, bias_shape = shape((EXTRA, width), F32), shape((EXTRA, qkv_width), F32)
    full_weight = shape((width, inner_width), BF)
    last_row = jnp.pad(attn_in_bias.reshape(1, 2 * head_bias), ((0, 0), (0, block - 2 * head_bias)))
    if ring:
        small = jnp.concatenate(
            [out_biases, norm_gains, norm_shifts, ffn_in_bias[None], last_row, jnp.zeros((EXTRA - 8, block), BF)]
        )
        attn_block = kernel_call(
            pack_attn_body, "pack_attn", [VMEM] * 3, [shape((block + EXTRA, all_cols), BF)], [attn_in, attn_out, small], 1e6, 1e6
        )[0]
        ffn_block = kernel_call(
            pack_ffn_body,
            "pack_ffn",
            [VMEM] * 3,
            [shape((2 * block, inner_width), BF)],
            [ffn_in, ffn_out.T, after(tokens, attn_block)],
            1e6,
            1e6,
        )[0]
        more, less = mesh_dp // 2, mesh_dp - 1 - mesh_dp // 2

        def assemble(blocks, steps, held=()):
            return kernel_call(
                assemble_body(block, head_bias, mesh_dp, steps, not held),
                "assemble",
                [SMEM] + [VMEM] * (len(blocks) + len(held)),
                [shape((width, all_cols), BF), vec_shape, bias_shape],
                [ids, *blocks, *held],
                1e8,
                3e6,
                aliases={1 + len(blocks): 0} if held else None,
            )

        ups, downs = [attn_block], [attn_block]
        weights = ()
        for step in range(more):
            if step == more - 1:
                steps = [0, *range(1, less), *range(mesh_dp - less + 1, mesh_dp)]
                weights = assemble([attn_block, *downs[1:less], *ups[less - 1 : 0 : -1]], steps)
                ups[-1] = after(ups[-1], weights[1])
            ups.append(ring_step(ups[-1], order, 1))
            if step < less:
                downs.append(ring_step(downs[-1], order, -1))
        w_attn, vec, qkv_bias = assemble([downs[less], *ups[: less - 1 : -1]], [less, *range(less + 1, mesh_dp - less + 1)], weights)
        ffn_ups, ffn_downs = [after(ffn_block, ups[-1])], [after(ffn_block, downs[-1])]
        ffn_downs.append(ring_step(ffn_downs[-1], order, -1))
        ffn_downs.append(ring_step(ffn_downs[-1], order, -1))
        ffn_ups.append(ring_step(ffn_ups[-1], order, 1))
    else:
        attn_rows = jnp.concatenate([attn_in.transpose(1, 0, 2).reshape(block, qkv_width), attn_out.T], axis=1)
        vectors = jnp.concatenate([out_biases, norm_gains, norm_shifts, ffn_in_bias[None], last_row])
        w_attn = lax.all_gather(attn_rows, "dp", axis=0, tiled=True)
        every = lax.all_gather(vectors, "dp", axis=0).astype(F32)
        vec = jnp.pad(every.transpose(1, 0, 2).reshape(8, width), ((0, EXTRA - 8), (0, 0)))
        pair = every[:, 7, : 2 * head_bias].reshape(mesh_dp, 2, head_bias).transpose(1, 0, 2).reshape(2, head_width)
        both = jnp.concatenate([pair[0], jnp.zeros((head_width,), F32), pair[1]])
        qkv_bias = jnp.pad(both[None], ((7, EXTRA - 8), (0, 0)))
        w_fi = lax.all_gather(ffn_in, "dp", axis=0, tiled=True)
        w_fo = lax.all_gather(ffn_out.T, "dp", axis=0, tiled=True)

    part_out = [shape((half // 2, width), BF)] * 2 + [shape((half, width), BF)]
    full_low = pltpu.VMEM((rows, width), BF)
    full_sum = pltpu.VMEM((rows, width), F32)

    attended, part = [], []
    done = []
    for m in micros:
        qkv, mixed, p_query, p_passage, *sends = kernel_call(
            attend_body(),
            "attend",
            [SMEM, SMEM, VMEM, VMEM, VMEM],
            [
                shape((rows, qkv_width), BF),
                shape((rows, head_width), BF),
                shape((heads, QLEN, QLEN), BF),
                shape((heads, rows - QLEN, rows - QLEN), BF),
            ]
            + part_out,
            [after(ids_of[m], *done), lengths, tokens, w_attn, qkv_bias],
            matmul * all_cols * 4,
            6e6,
            scratch=[full_low],
        )
        attended.append((qkv, mixed, p_query, p_passage))
        arrived = []
        if ring:
            arrived = [ffn_ups[-1], ffn_downs[-1]]
            if len(ffn_ups) <= less:
                ffn_ups.append(ring_step(after(ffn_ups[-1], qkv), order, 1))
            if len(ffn_downs) <= more:
                ffn_downs.append(ring_step(after(ffn_downs[-1], qkv), order, -1))
        part.append(tp_start(sends, mesh_tp, arrived))
        done = [part[m][0]]

    ffn_here = ()
    if ring:
        while len(ffn_ups) <= less:
            ffn_ups.append(ring_step(ffn_ups[-1], order, 1))
        while len(ffn_downs) <= more:
            ffn_downs.append(ring_step(ffn_downs[-1], order, -1))
        ffn_here = [ffn_ups[-1], ffn_downs[-1]]
        w_fi, w_fo = kernel_call(
            assemble_pair_body(block, mesh_dp),
            "assemble_ffn",
            [SMEM] + [VMEM] * mesh_dp,
            [full_weight, full_weight],
            [ids, ffn_block, *ffn_downs[1:], *ffn_ups[:0:-1]],
            1e6,
            5e6,
        )

    fed, before = [], part[-1][0]
    for m in micros:
        branch = tp_finish(part[m], mesh_tp, before, *(ffn_here if m == 0 else ()))
        normed, inverse, first, first_low, hidden, slope, *sends = kernel_call(
            ffn_body(),
            "ffn",
            [SMEM] + [VMEM] * 8,
            [
                shape((rows, width), BF),
                shape((rows, 1), F32),
                shape((rows, width), F32),
                shape((rows, width), BF),
                shape((rows, inner_width), BF),
                shape((rows, inner_width), BF),
            ]
            + part_out,
            [after(ids_of[m], *done), tokens, *branch, vec, w_fi, w_fo],
            matmul * inner_width * 3,
            9e6,
        )
        fed.append((first, first_low, hidden, slope, normed, inverse))
        part[m] = tp_start(sends, mesh_tp)
        before = part[m][0]
        done = [part[m][0]]

    finals = []
    pooled = []
    for m in micros:
        second = tp_finish(part[m], mesh_tp, before)
        final_low, normed, inverse, sums, emb = kernel_call(
            pool_body(),
            "pool",
            [SMEM, SMEM] + [VMEM] * 6,
            [
                shape((rows, width), BF),
                shape((rows, width), BF),
                shape((rows, 1), F32),
                shape((8, width), F32),
                shape((1, 2, width), F32),
            ],
            [after(ids_of[m], *done), lengths, fed[m][0], *second, vec],
            2e8,
            6e6,
        )
        finals.append(final_low)
        done = [sums]
        gathered = pair_gather(emb, mesh_dp)
        before = gathered[min(2, len(gathered) - 1)]
        pooled.append((normed, inverse, sums, gathered))

    back, entropies = [], []
    for m in micros:
        normed, inverse, sums, gathered = pooled[m]
        spread, entropy = kernel_call(
            loss_body,
            "loss",
            [SMEM, SMEM] + [VMEM] * (1 + len(gathered)),
            [shape((8, width), F32), shape((8, 128), F32)],
            [after(ids_of[m], pooled[-1][2]), lengths, sums, *gathered],
            1e6,
            1e5,
            scratch=[pltpu.VMEM((mesh_dp, 2, width), F32)],
        )
        grad_second, grad_inner, sums4, *sends = kernel_call(
            ffn_back_body(),
            "ffn_back",
            [SMEM, SMEM] + [VMEM] * 8,
            [
                shape((rows, width), BF),
                shape((rows, inner_width), BF),
                shape((EXTRA, width), F32),
            ]
            + part_out,
            [after(ids_of[m], *done), lengths, spread, out_grad, normed, inverse, fed[m][3], vec, w_fi, w_fo],
            matmul * inner_width * 3,
            10e6,
            scratch=[full_low],
        )
        back.append((grad_second, grad_inner, sums4))
        entropies.append(entropy[0, 0])
        part[m] = tp_start(sends, mesh_tp, [pooled[m + 1][3][1]] if m + 1 < micro_count else ())
        before = part[m][0]
        done = [part[m][0]]

    grad_first = [tp_finish(part[0], mesh_tp, before)]
    if ring:
        ffn_blocks = kernel_call(
            ffn_weight_body(block, mesh_dp),
            "ffn_weights",
            [SMEM] + [VMEM] * 8,
            [shape((2 * block, width), BF)] * mesh_dp,
            [after(ids, *done, grad_first[0][3])] + [fed[m][1] for m in micros] + [back[m][1] for m in micros] + [fed[m][2] for m in micros] + [back[m][0] for m in micros],
            matmul * inner_width * 4,
            14e6,
            scratch=[pltpu.VMEM((width, inner_width), F32)] * 2,
        )
        done = [ffn_blocks[0]]
        ffn_up, ffn_down = ring_sums(ffn_blocks, order, less)
        ffn_up.send()
        ffn_down.send()
    else:
        grad_fi = sum(mm(fed[m][1], back[m][1], TN) for m in micros)
        grad_fo = sum(mm(back[m][0], fed[m][2], TN) for m in micros)
        grad_fi = lax.psum_scatter(grad_fi, "dp", scatter_dimension=0, tiled=True)
        grad_fo = lax.psum_scatter(grad_fo, "dp", scatter_dimension=0, tiled=True).T

    last = []
    for m in micros:
        if m:
            grad_first.append(tp_finish(part[m], mesh_tp, before))
        qkv, mixed, p_query, p_passage = attended[m]
        grad_branch, grad_qkv, sums5, bias5, *sends = kernel_call(
            attend_back_body(),
            "attend_back",
            [SMEM] + [VMEM] * 13,
            [
                shape((rows, width), BF),
                shape((rows, qkv_width), BF),
                shape((EXTRA, width), F32),
                shape((EXTRA, qkv_width), F32),
            ]
            + part_out,
            [after(ids, *done), fed[m][4], fed[m][5], *grad_first[m], back[m][0], qkv, mixed, p_query, p_passage, vec, w_attn],
            matmul * all_cols * 6,
            12e6,
            scratch=[full_sum, pltpu.VMEM((rows, head_width), BF), full_low],
        )
        last.append((grad_branch, grad_qkv, sums5, bias5, sends))
        arrived = []
        if ring:
            arrived = [ffn_up.absorb(grad_qkv), ffn_down.absorb(grad_qkv)]
            ffn_up.send()
            ffn_down.send()
        if m + 1 < micro_count:
            part[m] = tp_start(sends, mesh_tp, arrived)
            done = [part[m][0]]
            before = part[m][0]

    if ring:
        attn_blocks = kernel_call(
            attend_weight_body(block, head_bias, mesh_dp),
            "attend_weights",
            [SMEM] + [VMEM] * 13,
            [shape((block + EXTRA, all_cols), BF)] * mesh_dp,
            [after(ids, *arrived), tokens]
            + [last[m][1] for m in micros]
            + [last[m][0] for m in micros]
            + [attended[m][1] for m in micros]
            + [back[m][2] for m in micros]
            + [last[m][2] for m in micros]
            + [last[m][3] for m in micros],
            matmul * all_cols * 2,
            8e6,
            scratch=[pltpu.VMEM((width, all_cols), F32)],
        )
    else:
        grad_w = sum(
            jnp.concatenate([mm(tokens[m, 0], last[m][1], TN), mm(last[m][0], attended[m][1], TN)], axis=1) for m in micros
        )
        attn_blocks = [grad_w]
    part[-1] = tp_start(last[-1][4], mesh_tp, [attn_blocks[0]])
    if ring:
        attn_up, attn_down = ring_sums(attn_blocks, order, more)
        attn_up.send()
        attn_down.send()
        attn_up.absorb(ffn_up.absorb(), part[0][1])
        attn_down.absorb(ffn_down.absorb())
        attn_up.send()
        attn_down.send()
        ffn_down.send()
        attn_up.absorb()
        attn_up.send()
        attn_down.absorb(ffn_down.absorb())
        attn_down.send()
    out_tokens, in_grad, in_grads = None, None, []
    for m in micros:
        aliased = 0 if in_grad is None else 2
        out_tokens, in_grad = kernel_call(
            finish_body(aliased),
            "finish",
            [SMEM] + [VMEM] * 6 + [HBM] * aliased,
            [shape(tokens.shape, BF), shape(tokens.shape, F32)],
            [ids, finals[m], last[m][0], *tp_finish(part[m], mesh_tp, attn_blocks[0])] + ([out_tokens, in_grad] if aliased else []),
            1e8,
            5e6,
            out_specs=[micro_spec(tokens, m)] * 2,
            aliases={7: 0, 8: 1} if aliased else None,
            scratch=[full_sum],
        )
        in_grads.append(in_grad)

    if ring:
        attn_up.absorb(part[1][1], in_grads[0])
        attn_up.send()
        attn_down.absorb()
        pieces = [attn_blocks[0], attn_up.absorb(), attn_down.moving]
        grad_fi, grad_fo = kernel_call(
            unpack_ffn_body,
            "unpack_ffn",
            [VMEM] * 3,
            [shape(ffn_in.shape, F32)] * 2,
            [ffn_blocks[0], ffn_up.moving, ffn_down.moving],
            1e6,
            2e6,
        )
        grad_fo = grad_fo.T
        grads = kernel_call(
            unpack_attn_body,
            "unpack_attn",
            [VMEM] * 3,
            [
                shape(attn_in.shape, F32),
                shape(attn_in_bias.shape, F32),
                shape(attn_out.shape, F32),
                shape(out_biases.shape, F32),
                shape((1, block), F32),
                shape(norm_gains.shape, F32),
                shape(norm_shifts.shape, F32),
            ],
            [after(pieces[0], in_grad), *pieces[1:]],
            1e6,
            2e6,
        )
        grad_ai, grad_ab, grad_ao, grad_ob, grad_fb, grad_ng, grad_ns = grads
        grad_fb = grad_fb.reshape(block)
    else:
        attn_total = lax.psum_scatter(grad_w, "dp", scatter_dimension=0, tiled=True)
        sums = sum(back[m][2] + last[m][2] for m in micros)[:8].reshape(8, mesh_dp, block).transpose(1, 0, 2)
        bias = sum(last[m][3] for m in micros)[7].reshape(3, mesh_dp, head_bias)[0::2].transpose(1, 0, 2)
        bias = jnp.pad(bias.reshape(mesh_dp, 1, 2 * head_bias), ((0, 0), (7, 0), (0, block - 2 * head_bias)))
        small = lax.psum_scatter(sums + bias, "dp", scatter_dimension=0)
        grad_ai = attn_total[:, :qkv_width].reshape(block, 3, head_width).transpose(1, 0, 2)
        grad_ao = attn_total[:, qkv_width:].T
        grad_ab = small[7, : 2 * head_bias].reshape(2, head_bias)
        grad_ob, grad_ng, grad_ns, grad_fb = small[0:2], small[2:4], small[4:6], small[6]

    loss = sum(entropies) / (micro_count * mesh_dp)
    return out_tokens, in_grad, loss, grad_ai, grad_ab, grad_ao, grad_ob, grad_fi, grad_fb, grad_fo, grad_ng, grad_ns


def solution(mesh):
    placed = (
        P(None, "dp", None, None),
        P(None, "dp", None, None),
        P(None, "dp", None),
        P(None, "dp", "tp"),
        P(None, ("tp", "dp")),
        P("tp", "dp"),
        P(None, "dp"),
        P("dp", "tp"),
        P(("tp", "dp")),
        P("tp", "dp"),
        P(None, "dp"),
        P(None, "dp"),
    )
    sizes = (mesh.shape["tp"], mesh.shape["dp"])

    def run(*arrays):
        return on_device(*sizes, *arrays)

    return jax.shard_map(
        run,
        mesh=mesh,
        in_specs=placed,
        out_specs=placed[:2] + (P(),) + placed[3:],
        check_vma=False,
    )
```

```python
import math

import jax
import jax.numpy as jnp
from jax import lax
from jax.experimental import pallas as pl
from jax.experimental.pallas import tpu as pltpu
from jax.sharding import PartitionSpec as P

HEAD_DIM = 64
QLEN = 128
SOFTMAX_TEMP = 0.01
NEG_LARGE = -1e30
ROOT_HALF = 0.7071067811865476
DENSITY_NORM = 0.3989422804014327
VMEM_BYTES = 20 * 2**20
EXTRA = 16
BF = jnp.bfloat16
F32 = jnp.float32
NN = (((1,), (0,)), ((), ()))
NT = (((1,), (1,)), ((), ()))
TN = (((0,), (0,)), ((), ()))
HBM = pl.BlockSpec(memory_space=pl.ANY)
SMEM = pl.BlockSpec(memory_space=pltpu.SMEM)
VMEM = pl.BlockSpec(memory_space=pltpu.VMEM)


def mm(left, right, dims=NN, precision=None):
    return lax.dot_general(left, right, dims, precision=precision, preferred_element_type=F32)


def shape(dims, dtype):
    return jax.ShapeDtypeStruct(dims, dtype)


def kernel_call(body, name, in_specs, outs, args, flops, moved, scratch=(), out_specs=None, aliases=None):
    return pl.pallas_call(
        body,
        name=name,
        grid=(1,) if out_specs is not None else (),
        in_specs=in_specs,
        out_specs=out_specs if out_specs is not None else [VMEM] * len(outs),
        out_shape=outs,
        scratch_shapes=scratch,
        input_output_aliases=aliases or {},
        compiler_params=pltpu.CompilerParams(vmem_limit_bytes=VMEM_BYTES),
        cost_estimate=pl.CostEstimate(flops=int(flops), bytes_accessed=int(moved), transcendentals=0),
    )(*args)


def micro_spec(arr, micro):
    return pl.BlockSpec((1,) + arr.shape[1:], lambda i: (micro,) + (0,) * (len(arr.shape) - 1))


def ring_owner(at, step, count):
    half = count // 2
    place = jnp.where(at % 2 == 0, at // 2, half + (count - 1 - at) // 2)
    place = (place + step) % count
    return jnp.where(place < half, 2 * place, count - 1 - 2 * (place - half))


def pack_attn_body(ai_ref, ao_ref, small_ref, out_ref):
    block, head_width = ai_ref.shape[1], ai_ref.shape[2]
    for j in range(3):
        out_ref[:block, j * head_width : (j + 1) * head_width] = ai_ref[j]
    out_ref[:block, 3 * head_width :] = ao_ref[...].T
    out_ref[block:, :] = jnp.zeros((out_ref.shape[0] - block, out_ref.shape[1]), BF)
    out_ref[block:, :block] = small_ref[...]


def pack_ffn_body(fi_ref, fo_ref, tokens_ref, out_ref):
    block = fi_ref.shape[0]
    out_ref[:block, :] = fi_ref[...]
    out_ref[block:, :] = fo_ref[...]


def assemble_body(block_rows, head_bias, count, steps, first):
    def body(ids_ref, *refs):
        blocks, (w_ref, vec_ref, bias_ref, out_ref) = refs[: len(steps)], refs[-4:]
        width = w_ref.shape[1]
        qkv_width = bias_ref.shape[1]
        vectors, biases = jnp.zeros(vec_ref.shape, F32), jnp.zeros(bias_ref.shape, F32)
        if not first:
            vectors, biases = refs[len(steps) + 1][...], refs[len(steps) + 2][...]
        lane = lax.broadcasted_iota(jnp.int32, (128, width), 0)
        place = lax.broadcasted_iota(jnp.int32, (128, width), 1)
        for block, k in zip(blocks, steps):
            owner = ring_owner(ids_ref[1], k, count)
            at = pl.ds(pl.multiple_of(owner * block_rows, 16), block_rows)
            w_ref[at, :] = block[:block_rows, :]
            out_ref[at, :] = block[:block_rows, qkv_width:]
            small = block[block_rows : block_rows + EXTRA, :128]
            pick = (place == owner * block_rows + lane) & (lane < block_rows)
            vectors += mm(small, jnp.where(pick, 1.0, 0.0).astype(BF))
            biases += mm(small, bias_pick(owner, head_bias, qkv_width, lane, place))
        vec_ref[...] = vectors
        bias_ref[...] = biases

    return body


def assemble_pair_body(block_rows, count):
    def body(ids_ref, *refs):
        blocks, (fi_ref, fo_ref) = refs[:count], refs[count:]
        for k in range(count):
            owner = ring_owner(ids_ref[1], k, count)
            at = pl.ds(pl.multiple_of(owner * block_rows, 16), block_rows)
            fi_ref[at, :] = blocks[k][:block_rows, :]
            fo_ref[at, :] = blocks[k][block_rows:, :]

    return body


def bias_pick(owner, head_bias, qkv_width, lane, place):
    lane, place = lane[:, :qkv_width], place[:, :qkv_width]
    values_at = qkv_width * 2 // 3
    for_query = (lane < head_bias) & (place == owner * head_bias + lane)
    for_value = (
        (lane >= head_bias)
        & (lane < 2 * head_bias)
        & (place == values_at + owner * head_bias + lane - head_bias)
    )
    return jnp.where(for_query | for_value, 1.0, 0.0).astype(BF)


def split_halves(full_ref, core, send_a, send_b, keep_ref):
    half, piece = keep_ref.shape[0], send_a.shape[0]
    keep_ref[...] = full_ref[pl.ds(pl.multiple_of(core * half, 16), half), :]
    for k, ref in enumerate((send_a, send_b)):
        ref[...] = full_ref[pl.ds(pl.multiple_of((1 - core) * half + k * piece, 16), piece), :]


def halves(core, half):
    return [pl.ds(pl.multiple_of(place * half, 16), half) for place in (1 - core, core)]


def send_halves(make, core, send_a, send_b, keep_ref):
    half, piece = keep_ref.shape[0], send_a.shape[0]
    away, here = halves(core, half)
    value = make(away).astype(BF)
    send_a[...] = value[:piece]
    send_b[...] = value[piece:]
    keep_ref[...] = make(here).astype(BF)


def half_body(keep_ref, a_ref, b_ref, out_ref):
    piece = a_ref.shape[0]
    for k, ref in enumerate((a_ref, b_ref)):
        part = slice(k * piece, (k + 1) * piece)
        out_ref[part, :] = add_low(keep_ref[part, :], ref[...])


def join_halves(full_ref, core, parts):
    half = parts[0].shape[0]
    for near, far, place in ((parts[0], parts[1], core), (parts[2], parts[3], 1 - core)):
        full_ref[pl.ds(pl.multiple_of(place * half, 16), half), :] = near[...].astype(F32) + far[...].astype(F32)


def over_sum(core, parts, step):
    half = parts[0].shape[0]
    piece = half // 2
    for near, far, place in ((parts[0], parts[1], core), (parts[2], parts[3], 1 - core)):

        def one(k, carry, near=near, far=far, place=place):
            at = pl.ds(pl.multiple_of(k * piece, 16), piece)
            start = pl.multiple_of(place * half + k * piece, 16)
            step(pl.ds(start, piece), start, near[at, :].astype(F32) + far[at, :].astype(F32))
            return carry

        lax.fori_loop(0, 2, one, 0)


def segment_masks(start, dims, lengths):
    row = lax.broadcasted_iota(jnp.int32, dims, 0) + start
    return row < QLEN, (row < QLEN) & (row < lengths[0]), (row >= QLEN) & (row - QLEN < lengths[1])


def segments(rows):
    return ((0, QLEN), (QLEN, rows))


def attend_body():
    def body(ids_ref, len_ref, x_ref, w_ref, bias_ref, qkv_ref, mixed_ref, pq_ref, pp_ref):
        micro = ids_ref[2]
        rows = x_ref.shape[2]
        heads = pq_ref.shape[0]
        width = heads * HEAD_DIM
        x = x_ref[micro, 0]
        bias = bias_ref[7:8, :]
        qkv_ref[...] = (mm(x, w_ref[:, : 3 * width]) + bias).astype(BF)
        factor = 1.0 / math.sqrt(HEAD_DIM)
        for seg, (low, high) in enumerate(segments(rows)):
            length = len_ref[micro, 0, seg]
            size = high - low
            p_ref = pp_ref if seg else pq_ref
            visible = lax.broadcasted_iota(jnp.int32, (size, size), 0) < length
            for h in range(heads):
                at = h * HEAD_DIM
                queries = qkv_ref[low:high, at : at + HEAD_DIM]
                keys_low = qkv_ref[low:high, width + at : width + at + HEAD_DIM]
                values = qkv_ref[low:high, 2 * width + at : 2 * width + at + HEAD_DIM]
                scores = jnp.where(visible, mm(keys_low, queries, NT) * factor, NEG_LARGE)
                raised = jnp.exp(scores - jnp.max(scores, axis=0, keepdims=True))
                weights = (raised * (1.0 / jnp.sum(raised, axis=0, keepdims=True))).astype(BF)
                p_ref[h] = weights
                mixed_ref[low:high, at : at + HEAD_DIM] = mm(values, weights, TN).T.astype(BF)

    return body


def norm_one(x, branch, shift_out):
    hidden = x.astype(F32) + (branch.astype(F32) + shift_out)
    center = hidden - jnp.mean(hidden, axis=-1, keepdims=True)
    inverse = lax.rsqrt(jnp.mean(center * center, axis=-1, keepdims=True) + 1e-12)
    return center * inverse, inverse


def place_heads(own, parts, full_ref):
    for at in range(len(parts)):

        @pl.when(own == at)
        def _():
            for k, ref in enumerate(parts):
                width = ref.shape[1]
                full_ref[:, (at ^ k) * width : ((at ^ k) + 1) * width] = ref[...]


def gather_out_body(ids_ref, s0, s1, s2, s3, out_ref):
    place_heads(ids_ref[3], (s0, s1, s2, s3), out_ref)


def gelu_parts(inner):
    cumulative = 0.5 * (1.0 + lax.erf(inner * ROOT_HALF))
    density = jnp.exp(-0.5 * inner * inner) * DENSITY_NORM
    return (inner * cumulative).astype(BF), (cumulative + inner * density).astype(BF)


def ffn_body():
    def body(
        ids_ref, x_ref, s0, s1, s2, s3, out_ref, vec_ref, fi_ref, fo_ref,
        normed_ref, inv_ref, first_ref, low_ref, hidden_ref, slope_ref, send_a, send_b, keep_ref, mixed_ref,
    ):
        micro, core = ids_ref[2], ids_ref[0]
        half, piece = keep_ref.shape[0], send_a.shape[0]
        place_heads(ids_ref[3], (s0, s1, s2, s3), mixed_ref)
        for part, away in zip(halves(core, half), (True, False)):
            branch = mm(mixed_ref[part, :], out_ref[...], NT)
            normed, inverse = norm_one(x_ref[micro, 0, part, :], branch, vec_ref[0:1, :])
            normed_ref[part, :] = normed.astype(BF)
            inv_ref[part, :] = inverse
            first = normed * vec_ref[2:3, :] + vec_ref[4:5, :]
            first_ref[part, :] = first
            low = first.astype(BF)
            low_ref[part, :] = low
            hidden, slope = gelu_parts(mm(low, fi_ref[...]) + vec_ref[6:7, :])
            hidden_ref[part, :] = hidden
            slope_ref[part, :] = slope
            second = mm(hidden, fo_ref[...], NT).astype(BF)
            if away:
                send_a[...] = second[:piece]
                send_b[...] = second[piece:]
            else:
                keep_ref[...] = second

    return body


def pool_body():
    def body(
        ids_ref, len_ref, first_ref, s0, s1, s2, s3, vec_ref, out_ref, normed_ref, inv_ref, pooled_ref, emb_ref
    ):
        micro = ids_ref[2]
        pooled_ref[...] = jnp.zeros(pooled_ref.shape, F32)
        lengths = [len_ref[micro, 0, seg] for seg in range(2)]

        def step(part, start, second):
            hidden = first_ref[part, :] + (second + vec_ref[1:2, :])
            center = hidden - jnp.mean(hidden, axis=-1, keepdims=True)
            inverse = lax.rsqrt(jnp.mean(center * center, axis=-1, keepdims=True) + 1e-12)
            normed = center * inverse
            normed_ref[part, :] = normed.astype(BF)
            inv_ref[part, :] = inverse
            final = normed * vec_ref[3:4, :] + vec_ref[5:6, :]
            out_ref[part, :] = final.astype(BF)
            masks = segment_masks(start, (final.shape[0], 1), lengths)
            for seg in range(2):
                kept = jnp.where(masks[seg + 1], final, 0.0)
                pooled_ref[seg : seg + 1, :] += jnp.sum(kept, axis=0, keepdims=True)

        over_sum(ids_ref[0], (s0, s1, s2, s3), step)
        for seg in range(2):
            summed = pooled_ref[seg : seg + 1, :] / len_ref[micro, 0, seg].astype(F32)
            unit = summed * lax.rsqrt(jnp.sum(summed * summed, axis=-1, keepdims=True) + 1e-06)
            pooled_ref[seg : seg + 1, :] = summed
            emb_ref[0, seg : seg + 1, :] = unit

    return body


def loss_grads(queries, passages, own):
    highest = lax.Precision.HIGHEST
    count = queries.shape[0]
    row = lax.broadcasted_iota(jnp.int32, (count, count), 0)
    col = lax.broadcasted_iota(jnp.int32, (count, count), 1)
    same = jnp.where(row == col, 1.0, 0.0)
    logits = mm(queries, passages, NT, highest) / SOFTMAX_TEMP
    top = jnp.max(logits, axis=-1, keepdims=True)
    log_norm = top + jnp.log(jnp.sum(jnp.exp(logits - top), axis=-1, keepdims=True))
    entropy = jnp.sum(jnp.sum(same * (log_norm - logits), axis=-1, keepdims=True), axis=0, keepdims=True)
    grad = (jnp.exp(logits - log_norm) - same) / SOFTMAX_TEMP
    turned = mm(passages, queries, NT, highest) / SOFTMAX_TEMP
    top_t = jnp.max(turned, axis=0, keepdims=True)
    norm_t = top_t + jnp.log(jnp.sum(jnp.exp(turned - top_t), axis=0, keepdims=True))
    grad_t = (jnp.exp(turned - norm_t) - same) / SOFTMAX_TEMP
    own_col = jnp.sum(jnp.where(col == own, grad, 0.0), axis=1, keepdims=True)
    own_row = jnp.sum(jnp.where(col == own, grad_t, 0.0), axis=1, keepdims=True)
    grad_query = jnp.sum(own_row * passages, axis=0, keepdims=True)
    grad_passage = jnp.sum(own_col * queries, axis=0, keepdims=True)
    return entropy, (grad_query, grad_passage)


def norm_backward(upstream, normed, inverse, gain):
    scaled = upstream * gain
    centered = scaled - jnp.mean(scaled, axis=-1, keepdims=True)
    return inverse * (centered - normed * jnp.mean(scaled * normed, axis=-1, keepdims=True))


def loss_body(*refs):
    ids_ref, len_ref, pooled_ref = refs[:3]
    pieces, (spread_ref, loss_ref, emb_ref) = refs[3:-3], refs[-3:]
    place = 0
    for piece in pieces:
        for k in range(piece.shape[0]):
            emb_ref[ids_ref[1] ^ place] = piece[k]
            place += 1
    entropy, unit_grads = loss_grads(emb_ref[:, 0, :], emb_ref[:, 1, :], ids_ref[1])
    loss_ref[...] = jnp.broadcast_to(entropy, loss_ref.shape)
    for seg in range(2):
        summed = pooled_ref[seg : seg + 1, :]
        up = unit_grads[seg]
        inverse = lax.rsqrt(jnp.sum(summed * summed, axis=-1, keepdims=True) + 1e-06)
        cubed = inverse * inverse * inverse
        grad = inverse * up - cubed * summed * jnp.sum(summed * up, axis=-1, keepdims=True)
        spread_ref[seg : seg + 1, :] = grad / len_ref[ids_ref[2], 0, seg].astype(F32)


def ffn_back_body():
    def body(
        ids_ref, len_ref, spread_ref, cot_ref, normed_ref, inv_ref, slope_ref, vec_ref, fi_ref, fo_ref,
        second_ref, inner_ref, sums_ref, send_a, send_b, keep_ref, part_ref,
    ):
        micro = ids_ref[2]
        rows = normed_ref.shape[0]
        zero = jnp.zeros((1, normed_ref.shape[1]), F32)

        def step(k, sums):
            part = pl.ds(pl.multiple_of(k * QLEN, QLEN), QLEN)
            seg = jnp.minimum(k, 1)
            cot = cot_ref[micro, 0, part, :].astype(F32) + spread_ref[pl.ds(seg, 1), :]
            place = lax.broadcasted_iota(jnp.int32, cot.shape, 0) + (k - seg) * QLEN
            grad_final = jnp.where(place < len_ref[micro, 0, seg], cot, 0.0)
            normed = normed_ref[part, :].astype(F32)
            low = norm_backward(grad_final, normed, inv_ref[part, :], vec_ref[3:4, :]).astype(BF)
            second_ref[part, :] = low
            terms = (grad_final * normed, grad_final, low.astype(F32))
            return tuple(total + jnp.sum(term, axis=0, keepdims=True) for total, term in zip(sums, terms))

        gain_sum, shift_sum, bias_sum = lax.fori_loop(0, rows // QLEN, step, (zero, zero, zero))
        grad_hidden = mm(second_ref[...], fo_ref[...])
        grad_inner = (grad_hidden * slope_ref[...].astype(F32)).astype(BF)
        inner_ref[...] = grad_inner
        inner_sum = jnp.sum(grad_inner.astype(F32), axis=0, keepdims=True)
        part_ref[...] = mm(inner_ref[...], fi_ref[...], NT).astype(BF)
        split_halves(part_ref, ids_ref[0], send_a, send_b, keep_ref)
        sums_ref[...] = jnp.zeros(sums_ref.shape, F32)
        sums_ref[1:2, :] = bias_sum
        sums_ref[3:4, :] = gain_sum
        sums_ref[5:6, :] = shift_sum
        sums_ref[6:7, :] = inner_sum

    return body


def attend_back_body():
    def body(
        ids_ref, normed_ref, inv_ref, s0, s1, s2, s3, second_ref, qkv_ref, mixed_ref, pq_ref, pp_ref, vec_ref, w_ref,
        branch_ref, gqkv_ref, sums_ref, bias_ref, send_a, send_b, keep_ref, sum_ref, gm_ref, part_ref,
    ):
        rows = normed_ref.shape[0]
        heads = pq_ref.shape[0]
        width = heads * HEAD_DIM
        core = ids_ref[0]
        join_halves(sum_ref, core, (s0, s1, s2, s3))
        zero = jnp.zeros((1, normed_ref.shape[1]), F32)

        def step(k, sums):
            part = pl.ds(pl.multiple_of(k * QLEN, QLEN), QLEN)
            normed = normed_ref[part, :].astype(F32)
            upstream = sum_ref[part, :] + second_ref[part, :].astype(F32)
            low = norm_backward(upstream, normed, inv_ref[part, :], vec_ref[2:3, :]).astype(BF)
            branch_ref[part, :] = low
            terms = (upstream * normed, upstream, low.astype(F32))
            return tuple(total + jnp.sum(term, axis=0, keepdims=True) for total, term in zip(sums, terms))

        gain_sum, shift_sum, out_sum = lax.fori_loop(0, rows // QLEN, step, (zero, zero, zero))
        sums_ref[...] = jnp.zeros(sums_ref.shape, F32)
        sums_ref[0:1, :] = out_sum
        sums_ref[2:3, :] = gain_sum
        sums_ref[4:5, :] = shift_sum
        gm_ref[...] = mm(branch_ref[...], w_ref[:, 3 * width :]).astype(BF)
        factor = 1.0 / math.sqrt(HEAD_DIM)
        for seg, (low_row, high_row) in enumerate(segments(rows)):
            part = slice(low_row, high_row)
            p_ref = pp_ref if seg else pq_ref
            for h in range(heads):
                at = h * HEAD_DIM
                columns = [slice(j * width + at, j * width + at + HEAD_DIM) for j in range(3)]
                grad = gm_ref[part, columns[0]]
                weights = p_ref[h]
                grad_weights = mm(qkv_ref[part, columns[2]], grad, NT)
                low_weights = weights.astype(F32)
                delta = jnp.sum(low_weights * grad_weights, axis=0, keepdims=True)
                grad_scores = (low_weights * (grad_weights - delta)).astype(BF)
                gqkv_ref[part, columns[0]] = (mm(qkv_ref[part, columns[1]], grad_scores, TN) * factor).T.astype(BF)
                gqkv_ref[part, columns[1]] = (mm(grad_scores, qkv_ref[part, columns[0]]) * factor).astype(BF)
                gqkv_ref[part, columns[2]] = mm(weights, grad).astype(BF)
        gqkv = gqkv_ref[...]
        bias_ref[...] = jnp.zeros(bias_ref.shape, F32)
        bias_ref[7:8, :] = jnp.sum(gqkv.astype(F32), axis=0, keepdims=True)
        part_ref[...] = mm(gqkv, w_ref[:, : 3 * width], NT).astype(BF)
        split_halves(part_ref, core, send_a, send_b, keep_ref)

    return body


def ffn_weight_body(block_rows, count):
    def body(ids_ref, low_a, low_b, gi_a, gi_b, hid_a, hid_b, gs_a, gs_b, *refs):
        outs, (fi_ref, fo_ref) = refs[:-2], refs[-2:]
        fi_ref[...] = mm(low_a[...], gi_a[...], TN) + mm(low_b[...], gi_b[...], TN)
        fo_ref[...] = mm(gs_a[...], hid_a[...], TN) + mm(gs_b[...], hid_b[...], TN)
        for k in range(count):
            at = pl.ds(pl.multiple_of(ring_owner(ids_ref[1], k, count) * block_rows, 16), block_rows)
            outs[k][:block_rows, :] = fi_ref[at, :].astype(BF)
            outs[k][block_rows:, :] = fo_ref[at, :].astype(BF)

    return body


def attend_weight_body(block_rows, head_bias, count):
    def body(
        ids_ref, x_ref, gq_a, gq_b, gb_a, gb_b, mx_a, mx_b, s4_a, s4_b, s5_a, s5_b, b_a, b_b, *refs
    ):
        outs, w_ref = refs[:-1], refs[-1]
        qkv = gq_a.shape[1]
        width = w_ref.shape[0]
        w_ref[:, :qkv] = mm(x_ref[0, 0], gq_a[...], TN) + mm(x_ref[1, 0], gq_b[...], TN)
        w_ref[:, qkv:] = mm(gb_a[...], mx_a[...], TN) + mm(gb_b[...], mx_b[...], TN)
        sums = (s4_a[...] + s4_b[...] + s5_a[...] + s5_b[...]).astype(BF)
        biases = (b_a[...] + b_b[...]).astype(BF)
        lane = lax.broadcasted_iota(jnp.int32, (128, width), 0)
        place = lax.broadcasted_iota(jnp.int32, (128, width), 1)
        for k in range(count):
            owner = ring_owner(ids_ref[1], k, count)
            outs[k][:block_rows, :] = w_ref[pl.ds(pl.multiple_of(owner * block_rows, 16), block_rows), :].astype(BF)
            outs[k][block_rows:, 128:] = jnp.zeros((EXTRA, width - 128), BF)
            pick = (place == owner * block_rows + lane) & (lane < block_rows)
            small = mm(sums, jnp.where(pick, 1.0, 0.0).astype(BF), NT)
            small += mm(biases, bias_pick(owner, head_bias, qkv, lane, place), NT)
            outs[k][block_rows:, :128] = small.astype(BF)

    return body


def unpack_attn_body(own_ref, up_ref, down_ref, ai_ref, ab_ref, ao_ref, ob_ref, fb_ref, ng_ref, ns_ref):
    block, head_width = ai_ref.shape[1], ai_ref.shape[2]
    head_bias = ab_ref.shape[1]
    total = own_ref[...].astype(F32) + up_ref[...].astype(F32) + down_ref[...].astype(F32)
    for j in range(3):
        ai_ref[j] = total[:block, j * head_width : (j + 1) * head_width]
    ao_ref[...] = total[:block, 3 * head_width :].T
    small = total[block : block + 8, :128]
    ob_ref[...] = small[0:2, :block]
    ng_ref[...] = small[2:4, :block]
    ns_ref[...] = small[4:6, :block]
    fb_ref[...] = small[6:7, :block]
    for j in range(2):
        ab_ref[j : j + 1, :] = small[7:8, j * head_bias : (j + 1) * head_bias]


def unpack_ffn_body(own_ref, up_ref, down_ref, fi_ref, fo_ref):
    block = fi_ref.shape[0]
    for part, out_ref in ((slice(0, block), fi_ref), (slice(block, 2 * block), fo_ref)):
        out_ref[...] = own_ref[part, :].astype(F32) + up_ref[part, :].astype(F32) + down_ref[part, :].astype(F32)


def finish_body(aliased):
    def body(ids_ref, final_ref, gh_ref, s0, s1, s2, s3, *refs):
        tokens_ref, out_ref, full_ref = refs[aliased:]
        tokens_ref[0, 0] = final_ref[...]
        join_halves(full_ref, ids_ref[0], (s0, s1, s2, s3))
        out_ref[0, 0] = full_ref[...] + gh_ref[...].astype(F32)

    return body


def core_swap(value, count):
    return lax.ppermute(value, "tp", [(i, i ^ 1) for i in range(count)])


def chip_swap(value, count):
    return lax.ppermute(value, "tp", [(i, i ^ 2) for i in range(count)])


def add_low(left, right):
    return (left.astype(F32) + right.astype(F32)).astype(BF)


def tp_start(parts, count, ready=()):
    send_a, send_b, keep = parts
    send_a = after(send_a, *ready)
    got = [core_swap(send_a, count), core_swap(send_b, count)]
    near = kernel_call(half_body, "half", [VMEM] * 3, [shape(keep.shape, BF)], [keep, *got], 5e5, 2e6)[0]
    return near, chip_swap(near, count), core_swap(near, count)


def tp_finish(started, count, *later):
    near, far, near_other = started
    return near, far, near_other, core_swap(after(far, *later), count)


def pair_gather(value, count):
    pieces, step = [value], 1
    while step < count:
        send = pieces[0] if step == 1 else jnp.concatenate(pieces)
        pieces.append(lax.ppermute(send, "dp", [(i, i ^ step) for i in range(count)]))
        step *= 2
    return pieces


def after(ids, *values):
    return lax.optimization_barrier((ids, *values))[0]


def ring_order(count):
    return list(range(0, count, 2)) + list(range(count - 1, 0, -2))


def ring_step(value, order, step):
    count = len(order)
    return lax.ppermute(value, "dp", [(order[i], order[(i + step) % count]) for i in range(count)])


class RingSum:
    def __init__(self, parts, order, way):
        self.parts, self.order, self.way = parts, order, way
        self.moving, self.at = parts[0], 1

    def send(self, *ready):
        self.moving = ring_step(after(self.moving, *ready), self.order, self.way)

    def absorb(self, *ready):
        self.moving = after(self.moving, *ready)
        if self.at < len(self.parts):
            self.moving = add_low(self.moving, self.parts[self.at])
        self.at += 1
        return self.moving


def ring_sums(blocks, order, up):
    return RingSum(blocks[up:0:-1], order, 1), RingSum(blocks[up + 1 :], order, -1)


def on_device(mesh_tp, mesh_dp, *arrays):
    tokens, out_grad, lengths, attn_in, attn_in_bias, attn_out, out_biases, ffn_in, ffn_in_bias, ffn_out, norm_gains, norm_shifts = arrays
    micro_count, _, rows, width = tokens.shape
    block = attn_in.shape[1]
    inner_width = ffn_in.shape[1]
    head_width = attn_in.shape[2]
    heads = head_width // HEAD_DIM
    qkv_width = 3 * head_width
    head_bias = attn_in_bias.shape[1]
    half = rows // 2
    ring = block % 16 == 0
    order = ring_order(mesh_dp)
    all_cols = qkv_width + head_width
    matmul = 2.0 * rows * width
    micros = range(micro_count)
    tp_at = lax.axis_index("tp")
    ids_of = [jnp.stack([tp_at % 2, lax.axis_index("dp"), m, tp_at]).astype(jnp.int32) for m in micros]
    ids = ids_of[0]
    attn_in, out_biases = after(attn_in, *ids_of), after(out_biases, *ids_of)

    vec_shape, bias_shape = shape((EXTRA, width), F32), shape((EXTRA, qkv_width), F32)
    full_weight = shape((width, inner_width), BF)
    last_row = jnp.pad(attn_in_bias.reshape(1, 2 * head_bias), ((0, 0), (0, block - 2 * head_bias)))
    if ring:
        small = jnp.concatenate(
            [out_biases, norm_gains, norm_shifts, ffn_in_bias[None], last_row, jnp.zeros((EXTRA - 8, block), BF)]
        )
        attn_block = kernel_call(
            pack_attn_body, "pack_attn", [VMEM] * 3, [shape((block + EXTRA, all_cols), BF)], [attn_in, attn_out, small], 1e6, 1e6
        )[0]
        ffn_block = kernel_call(
            pack_ffn_body,
            "pack_ffn",
            [VMEM] * 3,
            [shape((2 * block, inner_width), BF)],
            [ffn_in, ffn_out.T, after(tokens, attn_block)],
            1e6,
            1e6,
        )[0]
        more, less = mesh_dp // 2, mesh_dp - 1 - mesh_dp // 2

        def assemble(blocks, steps, held=()):
            return kernel_call(
                assemble_body(block, head_bias, mesh_dp, steps, not held),
                "assemble",
                [SMEM] + [VMEM] * (len(blocks) + len(held)),
                [shape((width, all_cols), BF), vec_shape, bias_shape, shape((width, head_width), BF)],
                [ids, *blocks, *held],
                1e8,
                3e6,
                aliases={1 + len(blocks): 0, 4 + len(blocks): 3} if held else None,
            )

        ups, downs = [attn_block], [attn_block]
        weights = ()
        for step in range(more):
            if step == more - 1:
                steps = [0, *range(1, less), *range(mesh_dp - less + 1, mesh_dp)]
                weights = assemble([attn_block, *downs[1:less], *ups[less - 1 : 0 : -1]], steps)
            ups.append(ring_step(ups[-1], order, 1))
            if step < less:
                downs.append(ring_step(downs[-1], order, -1))
        w_attn, vec, qkv_bias, w_out = assemble([downs[less], *ups[: less - 1 : -1]], [less, *range(less + 1, mesh_dp - less + 1)], weights)
        ffn_ups, ffn_downs = [after(ffn_block, ups[-1])], [after(ffn_block, downs[-1])]
        ffn_downs.append(ring_step(ffn_downs[-1], order, -1))
        ffn_downs.append(ring_step(ffn_downs[-1], order, -1))
        ffn_ups.append(ring_step(ffn_ups[-1], order, 1))
    else:
        attn_rows = jnp.concatenate([attn_in.transpose(1, 0, 2).reshape(block, qkv_width), attn_out.T], axis=1)
        vectors = jnp.concatenate([out_biases, norm_gains, norm_shifts, ffn_in_bias[None], last_row])
        w_attn = lax.all_gather(attn_rows, "dp", axis=0, tiled=True)
        every = lax.all_gather(vectors, "dp", axis=0).astype(F32)
        vec = jnp.pad(every.transpose(1, 0, 2).reshape(8, width), ((0, EXTRA - 8), (0, 0)))
        pair = every[:, 7, : 2 * head_bias].reshape(mesh_dp, 2, head_bias).transpose(1, 0, 2).reshape(2, head_width)
        both = jnp.concatenate([pair[0], jnp.zeros((head_width,), F32), pair[1]])
        qkv_bias = jnp.pad(both[None], ((7, EXTRA - 8), (0, 0)))
        w_out = w_attn[:, qkv_width:]
        w_fi = lax.all_gather(ffn_in, "dp", axis=0, tiled=True)
        w_fo = lax.all_gather(ffn_out.T, "dp", axis=0, tiled=True)

    part_out = [shape((half // 2, width), BF)] * 2 + [shape((half, width), BF)]
    full_low = pltpu.VMEM((rows, width), BF)
    full_sum = pltpu.VMEM((rows, width), F32)

    far_out = chip_swap(w_out, mesh_tp)
    attended, far_heads, part = [], [], [None] * micro_count
    done, waiting = [], []
    for m in micros:
        qkv, mixed, p_query, p_passage = kernel_call(
            attend_body(),
            "attend",
            [SMEM, SMEM, VMEM, VMEM, VMEM],
            [
                shape((rows, qkv_width), BF),
                shape((rows, head_width), BF),
                shape((heads, QLEN, QLEN), BF),
                shape((heads, rows - QLEN, rows - QLEN), BF),
            ],
            [after(ids_of[m], *done), lengths, tokens, w_attn, qkv_bias],
            matmul * all_cols * 4,
            6e6,
        )
        attended.append((qkv, mixed, p_query, p_passage))
        done = [mixed]
        if ring:
            waiting = waiting + [ffn_ups[-1], ffn_downs[-1]]
            if len(ffn_ups) <= less:
                ffn_ups.append(ring_step(after(ffn_ups[-1], qkv), order, 1))
            if len(ffn_downs) <= more:
                ffn_downs.append(ring_step(after(ffn_downs[-1], qkv), order, -1))
        far_heads.append(chip_swap(after(mixed, *waiting), mesh_tp))
        waiting = []
    out_full = kernel_call(
        gather_out_body,
        "gather_out",
        [SMEM] + [VMEM] * 4,
        [shape((width, mesh_tp * head_width), BF)],
        [ids, w_out, core_swap(w_out, mesh_tp), far_out, core_swap(far_out, mesh_tp)],
        1e6,
        3e6,
    )[0]
    done = []

    if ring:
        while len(ffn_ups) <= less:
            ffn_ups.append(ring_step(ffn_ups[-1], order, 1))
        while len(ffn_downs) <= more:
            ffn_downs.append(ring_step(ffn_downs[-1], order, -1))
        w_fi, w_fo = kernel_call(
            assemble_pair_body(block, mesh_dp),
            "assemble_ffn",
            [SMEM] + [VMEM] * mesh_dp,
            [full_weight, full_weight],
            [ids, ffn_block, *ffn_downs[1:], *ffn_ups[:0:-1]],
            1e6,
            5e6,
        )

    fed = []
    for m in micros:
        ready = [part[0][0]] if m else []
        branch = [attended[m][1], core_swap(attended[m][1], mesh_tp), far_heads[m], core_swap(after(far_heads[m], *ready), mesh_tp)]
        normed, inverse, first, first_low, hidden, slope, *sends = kernel_call(
            ffn_body(),
            "ffn",
            [SMEM] + [VMEM] * 9,
            [
                shape((rows, width), BF),
                shape((rows, 1), F32),
                shape((rows, width), F32),
                shape((rows, width), BF),
                shape((rows, inner_width), BF),
                shape((rows, inner_width), BF),
            ]
            + part_out,
            [after(ids_of[m], *done), tokens, *branch, out_full, vec, w_fi, w_fo],
            matmul * (inner_width * 2 + width),
            9e6,
            scratch=[pltpu.VMEM((rows, mesh_tp * head_width), BF)],
        )
        fed.append((first, first_low, hidden, slope, normed, inverse))
        part[m] = tp_start(sends, mesh_tp, [far_heads[m + 1]] if m + 1 < micro_count else [])
        before = part[m][0]
        done = [part[m][0]]

    finals = []
    pooled = []
    for m in micros:
        second = tp_finish(part[m], mesh_tp, before)
        final_low, normed, inverse, sums, emb = kernel_call(
            pool_body(),
            "pool",
            [SMEM, SMEM] + [VMEM] * 6,
            [
                shape((rows, width), BF),
                shape((rows, width), BF),
                shape((rows, 1), F32),
                shape((8, width), F32),
                shape((1, 2, width), F32),
            ],
            [after(ids_of[m], *done), lengths, fed[m][0], *second, vec],
            2e8,
            6e6,
        )
        finals.append(final_low)
        done = [sums]
        gathered = pair_gather(emb, mesh_dp)
        before = gathered[min(2, len(gathered) - 1)]
        pooled.append((normed, inverse, sums, gathered))

    back, entropies = [], []
    for m in micros:
        normed, inverse, sums, gathered = pooled[m]
        spread, entropy = kernel_call(
            loss_body,
            "loss",
            [SMEM, SMEM] + [VMEM] * (1 + len(gathered)),
            [shape((8, width), F32), shape((8, 128), F32)],
            [after(ids_of[m], pooled[-1][2]), lengths, sums, *gathered],
            1e6,
            1e5,
            scratch=[pltpu.VMEM((mesh_dp, 2, width), F32)],
        )
        grad_second, grad_inner, sums4, *sends = kernel_call(
            ffn_back_body(),
            "ffn_back",
            [SMEM, SMEM] + [VMEM] * 8,
            [
                shape((rows, width), BF),
                shape((rows, inner_width), BF),
                shape((EXTRA, width), F32),
            ]
            + part_out,
            [after(ids_of[m], *done), lengths, spread, out_grad, normed, inverse, fed[m][3], vec, w_fi, w_fo],
            matmul * inner_width * 3,
            10e6,
            scratch=[full_low],
        )
        back.append((grad_second, grad_inner, sums4))
        entropies.append(entropy[0, 0])
        part[m] = tp_start(sends, mesh_tp, [pooled[m + 1][3][1]] if m + 1 < micro_count else ())
        before = part[m][0]
        done = [part[m][0]]

    grad_first = [tp_finish(part[0], mesh_tp, before)]
    if ring:
        ffn_blocks = kernel_call(
            ffn_weight_body(block, mesh_dp),
            "ffn_weights",
            [SMEM] + [VMEM] * 8,
            [shape((2 * block, width), BF)] * mesh_dp,
            [after(ids, *done, grad_first[0][3])] + [fed[m][1] for m in micros] + [back[m][1] for m in micros] + [fed[m][2] for m in micros] + [back[m][0] for m in micros],
            matmul * inner_width * 4,
            14e6,
            scratch=[pltpu.VMEM((width, inner_width), F32)] * 2,
        )
        done = [ffn_blocks[0]]
        ffn_up, ffn_down = ring_sums(ffn_blocks, order, less)
        ffn_up.send()
        ffn_down.send()
    else:
        grad_fi = sum(mm(fed[m][1], back[m][1], TN) for m in micros)
        grad_fo = sum(mm(back[m][0], fed[m][2], TN) for m in micros)
        grad_fi = lax.psum_scatter(grad_fi, "dp", scatter_dimension=0, tiled=True)
        grad_fo = lax.psum_scatter(grad_fo, "dp", scatter_dimension=0, tiled=True).T

    last = []
    for m in micros:
        if m:
            grad_first.append(tp_finish(part[m], mesh_tp, before))
        qkv, mixed, p_query, p_passage = attended[m]
        grad_branch, grad_qkv, sums5, bias5, *sends = kernel_call(
            attend_back_body(),
            "attend_back",
            [SMEM] + [VMEM] * 13,
            [
                shape((rows, width), BF),
                shape((rows, qkv_width), BF),
                shape((EXTRA, width), F32),
                shape((EXTRA, qkv_width), F32),
            ]
            + part_out,
            [after(ids, *done), fed[m][4], fed[m][5], *grad_first[m], back[m][0], qkv, mixed, p_query, p_passage, vec, w_attn],
            matmul * all_cols * 6,
            12e6,
            scratch=[full_sum, pltpu.VMEM((rows, head_width), BF), full_low],
        )
        last.append((grad_branch, grad_qkv, sums5, bias5, sends))
        arrived = []
        if ring:
            arrived = [ffn_up.absorb(grad_qkv), ffn_down.absorb(grad_qkv)]
            ffn_up.send()
            ffn_down.send()
        if m + 1 < micro_count:
            part[m] = tp_start(sends, mesh_tp, arrived)
            done = [part[m][0]]
            before = part[m][0]

    if ring:
        attn_blocks = kernel_call(
            attend_weight_body(block, head_bias, mesh_dp),
            "attend_weights",
            [SMEM] + [VMEM] * 13,
            [shape((block + EXTRA, all_cols), BF)] * mesh_dp,
            [ids, tokens]
            + [last[m][1] for m in micros]
            + [last[m][0] for m in micros]
            + [attended[m][1] for m in micros]
            + [back[m][2] for m in micros]
            + [last[m][2] for m in micros]
            + [last[m][3] for m in micros],
            matmul * all_cols * 2,
            8e6,
            scratch=[pltpu.VMEM((width, all_cols), F32)],
        )
    else:
        grad_w = sum(
            jnp.concatenate([mm(tokens[m, 0], last[m][1], TN), mm(last[m][0], attended[m][1], TN)], axis=1) for m in micros
        )
        attn_blocks = [grad_w]
    part[-1] = tp_start(last[-1][4], mesh_tp)
    if ring:
        attn_up, attn_down = ring_sums(attn_blocks, order, more)
        attn_down.send()
        attn_up.send()
        f3u, f3d = ffn_up.absorb(attn_blocks[0]), ffn_down.absorb(attn_blocks[0])
        attn_up.absorb(f3u, part[0][1])
        attn_down.absorb(f3d)
        attn_up.send()
        attn_down.send()
        ffn_down.send()
        f4 = ffn_down.absorb()
        attn_up.absorb()
        attn_up.send()
        attn_down.absorb(f4)
        attn_down.send()
    out_tokens, in_grad, in_grads = None, None, []
    for m in micros:
        aliased = 0 if in_grad is None else 2
        out_tokens, in_grad = kernel_call(
            finish_body(aliased),
            "finish",
            [SMEM] + [VMEM] * 6 + [HBM] * aliased,
            [shape(tokens.shape, BF), shape(tokens.shape, F32)],
            [ids, finals[m], last[m][0], *tp_finish(part[m], mesh_tp, attn_blocks[0])] + ([out_tokens, in_grad] if aliased else []),
            1e8,
            5e6,
            out_specs=[micro_spec(tokens, m)] * 2,
            aliases={7: 0, 8: 1} if aliased else None,
            scratch=[full_sum],
        )
        in_grads.append(in_grad)

    if ring:
        attn_up.absorb(part[1][1], in_grads[0])
        attn_up.send()
        attn_down.absorb()
        pieces = [attn_blocks[0], attn_up.absorb(), attn_down.moving]
        grad_fi, grad_fo = kernel_call(
            unpack_ffn_body,
            "unpack_ffn",
            [VMEM] * 3,
            [shape(ffn_in.shape, F32)] * 2,
            [ffn_blocks[0], ffn_up.moving, ffn_down.moving],
            1e6,
            2e6,
        )
        grad_fo = grad_fo.T
        grads = kernel_call(
            unpack_attn_body,
            "unpack_attn",
            [VMEM] * 3,
            [
                shape(attn_in.shape, F32),
                shape(attn_in_bias.shape, F32),
                shape(attn_out.shape, F32),
                shape(out_biases.shape, F32),
                shape((1, block), F32),
                shape(norm_gains.shape, F32),
                shape(norm_shifts.shape, F32),
            ],
            [after(pieces[0], in_grad), *pieces[1:]],
            1e6,
            2e6,
        )
        grad_ai, grad_ab, grad_ao, grad_ob, grad_fb, grad_ng, grad_ns = grads
        grad_fb = grad_fb.reshape(block)
    else:
        attn_total = lax.psum_scatter(grad_w, "dp", scatter_dimension=0, tiled=True)
        sums = sum(back[m][2] + last[m][2] for m in micros)[:8].reshape(8, mesh_dp, block).transpose(1, 0, 2)
        bias = sum(last[m][3] for m in micros)[7].reshape(3, mesh_dp, head_bias)[0::2].transpose(1, 0, 2)
        bias = jnp.pad(bias.reshape(mesh_dp, 1, 2 * head_bias), ((0, 0), (7, 0), (0, block - 2 * head_bias)))
        small = lax.psum_scatter(sums + bias, "dp", scatter_dimension=0)
        grad_ai = attn_total[:, :qkv_width].reshape(block, 3, head_width).transpose(1, 0, 2)
        grad_ao = attn_total[:, qkv_width:].T
        grad_ab = small[7, : 2 * head_bias].reshape(2, head_bias)
        grad_ob, grad_ng, grad_ns, grad_fb = small[0:2], small[2:4], small[4:6], small[6]

    loss = sum(entropies) / (micro_count * mesh_dp)
    return out_tokens, in_grad, loss, grad_ai, grad_ab, grad_ao, grad_ob, grad_fi, grad_fb, grad_fo, grad_ng, grad_ns


def solution(mesh):
    placed = (
        P(None, "dp", None, None),
        P(None, "dp", None, None),
        P(None, "dp", None),
        P(None, "dp", "tp"),
        P(None, ("tp", "dp")),
        P("tp", "dp"),
        P(None, "dp"),
        P("dp", "tp"),
        P(("tp", "dp")),
        P("tp", "dp"),
        P(None, "dp"),
        P(None, "dp"),
    )
    sizes = (mesh.shape["tp"], mesh.shape["dp"])

    def run(*arrays):
        return on_device(*sizes, *arrays)

    return jax.shard_map(
        run,
        mesh=mesh,
        in_specs=placed,
        out_specs=placed[:2] + (P(),) + placed[3:],
        check_vma=False,
    )
```

```python
import math

import jax
import jax.numpy as jnp
from jax import lax
from jax.experimental import pallas as pl
from jax.experimental.pallas import tpu as pltpu
from jax.sharding import PartitionSpec as P

HEAD_DIM = 64
QLEN = 128
SOFTMAX_TEMP = 0.01
NEG_LARGE = -1e30
ROOT_HALF = 0.7071067811865476
DENSITY_NORM = 0.3989422804014327
VMEM_BYTES = 20 * 2**20
EXTRA = 16
BF = jnp.bfloat16
F32 = jnp.float32
NN = (((1,), (0,)), ((), ()))
NT = (((1,), (1,)), ((), ()))
TN = (((0,), (0,)), ((), ()))
HBM = pl.BlockSpec(memory_space=pl.ANY)
SMEM = pl.BlockSpec(memory_space=pltpu.SMEM)
VMEM = pl.BlockSpec(memory_space=pltpu.VMEM)


def mm(left, right, dims=NN, precision=None):
    return lax.dot_general(left, right, dims, precision=precision, preferred_element_type=F32)


def shape(dims, dtype):
    return jax.ShapeDtypeStruct(dims, dtype)


def kernel_call(body, name, in_specs, outs, args, flops, moved, scratch=(), out_specs=None, aliases=None):
    return pl.pallas_call(
        body,
        name=name,
        grid=(1,) if out_specs is not None else (),
        in_specs=in_specs,
        out_specs=out_specs if out_specs is not None else [VMEM] * len(outs),
        out_shape=outs,
        scratch_shapes=scratch,
        input_output_aliases=aliases or {},
        compiler_params=pltpu.CompilerParams(vmem_limit_bytes=VMEM_BYTES),
        cost_estimate=pl.CostEstimate(flops=int(flops), bytes_accessed=int(moved), transcendentals=0),
    )(*args)


def micro_spec(arr, micro):
    return pl.BlockSpec((1,) + arr.shape[1:], lambda i: (micro,) + (0,) * (len(arr.shape) - 1))


def ring_owner(at, step, count):
    half = count // 2
    place = jnp.where(at % 2 == 0, at // 2, half + (count - 1 - at) // 2)
    place = (place + step) % count
    return jnp.where(place < half, 2 * place, count - 1 - 2 * (place - half))


def pack_attn_body(head_bias):
    def body(ai_ref, ao_ref, small_ref, out_ref):
        block, head_width = ai_ref.shape[1], ai_ref.shape[2]
        for j in range(3):
            out_ref[:block, j * head_width : (j + 1) * head_width] = ai_ref[j]
        out_ref[:block, 3 * head_width :] = ao_ref[...].T
        out_ref[block:, :] = jnp.zeros((out_ref.shape[0] - block, out_ref.shape[1]), BF)
        out_ref[block:, :block] = small_ref[...]
        out_ref[block + 7 : block + 8, head_bias : 2 * head_bias] = small_ref[8:9, :head_bias]

    return body


def pack_ffn_body(fi_ref, fo_ref, tokens_ref, out_ref):
    block = fi_ref.shape[0]
    out_ref[:block, :] = fi_ref[...]
    out_ref[block:, :] = fo_ref[...]


def assemble_body(block_rows, head_bias, count, steps, first):
    def body(ids_ref, *refs):
        blocks, (w_ref, vec_ref, bias_ref, out_ref) = refs[: len(steps)], refs[-4:]
        width = w_ref.shape[1]
        qkv_width = bias_ref.shape[1]
        vectors, biases = jnp.zeros(vec_ref.shape, F32), jnp.zeros(bias_ref.shape, F32)
        if not first:
            vectors, biases = refs[len(steps) + 1][...], refs[len(steps) + 2][...]
        lane = lax.broadcasted_iota(jnp.int32, (128, width), 0)
        place = lax.broadcasted_iota(jnp.int32, (128, width), 1)
        for block, k in zip(blocks, steps):
            owner = ring_owner(ids_ref[1], k, count)
            at = pl.ds(pl.multiple_of(owner * block_rows, 16), block_rows)
            w_ref[at, :] = block[:block_rows, :]
            out_ref[at, :] = block[:block_rows, qkv_width:]
            small = block[block_rows : block_rows + EXTRA, :128]
            pick = (place == owner * block_rows + lane) & (lane < block_rows)
            vectors += mm(small, jnp.where(pick, 1.0, 0.0).astype(BF))
            biases += mm(small, bias_pick(owner, head_bias, qkv_width, lane, place))
        vec_ref[...] = vectors
        bias_ref[...] = biases

    return body


def assemble_pair_body(block_rows, count):
    def body(ids_ref, *refs):
        blocks, (fi_ref, fo_ref) = refs[:count], refs[count:]
        for k in range(count):
            owner = ring_owner(ids_ref[1], k, count)
            at = pl.ds(pl.multiple_of(owner * block_rows, 16), block_rows)
            fi_ref[at, :] = blocks[k][:block_rows, :]
            fo_ref[at, :] = blocks[k][block_rows:, :]

    return body


def bias_pick(owner, head_bias, qkv_width, lane, place):
    lane, place = lane[:, :qkv_width], place[:, :qkv_width]
    values_at = qkv_width * 2 // 3
    for_query = (lane < head_bias) & (place == owner * head_bias + lane)
    for_value = (
        (lane >= head_bias)
        & (lane < 2 * head_bias)
        & (place == values_at + owner * head_bias + lane - head_bias)
    )
    return jnp.where(for_query | for_value, 1.0, 0.0).astype(BF)


def split_halves(full_ref, core, send_a, send_b, keep_ref):
    half, piece = keep_ref.shape[0], send_a.shape[0]
    keep_ref[...] = full_ref[pl.ds(pl.multiple_of(core * half, 16), half), :]
    for k, ref in enumerate((send_a, send_b)):
        ref[...] = full_ref[pl.ds(pl.multiple_of((1 - core) * half + k * piece, 16), piece), :]


def halves(core, half):
    return [pl.ds(pl.multiple_of(place * half, 16), half) for place in (1 - core, core)]


def send_halves(make, core, send_a, send_b, keep_ref):
    half, piece = keep_ref.shape[0], send_a.shape[0]
    away, here = halves(core, half)
    value = make(away).astype(BF)
    send_a[...] = value[:piece]
    send_b[...] = value[piece:]
    keep_ref[...] = make(here).astype(BF)


def half_body(keep_ref, a_ref, b_ref, out_ref):
    piece = a_ref.shape[0]
    for k, ref in enumerate((a_ref, b_ref)):
        part = slice(k * piece, (k + 1) * piece)
        out_ref[part, :] = add_low(keep_ref[part, :], ref[...])


def join_halves(full_ref, core, parts):
    half = parts[0].shape[0]
    for near, far, place in ((parts[0], parts[1], core), (parts[2], parts[3], 1 - core)):
        full_ref[pl.ds(pl.multiple_of(place * half, 16), half), :] = near[...].astype(F32) + far[...].astype(F32)


def over_sum(core, parts, step):
    half = parts[0].shape[0]
    piece = half // 2
    for near, far, place in ((parts[0], parts[1], core), (parts[2], parts[3], 1 - core)):

        def one(k, carry, near=near, far=far, place=place):
            at = pl.ds(pl.multiple_of(k * piece, 16), piece)
            start = pl.multiple_of(place * half + k * piece, 16)
            step(pl.ds(start, piece), start, near[at, :].astype(F32) + far[at, :].astype(F32))
            return carry

        lax.fori_loop(0, 2, one, 0)


def segment_masks(start, dims, lengths):
    row = lax.broadcasted_iota(jnp.int32, dims, 0) + start
    return row < QLEN, (row < QLEN) & (row < lengths[0]), (row >= QLEN) & (row - QLEN < lengths[1])


def segments(rows):
    return ((0, QLEN), (QLEN, rows))


def attend_body():
    def body(ids_ref, len_ref, x_ref, w_ref, bias_ref, qkv_ref, mixed_ref, pq_ref, pp_ref):
        micro = ids_ref[2]
        rows = x_ref.shape[2]
        heads = pq_ref.shape[0]
        width = heads * HEAD_DIM
        x = x_ref[micro, 0]
        bias = bias_ref[7:8, :]
        qkv_ref[...] = (mm(x, w_ref[:, : 3 * width]) + bias).astype(BF)
        factor = 1.0 / math.sqrt(HEAD_DIM)
        for seg, (low, high) in enumerate(segments(rows)):
            length = len_ref[micro, 0, seg]
            size = high - low
            p_ref = pp_ref if seg else pq_ref
            visible = lax.broadcasted_iota(jnp.int32, (size, size), 0) < length
            for h in range(heads):
                at = h * HEAD_DIM
                queries = qkv_ref[low:high, at : at + HEAD_DIM]
                keys_low = qkv_ref[low:high, width + at : width + at + HEAD_DIM]
                values = qkv_ref[low:high, 2 * width + at : 2 * width + at + HEAD_DIM]
                scores = jnp.where(visible, mm(keys_low, queries, NT) * factor, NEG_LARGE)
                raised = jnp.exp(scores - jnp.max(scores, axis=0, keepdims=True))
                weights = (raised * (1.0 / jnp.sum(raised, axis=0, keepdims=True))).astype(BF)
                p_ref[h] = weights
                mixed_ref[low:high, at : at + HEAD_DIM] = mm(values, weights, TN).T.astype(BF)

    return body


def norm_one(x, branch, shift_out):
    hidden = x.astype(F32) + (branch.astype(F32) + shift_out)
    center = hidden - jnp.mean(hidden, axis=-1, keepdims=True)
    inverse = lax.rsqrt(jnp.mean(center * center, axis=-1, keepdims=True) + 1e-12)
    return center * inverse, inverse


def place_heads(own, parts, full_ref):
    for at in range(len(parts)):

        @pl.when(own == at)
        def _():
            for k, ref in enumerate(parts):
                width = ref.shape[1]
                full_ref[:, (at ^ k) * width : ((at ^ k) + 1) * width] = ref[...]


def gather_out_body(ids_ref, s0, s1, s2, s3, out_ref):
    place_heads(ids_ref[3], (s0, s1, s2, s3), out_ref)


def gelu_parts(inner):
    cumulative = 0.5 * (1.0 + lax.erf(inner * ROOT_HALF))
    density = jnp.exp(-0.5 * inner * inner) * DENSITY_NORM
    return (inner * cumulative).astype(BF), (cumulative + inner * density).astype(BF)


def ffn_body():
    def body(
        ids_ref, x_ref, s0, s1, s2, s3, out_ref, vec_ref, fi_ref, fo_ref,
        normed_ref, inv_ref, first_ref, low_ref, hidden_ref, slope_ref, send_a, send_b, keep_ref, mixed_ref,
    ):
        micro, core = ids_ref[2], ids_ref[0]
        half, piece = keep_ref.shape[0], send_a.shape[0]
        place_heads(ids_ref[3], (s0, s1, s2, s3), mixed_ref)
        for part, away in zip(halves(core, half), (True, False)):
            branch = mm(mixed_ref[part, :], out_ref[...], NT)
            normed, inverse = norm_one(x_ref[micro, 0, part, :], branch, vec_ref[0:1, :])
            normed_ref[part, :] = normed.astype(BF)
            inv_ref[part, :] = inverse
            first = normed * vec_ref[2:3, :] + vec_ref[4:5, :]
            first_ref[part, :] = first
            low = first.astype(BF)
            low_ref[part, :] = low
            hidden, slope = gelu_parts(mm(low, fi_ref[...]) + vec_ref[6:7, :])
            hidden_ref[part, :] = hidden
            slope_ref[part, :] = slope
            second = mm(hidden, fo_ref[...], NT).astype(BF)
            if away:
                send_a[...] = second[:piece]
                send_b[...] = second[piece:]
            else:
                keep_ref[...] = second

    return body


def pool_body():
    def body(
        ids_ref, len_ref, first_ref, s0, s1, s2, s3, vec_ref, out_ref, normed_ref, inv_ref, pooled_ref, emb_ref
    ):
        micro = ids_ref[2]
        pooled_ref[...] = jnp.zeros(pooled_ref.shape, F32)
        lengths = [len_ref[micro, 0, seg] for seg in range(2)]

        def step(part, start, second):
            hidden = first_ref[part, :] + (second + vec_ref[1:2, :])
            center = hidden - jnp.mean(hidden, axis=-1, keepdims=True)
            inverse = lax.rsqrt(jnp.mean(center * center, axis=-1, keepdims=True) + 1e-12)
            normed = center * inverse
            normed_ref[part, :] = normed.astype(BF)
            inv_ref[part, :] = inverse
            final = normed * vec_ref[3:4, :] + vec_ref[5:6, :]
            out_ref[part, :] = final.astype(BF)
            masks = segment_masks(start, (final.shape[0], 1), lengths)
            for seg in range(2):
                kept = jnp.where(masks[seg + 1], final, 0.0)
                pooled_ref[seg : seg + 1, :] += jnp.sum(kept, axis=0, keepdims=True)

        over_sum(ids_ref[0], (s0, s1, s2, s3), step)
        for seg in range(2):
            summed = pooled_ref[seg : seg + 1, :] / len_ref[micro, 0, seg].astype(F32)
            unit = summed * lax.rsqrt(jnp.sum(summed * summed, axis=-1, keepdims=True) + 1e-06)
            pooled_ref[seg : seg + 1, :] = summed
            emb_ref[0, seg : seg + 1, :] = unit

    return body


def loss_grads(queries, passages, own):
    highest = lax.Precision.HIGHEST
    count = queries.shape[0]
    row = lax.broadcasted_iota(jnp.int32, (count, count), 0)
    col = lax.broadcasted_iota(jnp.int32, (count, count), 1)
    same = jnp.where(row == col, 1.0, 0.0)
    logits = mm(queries, passages, NT, highest) / SOFTMAX_TEMP
    top = jnp.max(logits, axis=-1, keepdims=True)
    log_norm = top + jnp.log(jnp.sum(jnp.exp(logits - top), axis=-1, keepdims=True))
    entropy = jnp.sum(jnp.sum(same * (log_norm - logits), axis=-1, keepdims=True), axis=0, keepdims=True)
    grad = (jnp.exp(logits - log_norm) - same) / SOFTMAX_TEMP
    turned = mm(passages, queries, NT, highest) / SOFTMAX_TEMP
    top_t = jnp.max(turned, axis=0, keepdims=True)
    norm_t = top_t + jnp.log(jnp.sum(jnp.exp(turned - top_t), axis=0, keepdims=True))
    grad_t = (jnp.exp(turned - norm_t) - same) / SOFTMAX_TEMP
    own_col = jnp.sum(jnp.where(col == own, grad, 0.0), axis=1, keepdims=True)
    own_row = jnp.sum(jnp.where(col == own, grad_t, 0.0), axis=1, keepdims=True)
    grad_query = jnp.sum(own_row * passages, axis=0, keepdims=True)
    grad_passage = jnp.sum(own_col * queries, axis=0, keepdims=True)
    return entropy, (grad_query, grad_passage)


def norm_backward(upstream, normed, inverse, gain):
    scaled = upstream * gain
    centered = scaled - jnp.mean(scaled, axis=-1, keepdims=True)
    return inverse * (centered - normed * jnp.mean(scaled * normed, axis=-1, keepdims=True))


def loss_body(*refs):
    ids_ref, len_ref, pooled_ref = refs[:3]
    pieces, (spread_ref, loss_ref, emb_ref) = refs[3:-3], refs[-3:]
    place = 0
    for piece in pieces:
        for k in range(piece.shape[0]):
            emb_ref[ids_ref[1] ^ place] = piece[k]
            place += 1
    entropy, unit_grads = loss_grads(emb_ref[:, 0, :], emb_ref[:, 1, :], ids_ref[1])
    loss_ref[...] = jnp.broadcast_to(entropy, loss_ref.shape)
    for seg in range(2):
        summed = pooled_ref[seg : seg + 1, :]
        up = unit_grads[seg]
        inverse = lax.rsqrt(jnp.sum(summed * summed, axis=-1, keepdims=True) + 1e-06)
        cubed = inverse * inverse * inverse
        grad = inverse * up - cubed * summed * jnp.sum(summed * up, axis=-1, keepdims=True)
        spread_ref[seg : seg + 1, :] = grad / len_ref[ids_ref[2], 0, seg].astype(F32)


def ffn_back_body():
    def body(
        ids_ref, len_ref, spread_ref, cot_ref, normed_ref, inv_ref, slope_ref, vec_ref, fi_ref, fo_ref,
        second_ref, inner_ref, sums_ref, send_a, send_b, keep_ref, part_ref,
    ):
        micro = ids_ref[2]
        rows = normed_ref.shape[0]
        zero = jnp.zeros((1, normed_ref.shape[1]), F32)

        def step(k, sums):
            part = pl.ds(pl.multiple_of(k * QLEN, QLEN), QLEN)
            seg = jnp.minimum(k, 1)
            cot = cot_ref[micro, 0, part, :].astype(F32) + spread_ref[pl.ds(seg, 1), :]
            place = lax.broadcasted_iota(jnp.int32, cot.shape, 0) + (k - seg) * QLEN
            grad_final = jnp.where(place < len_ref[micro, 0, seg], cot, 0.0)
            normed = normed_ref[part, :].astype(F32)
            low = norm_backward(grad_final, normed, inv_ref[part, :], vec_ref[3:4, :]).astype(BF)
            second_ref[part, :] = low
            terms = (grad_final * normed, grad_final, low.astype(F32))
            return tuple(total + jnp.sum(term, axis=0, keepdims=True) for total, term in zip(sums, terms))

        gain_sum, shift_sum, bias_sum = lax.fori_loop(0, rows // QLEN, step, (zero, zero, zero))
        grad_hidden = mm(second_ref[...], fo_ref[...])
        grad_inner = (grad_hidden * slope_ref[...].astype(F32)).astype(BF)
        inner_ref[...] = grad_inner
        inner_sum = jnp.sum(grad_inner.astype(F32), axis=0, keepdims=True)
        part_ref[...] = mm(inner_ref[...], fi_ref[...], NT).astype(BF)
        split_halves(part_ref, ids_ref[0], send_a, send_b, keep_ref)
        sums_ref[...] = jnp.zeros(sums_ref.shape, F32)
        sums_ref[1:2, :] = bias_sum
        sums_ref[3:4, :] = gain_sum
        sums_ref[5:6, :] = shift_sum
        sums_ref[6:7, :] = inner_sum

    return body


def attend_back_body():
    def body(
        ids_ref, normed_ref, inv_ref, s0, s1, s2, s3, second_ref, qkv_ref, mixed_ref, pq_ref, pp_ref, vec_ref, w_ref,
        branch_ref, gqkv_ref, sums_ref, bias_ref, send_a, send_b, keep_ref, sum_ref, gm_ref, part_ref,
    ):
        rows = normed_ref.shape[0]
        heads = pq_ref.shape[0]
        width = heads * HEAD_DIM
        core = ids_ref[0]
        join_halves(sum_ref, core, (s0, s1, s2, s3))
        zero = jnp.zeros((1, normed_ref.shape[1]), F32)

        def step(k, sums):
            part = pl.ds(pl.multiple_of(k * QLEN, QLEN), QLEN)
            normed = normed_ref[part, :].astype(F32)
            upstream = sum_ref[part, :] + second_ref[part, :].astype(F32)
            low = norm_backward(upstream, normed, inv_ref[part, :], vec_ref[2:3, :]).astype(BF)
            branch_ref[part, :] = low
            terms = (upstream * normed, upstream, low.astype(F32))
            return tuple(total + jnp.sum(term, axis=0, keepdims=True) for total, term in zip(sums, terms))

        gain_sum, shift_sum, out_sum = lax.fori_loop(0, rows // QLEN, step, (zero, zero, zero))
        sums_ref[...] = jnp.zeros(sums_ref.shape, F32)
        sums_ref[0:1, :] = out_sum
        sums_ref[2:3, :] = gain_sum
        sums_ref[4:5, :] = shift_sum
        gm_ref[...] = mm(branch_ref[...], w_ref[:, 3 * width :]).astype(BF)
        factor = 1.0 / math.sqrt(HEAD_DIM)
        for seg, (low_row, high_row) in enumerate(segments(rows)):
            part = slice(low_row, high_row)
            p_ref = pp_ref if seg else pq_ref
            for h in range(heads):
                at = h * HEAD_DIM
                columns = [slice(j * width + at, j * width + at + HEAD_DIM) for j in range(3)]
                grad = gm_ref[part, columns[0]]
                weights = p_ref[h]
                grad_weights = mm(qkv_ref[part, columns[2]], grad, NT)
                low_weights = weights.astype(F32)
                delta = jnp.sum(low_weights * grad_weights, axis=0, keepdims=True)
                grad_scores = (low_weights * (grad_weights - delta)).astype(BF)
                gqkv_ref[part, columns[0]] = (mm(qkv_ref[part, columns[1]], grad_scores, TN) * factor).T.astype(BF)
                gqkv_ref[part, columns[1]] = (mm(grad_scores, qkv_ref[part, columns[0]]) * factor).astype(BF)
                gqkv_ref[part, columns[2]] = mm(weights, grad).astype(BF)
        gqkv = gqkv_ref[...]
        bias_ref[...] = jnp.zeros(bias_ref.shape, F32)
        bias_ref[7:8, :] = jnp.sum(gqkv.astype(F32), axis=0, keepdims=True)
        part_ref[...] = mm(gqkv, w_ref[:, : 3 * width], NT).astype(BF)
        split_halves(part_ref, core, send_a, send_b, keep_ref)

    return body


def ffn_weight_body(block_rows, count):
    def body(ids_ref, low_a, low_b, gi_a, gi_b, hid_a, hid_b, gs_a, gs_b, *refs):
        outs, (fi_ref, fo_ref) = refs[:-2], refs[-2:]
        fi_ref[...] = mm(low_a[...], gi_a[...], TN) + mm(low_b[...], gi_b[...], TN)
        fo_ref[...] = mm(gs_a[...], hid_a[...], TN) + mm(gs_b[...], hid_b[...], TN)
        for k in range(count):
            at = pl.ds(pl.multiple_of(ring_owner(ids_ref[1], k, count) * block_rows, 16), block_rows)
            outs[k][:block_rows, :] = fi_ref[at, :].astype(BF)
            outs[k][block_rows:, :] = fo_ref[at, :].astype(BF)

    return body


def attend_weight_body(block_rows, head_bias, count):
    def body(
        ids_ref, x_ref, gq_a, gq_b, gb_a, gb_b, mx_a, mx_b, s4_a, s4_b, s5_a, s5_b, b_a, b_b, *refs
    ):
        outs, w_ref = refs[:-1], refs[-1]
        qkv = gq_a.shape[1]
        width = w_ref.shape[0]
        w_ref[:, :qkv] = mm(x_ref[0, 0], gq_a[...], TN) + mm(x_ref[1, 0], gq_b[...], TN)
        w_ref[:, qkv:] = mm(gb_a[...], mx_a[...], TN) + mm(gb_b[...], mx_b[...], TN)
        sums = (s4_a[...] + s4_b[...] + s5_a[...] + s5_b[...]).astype(BF)
        biases = (b_a[...] + b_b[...]).astype(BF)
        lane = lax.broadcasted_iota(jnp.int32, (128, width), 0)
        place = lax.broadcasted_iota(jnp.int32, (128, width), 1)
        for k in range(count):
            owner = ring_owner(ids_ref[1], k, count)
            outs[k][:block_rows, :] = w_ref[pl.ds(pl.multiple_of(owner * block_rows, 16), block_rows), :].astype(BF)
            outs[k][block_rows:, 128:] = jnp.zeros((EXTRA, width - 128), BF)
            pick = (place == owner * block_rows + lane) & (lane < block_rows)
            small = mm(sums, jnp.where(pick, 1.0, 0.0).astype(BF), NT)
            small += mm(biases, bias_pick(owner, head_bias, qkv, lane, place), NT)
            outs[k][block_rows:, :128] = small.astype(BF)

    return body


def unpack_attn_body(own_ref, up_ref, down_ref, ai_ref, ab_ref, ao_ref, ob_ref, fb_ref, ng_ref, ns_ref):
    block, head_width = ai_ref.shape[1], ai_ref.shape[2]
    head_bias = ab_ref.shape[1]
    total = own_ref[...].astype(F32) + up_ref[...].astype(F32) + down_ref[...].astype(F32)
    for j in range(3):
        ai_ref[j] = total[:block, j * head_width : (j + 1) * head_width]
    ao_ref[...] = total[:block, 3 * head_width :].T
    small = total[block : block + 8, :128]
    ob_ref[...] = small[0:2, :block]
    ng_ref[...] = small[2:4, :block]
    ns_ref[...] = small[4:6, :block]
    fb_ref[...] = small[6:7, :block]
    for j in range(2):
        ab_ref[j : j + 1, :] = small[7:8, j * head_bias : (j + 1) * head_bias]


def unpack_ffn_body(own_ref, up_ref, down_ref, fi_ref, fo_ref):
    block = fi_ref.shape[0]
    for part, out_ref in ((slice(0, block), fi_ref), (slice(block, 2 * block), fo_ref)):
        out_ref[...] = own_ref[part, :].astype(F32) + up_ref[part, :].astype(F32) + down_ref[part, :].astype(F32)


def write_sum(core, parts, gh_ref, out_ref):
    for near, far, place in ((parts[0], parts[1], core), (parts[2], parts[3], 1 - core)):
        half = near.shape[0]
        at = pl.ds(pl.multiple_of(place * half, 16), half)
        out_ref[0, 0, at, :] = near[...].astype(F32) + far[...].astype(F32) + gh_ref[at, :].astype(F32)


def finish_body(ids_ref, final_a, final_b, gh_ref, s0, s1, s2, s3, tokens_ref, out_ref):
    for micro, ref in enumerate((final_a, final_b)):
        tokens_ref[micro, 0] = ref[...]
    write_sum(ids_ref[0], (s0, s1, s2, s3), gh_ref, out_ref)


def finish_last_body(ids_ref, gh_ref, s0, s1, s2, s3, _, out_ref):
    write_sum(ids_ref[0], (s0, s1, s2, s3), gh_ref, out_ref)


def core_swap(value, count):
    return lax.ppermute(value, "tp", [(i, i ^ 1) for i in range(count)])


def chip_swap(value, count):
    return lax.ppermute(value, "tp", [(i, i ^ 2) for i in range(count)])


def add_low(left, right):
    return (left.astype(F32) + right.astype(F32)).astype(BF)


def tp_start(parts, count, ready=()):
    send_a, send_b, keep = parts
    send_a = after(send_a, *ready)
    got = [core_swap(send_a, count), core_swap(send_b, count)]
    near = kernel_call(half_body, "half", [VMEM] * 3, [shape(keep.shape, BF)], [keep, *got], 5e5, 2e6)[0]
    return near, chip_swap(near, count), core_swap(near, count)


def tp_finish(started, count, *later):
    near, far, near_other = started
    return near, far, near_other, core_swap(after(far, *later), count)


def pair_gather(value, count):
    pieces, step = [value], 1
    while step < count:
        send = pieces[0] if step == 1 else jnp.concatenate(pieces)
        pieces.append(lax.ppermute(send, "dp", [(i, i ^ step) for i in range(count)]))
        step *= 2
    return pieces


def after(ids, *values):
    return lax.optimization_barrier((ids, *values))[0]


def ring_order(count):
    return list(range(0, count, 2)) + list(range(count - 1, 0, -2))


def ring_step(value, order, step):
    count = len(order)
    return lax.ppermute(value, "dp", [(order[i], order[(i + step) % count]) for i in range(count)])


class RingSum:
    def __init__(self, parts, order, way):
        self.parts, self.order, self.way = parts, order, way
        self.moving, self.at = parts[0], 1

    def send(self, *ready):
        self.moving = ring_step(after(self.moving, *ready), self.order, self.way)

    def absorb(self, *ready):
        self.moving = after(self.moving, *ready)
        if self.at < len(self.parts):
            self.moving = add_low(self.moving, self.parts[self.at])
        self.at += 1
        return self.moving


def ring_sums(blocks, order, up):
    return RingSum(blocks[up:0:-1], order, 1), RingSum(blocks[up + 1 :], order, -1)


def on_device(mesh_tp, mesh_dp, *arrays):
    tokens, out_grad, lengths, attn_in, attn_in_bias, attn_out, out_biases, ffn_in, ffn_in_bias, ffn_out, norm_gains, norm_shifts = arrays
    micro_count, _, rows, width = tokens.shape
    block = attn_in.shape[1]
    inner_width = ffn_in.shape[1]
    head_width = attn_in.shape[2]
    heads = head_width // HEAD_DIM
    qkv_width = 3 * head_width
    head_bias = attn_in_bias.shape[1]
    half = rows // 2
    ring = block % 16 == 0
    order = ring_order(mesh_dp)
    all_cols = qkv_width + head_width
    matmul = 2.0 * rows * width
    micros = range(micro_count)
    tp_at = lax.axis_index("tp")
    ids_of = [jnp.stack([tp_at % 2, lax.axis_index("dp"), m, tp_at]).astype(jnp.int32) for m in micros]
    ids = ids_of[0]
    attn_in, out_biases = after(attn_in, *ids_of), after(out_biases, *ids_of)

    vec_shape, bias_shape = shape((EXTRA, width), F32), shape((EXTRA, qkv_width), F32)
    full_weight = shape((width, inner_width), BF)
    last_row = jnp.pad(attn_in_bias.reshape(1, 2 * head_bias), ((0, 0), (0, block - 2 * head_bias)))
    if ring:
        bias_rows = jnp.pad(attn_in_bias, ((0, 0), (0, block - head_bias)))
        small = jnp.concatenate(
            [out_biases, norm_gains, norm_shifts, ffn_in_bias[None], bias_rows, jnp.zeros((EXTRA - 9, block), BF)]
        )
        attn_block = kernel_call(
            pack_attn_body(head_bias), "pack_attn", [VMEM] * 3, [shape((block + EXTRA, all_cols), BF)], [attn_in, attn_out, small], 1e6, 1e6
        )[0]
        ffn_block = kernel_call(
            pack_ffn_body,
            "pack_ffn",
            [VMEM] * 3,
            [shape((2 * block, inner_width), BF)],
            [ffn_in, ffn_out.T, tokens],
            1e6,
            1e6,
        )[0]
        more, less = mesh_dp // 2, mesh_dp - 1 - mesh_dp // 2

        def assemble(blocks, steps, held=()):
            return kernel_call(
                assemble_body(block, head_bias, mesh_dp, steps, not held),
                "assemble",
                [SMEM] + [VMEM] * (len(blocks) + len(held)),
                [shape((width, all_cols), BF), vec_shape, bias_shape, shape((width, head_width), BF)],
                [ids, *blocks, *held],
                1e8,
                3e6,
                aliases={1 + len(blocks): 0, 4 + len(blocks): 3} if held else None,
            )

        ups, downs = [attn_block], [attn_block]
        weights = ()
        for step in range(more):
            if step == more - 1:
                steps = [0, *range(1, less), *range(mesh_dp - less + 1, mesh_dp)]
                weights = assemble([attn_block, *downs[1:less], *ups[less - 1 : 0 : -1]], steps)
            ups.append(ring_step(ups[-1], order, 1))
            if step < less:
                downs.append(ring_step(downs[-1], order, -1))
        w_attn, vec, qkv_bias, w_out = assemble([downs[less], *ups[: less - 1 : -1]], [less, *range(less + 1, mesh_dp - less + 1)], weights)
        ffn_ups, ffn_downs = [after(ffn_block, ups[-1])], [after(ffn_block, downs[-1])]
        ffn_downs.append(ring_step(ffn_downs[-1], order, -1))
        ffn_downs.append(ring_step(ffn_downs[-1], order, -1))
        ffn_ups.append(ring_step(ffn_ups[-1], order, 1))
    else:
        attn_rows = jnp.concatenate([attn_in.transpose(1, 0, 2).reshape(block, qkv_width), attn_out.T], axis=1)
        vectors = jnp.concatenate([out_biases, norm_gains, norm_shifts, ffn_in_bias[None], last_row])
        w_attn = lax.all_gather(attn_rows, "dp", axis=0, tiled=True)
        every = lax.all_gather(vectors, "dp", axis=0).astype(F32)
        vec = jnp.pad(every.transpose(1, 0, 2).reshape(8, width), ((0, EXTRA - 8), (0, 0)))
        pair = every[:, 7, : 2 * head_bias].reshape(mesh_dp, 2, head_bias).transpose(1, 0, 2).reshape(2, head_width)
        both = jnp.concatenate([pair[0], jnp.zeros((head_width,), F32), pair[1]])
        qkv_bias = jnp.pad(both[None], ((7, EXTRA - 8), (0, 0)))
        w_out = w_attn[:, qkv_width:]
        w_fi = lax.all_gather(ffn_in, "dp", axis=0, tiled=True)
        w_fo = lax.all_gather(ffn_out.T, "dp", axis=0, tiled=True)

    part_out = [shape((half // 2, width), BF)] * 2 + [shape((half, width), BF)]
    full_low = pltpu.VMEM((rows, width), BF)
    full_sum = pltpu.VMEM((rows, width), F32)

    far_out = chip_swap(w_out, mesh_tp)
    attended, far_heads, part = [], [], [None] * micro_count
    done, waiting = [], []
    for m in micros:
        qkv, mixed, p_query, p_passage = kernel_call(
            attend_body(),
            "attend",
            [SMEM, SMEM, VMEM, VMEM, VMEM],
            [
                shape((rows, qkv_width), BF),
                shape((rows, head_width), BF),
                shape((heads, QLEN, QLEN), BF),
                shape((heads, rows - QLEN, rows - QLEN), BF),
            ],
            [after(ids_of[m], *done), lengths, tokens, w_attn, qkv_bias],
            matmul * all_cols * 4,
            6e6,
        )
        attended.append((qkv, mixed, p_query, p_passage))
        done = [mixed]
        if ring:
            if len(ffn_ups) <= less:
                ffn_ups.append(ring_step(after(ffn_ups[-1], qkv), order, 1))
            if len(ffn_downs) <= more:
                ffn_downs.append(ring_step(after(ffn_downs[-1], qkv), order, -1))
        far_heads.append(chip_swap(after(mixed, *waiting), mesh_tp))
        waiting = []
    out_full = kernel_call(
        gather_out_body,
        "gather_out",
        [SMEM] + [VMEM] * 4,
        [shape((width, mesh_tp * head_width), BF)],
        [ids, w_out, core_swap(w_out, mesh_tp), far_out, core_swap(far_out, mesh_tp)],
        1e6,
        3e6,
    )[0]
    done = []

    if ring:
        while len(ffn_ups) <= less:
            ffn_ups.append(ring_step(ffn_ups[-1], order, 1))
        while len(ffn_downs) <= more:
            ffn_downs.append(ring_step(ffn_downs[-1], order, -1))
        w_fi, w_fo = kernel_call(
            assemble_pair_body(block, mesh_dp),
            "assemble_ffn",
            [SMEM] + [VMEM] * mesh_dp,
            [full_weight, full_weight],
            [ids, ffn_block, *ffn_downs[1:], *ffn_ups[:0:-1]],
            1e6,
            5e6,
        )

    fed = []
    for m in micros:
        ready = [part[0][0]] if m else []
        branch = [attended[m][1], core_swap(attended[m][1], mesh_tp), far_heads[m], core_swap(after(far_heads[m], *ready), mesh_tp)]
        normed, inverse, first, first_low, hidden, slope, *sends = kernel_call(
            ffn_body(),
            "ffn",
            [SMEM] + [VMEM] * 9,
            [
                shape((rows, width), BF),
                shape((rows, 1), F32),
                shape((rows, width), F32),
                shape((rows, width), BF),
                shape((rows, inner_width), BF),
                shape((rows, inner_width), BF),
            ]
            + part_out,
            [after(ids_of[m], *done), tokens, *branch, out_full, vec, w_fi, w_fo],
            matmul * (inner_width * 2 + width),
            9e6,
            scratch=[pltpu.VMEM((rows, mesh_tp * head_width), BF)],
        )
        fed.append((first, first_low, hidden, slope, normed, inverse))
        part[m] = tp_start(sends, mesh_tp, [far_heads[m + 1]] if m + 1 < micro_count else [])
        before = part[m][0]
        done = [part[m][0]]

    finals = []
    pooled = []
    for m in micros:
        second = tp_finish(part[m], mesh_tp, before)
        final_low, normed, inverse, sums, emb = kernel_call(
            pool_body(),
            "pool",
            [SMEM, SMEM] + [VMEM] * 6,
            [
                shape((rows, width), BF),
                shape((rows, width), BF),
                shape((rows, 1), F32),
                shape((8, width), F32),
                shape((1, 2, width), F32),
            ],
            [after(ids_of[m], *done), lengths, fed[m][0], *second, vec],
            2e8,
            6e6,
        )
        finals.append(final_low)
        done = [sums]
        gathered = pair_gather(emb, mesh_dp)
        before = gathered[min(2, len(gathered) - 1)]
        pooled.append((normed, inverse, sums, gathered))

    back, entropies = [], []
    for m in micros:
        normed, inverse, sums, gathered = pooled[m]
        spread, entropy = kernel_call(
            loss_body,
            "loss",
            [SMEM, SMEM] + [VMEM] * (1 + len(gathered)),
            [shape((8, width), F32), shape((8, 128), F32)],
            [after(ids_of[m], pooled[-1][2]), lengths, sums, *gathered],
            1e6,
            1e5,
            scratch=[pltpu.VMEM((mesh_dp, 2, width), F32)],
        )
        grad_second, grad_inner, sums4, *sends = kernel_call(
            ffn_back_body(),
            "ffn_back",
            [SMEM, SMEM] + [VMEM] * 8,
            [
                shape((rows, width), BF),
                shape((rows, inner_width), BF),
                shape((EXTRA, width), F32),
            ]
            + part_out,
            [after(ids_of[m], *done), lengths, spread, out_grad, normed, inverse, fed[m][3], vec, w_fi, w_fo],
            matmul * inner_width * 3,
            10e6,
            scratch=[full_low],
        )
        back.append((grad_second, grad_inner, sums4))
        entropies.append(entropy[0, 0])
        part[m] = tp_start(sends, mesh_tp, [pooled[m + 1][3][1]] if m + 1 < micro_count else ())
        before = part[m][0]
        done = [part[m][0]]

    grad_first = [tp_finish(part[0], mesh_tp, before)]
    if ring:
        ffn_blocks = kernel_call(
            ffn_weight_body(block, mesh_dp),
            "ffn_weights",
            [SMEM] + [VMEM] * 8,
            [shape((2 * block, width), BF)] * mesh_dp,
            [after(ids, *done, grad_first[0][3])] + [fed[m][1] for m in micros] + [back[m][1] for m in micros] + [fed[m][2] for m in micros] + [back[m][0] for m in micros],
            matmul * inner_width * 4,
            14e6,
            scratch=[pltpu.VMEM((width, inner_width), F32)] * 2,
        )
        done = [ffn_blocks[0]]
        ffn_up, ffn_down = ring_sums(ffn_blocks, order, less)
        ffn_up.send()
        ffn_down.send()
    else:
        grad_fi = sum(mm(fed[m][1], back[m][1], TN) for m in micros)
        grad_fo = sum(mm(back[m][0], fed[m][2], TN) for m in micros)
        grad_fi = lax.psum_scatter(grad_fi, "dp", scatter_dimension=0, tiled=True)
        grad_fo = lax.psum_scatter(grad_fo, "dp", scatter_dimension=0, tiled=True).T

    last = []
    for m in micros:
        if m:
            grad_first.append(tp_finish(part[m], mesh_tp, before))
        qkv, mixed, p_query, p_passage = attended[m]
        grad_branch, grad_qkv, sums5, bias5, *sends = kernel_call(
            attend_back_body(),
            "attend_back",
            [SMEM] + [VMEM] * 13,
            [
                shape((rows, width), BF),
                shape((rows, qkv_width), BF),
                shape((EXTRA, width), F32),
                shape((EXTRA, qkv_width), F32),
            ]
            + part_out,
            [after(ids, *done), fed[m][4], fed[m][5], *grad_first[m], back[m][0], qkv, mixed, p_query, p_passage, vec, w_attn],
            matmul * all_cols * 6,
            12e6,
            scratch=[full_sum, pltpu.VMEM((rows, head_width), BF), full_low],
        )
        last.append((grad_branch, grad_qkv, sums5, bias5, sends))
        arrived = []
        if ring:
            arrived = [ffn_up.absorb(grad_qkv), ffn_down.absorb(grad_qkv)]
            ffn_up.send()
            ffn_down.send()
        if m + 1 < micro_count:
            part[m] = tp_start(sends, mesh_tp, arrived)
            done = [part[m][0]]
            before = part[m][0]

    if ring:
        attn_blocks = kernel_call(
            attend_weight_body(block, head_bias, mesh_dp),
            "attend_weights",
            [SMEM] + [VMEM] * 13,
            [shape((block + EXTRA, all_cols), BF)] * mesh_dp,
            [ids, tokens]
            + [last[m][1] for m in micros]
            + [last[m][0] for m in micros]
            + [attended[m][1] for m in micros]
            + [back[m][2] for m in micros]
            + [last[m][2] for m in micros]
            + [last[m][3] for m in micros],
            matmul * all_cols * 2,
            8e6,
            scratch=[pltpu.VMEM((width, all_cols), F32)],
        )
    else:
        grad_w = sum(
            jnp.concatenate([mm(tokens[m, 0], last[m][1], TN), mm(last[m][0], attended[m][1], TN)], axis=1) for m in micros
        )
        attn_blocks = [grad_w]
    part[-1] = tp_start(last[-1][4], mesh_tp)
    if ring:
        attn_up, attn_down = ring_sums(attn_blocks, order, more)
        attn_down.send()
        attn_up.send()
        f3u, f3d = ffn_up.absorb(attn_blocks[0]), ffn_down.absorb(attn_blocks[0])
        attn_up.absorb(f3u, part[0][1])
        attn_down.absorb(f3d)
        attn_up.send()
        attn_down.send()
        ffn_down.send()
        f4 = ffn_down.absorb()
        attn_up.absorb()
        attn_up.send()
        attn_down.absorb(f4)
        attn_down.send()
    out_tokens, first_grad = kernel_call(
        finish_body,
        "finish",
        [SMEM] + [VMEM] * 7,
        [shape(tokens.shape, BF), shape(tokens.shape, F32)],
        [ids, *finals, last[0][0], *tp_finish(part[0], mesh_tp, last[0][1])],
        1e8,
        6e6,
        out_specs=[pl.BlockSpec(tokens.shape, lambda i: (0, 0, 0, 0)), micro_spec(tokens, 0)],
    )
    in_grad = kernel_call(
        finish_last_body,
        "finish_last",
        [SMEM] + [VMEM] * 5 + [HBM],
        [shape(tokens.shape, F32)],
        [ids, last[1][0], *tp_finish(part[1], mesh_tp, last[0][1]), first_grad],
        1e8,
        4e6,
        out_specs=[micro_spec(tokens, 1)],
        aliases={6: 0},
    )[0]

    if ring:
        attn_up.absorb(part[1][1], first_grad)
        attn_up.send()
        attn_down.absorb()
        pieces = [attn_blocks[0], attn_up.absorb(), attn_down.moving]
        grad_fi, grad_fo = kernel_call(
            unpack_ffn_body,
            "unpack_ffn",
            [VMEM] * 3,
            [shape(ffn_in.shape, F32)] * 2,
            [ffn_blocks[0], ffn_up.moving, ffn_down.moving],
            1e6,
            2e6,
        )
        grad_fo = grad_fo.T
        grads = kernel_call(
            unpack_attn_body,
            "unpack_attn",
            [VMEM] * 3,
            [
                shape(attn_in.shape, F32),
                shape(attn_in_bias.shape, F32),
                shape(attn_out.shape, F32),
                shape(out_biases.shape, F32),
                shape((1, block), F32),
                shape(norm_gains.shape, F32),
                shape(norm_shifts.shape, F32),
            ],
            [after(pieces[0], in_grad), *pieces[1:]],
            1e6,
            2e6,
        )
        grad_ai, grad_ab, grad_ao, grad_ob, grad_fb, grad_ng, grad_ns = grads
        grad_fb = grad_fb.reshape(block)
    else:
        attn_total = lax.psum_scatter(grad_w, "dp", scatter_dimension=0, tiled=True)
        sums = sum(back[m][2] + last[m][2] for m in micros)[:8].reshape(8, mesh_dp, block).transpose(1, 0, 2)
        bias = sum(last[m][3] for m in micros)[7].reshape(3, mesh_dp, head_bias)[0::2].transpose(1, 0, 2)
        bias = jnp.pad(bias.reshape(mesh_dp, 1, 2 * head_bias), ((0, 0), (7, 0), (0, block - 2 * head_bias)))
        small = lax.psum_scatter(sums + bias, "dp", scatter_dimension=0)
        grad_ai = attn_total[:, :qkv_width].reshape(block, 3, head_width).transpose(1, 0, 2)
        grad_ao = attn_total[:, qkv_width:].T
        grad_ab = small[7, : 2 * head_bias].reshape(2, head_bias)
        grad_ob, grad_ng, grad_ns, grad_fb = small[0:2], small[2:4], small[4:6], small[6]

    loss = sum(entropies) / (micro_count * mesh_dp)
    return out_tokens, in_grad, loss, grad_ai, grad_ab, grad_ao, grad_ob, grad_fi, grad_fb, grad_fo, grad_ng, grad_ns


def solution(mesh):
    placed = (
        P(None, "dp", None, None),
        P(None, "dp", None, None),
        P(None, "dp", None),
        P(None, "dp", "tp"),
        P(None, ("tp", "dp")),
        P("tp", "dp"),
        P(None, "dp"),
        P("dp", "tp"),
        P(("tp", "dp")),
        P("tp", "dp"),
        P(None, "dp"),
        P(None, "dp"),
    )
    sizes = (mesh.shape["tp"], mesh.shape["dp"])

    def run(*arrays):
        return on_device(*sizes, *arrays)

    return jax.shard_map(
        run,
        mesh=mesh,
        in_specs=placed,
        out_specs=placed[:2] + (P(),) + placed[3:],
        check_vma=False,
    )
```
